32 devices in a mesh: grp: 4 (over y, x), dev: 8 (over z, core).
Axes of the slice: x: 2, y: 2, z: 4, core: 2. Of those that a mesh axis runs over, the one named last changes fastest.
Arguments:
- batch_rows: bfloat16 [1024, 512], P(('grp', 'dev')), may hold values from -30 to 30
- batch_labels: int32 [1024], P(('grp', 'dev')), may hold values from 0 to 1023, as said below
- memory: bfloat16 [65536, 512], P(('grp', 'dev')), may hold values from -30 to 30
- memory_labels: int32 [65536], P(('grp', 'dev')), may hold values from 0 to 1023
- keep_bits: int32 [65536], P(('grp', 'dev')), may hold values from 0 to 1
- step_index: int32 [1], replicated, may hold values from 0 to 999999
Outputs:
- grad_batch: float32 [1024, 512], P(('grp', 'dev'))
- anchor_loss: float32 [1024], P(('grp', 'dev'))
- new_memory: bfloat16 [65536, 512], P(('grp', 'dev'))
- new_labels: int32 [65536], P(('grp', 'dev'))
The draws below stay inside these ranges and needn't reach their ends.
Inputs may be any that keep to these rules, and one draw needn't show every extreme that they name: `batch_labels`: labels of batch and memory rows are class numbers below 1024.
All inputs are finite; a program needn't handle non-finite values.
Results may differ from the reference program's by a relative error of at most 0.0034.
Values may be sent and summed in bfloat16 or wider, within the bound.
No kernel may reach another device: no remote copies, remote signals or barrier semaphores. Data moves between devices by JAX's collectives and lax.ppermute only.
A program may use at most 128 MiB of HBM per device.

```python
import jax
import jax.numpy as jnp
from jax import lax

D = 512
CLASSES = 1024
B_DEV = 32
M_DEV = 2048
BATCH = 1024
MEMORY = 65536
N_GRP = 4
N_DEV = 8


def labels_of(key, which, count):
    return jax.random.randint(jax.random.fold_in(key, which), (count,), 0, CLASSES)


def mixed_rows(key, which, labels, count):
    prototypes = jax.random.normal(jax.random.fold_in(key, 11), (CLASSES, D), jnp.float32)
    common = jax.random.normal(jax.random.fold_in(key, 12), (D,), jnp.float32)
    noise_rows = jax.random.normal(jax.random.fold_in(key, which), (count, D), jnp.float32)
    shared_part, class_part, noise_part = (0.67, 0.55, 0.5)
    values = shared_part * common[None, :] + class_part * prototypes[labels] + noise_part * noise_rows
    values = values / jnp.sqrt(1.0 * D)
    return jnp.clip(values, -30.0, 30.0)


def draw_batch_labels(key, part):
    return labels_of(key, 1, BATCH).astype(jnp.int32)


def draw_memory_labels(key, part):
    return labels_of(key, 2, MEMORY).astype(jnp.int32)


def draw_batch_rows(key, part):
    return mixed_rows(key, 3, labels_of(key, 1, BATCH), BATCH).astype(jnp.bfloat16)


def draw_memory(key, part):
    return mixed_rows(key, 4, labels_of(key, 2, MEMORY), MEMORY).astype(jnp.bfloat16)


def draw_keep_bits(key, part):
    tickets = jax.random.randint(jax.random.fold_in(key, 5), (MEMORY,), 0, 1000)
    position = jnp.arange(MEMORY).astype(jnp.int32)
    limits = 250 + 500 * position // MEMORY
    return (tickets < limits).astype(jnp.int32)


def setup_inputs(seed: int = 0) -> dict:
    seeds = jax.random.split(jax.random.key(seed), 7)
    return {
        "batch_rows": draw_batch_rows(jax.random.fold_in(seeds[6], 71), 0),
        "batch_labels": draw_batch_labels(jax.random.fold_in(seeds[6], 71), 0),
        "memory": draw_memory(jax.random.fold_in(seeds[6], 71), 0),
        "memory_labels": draw_memory_labels(jax.random.fold_in(seeds[6], 71), 0),
        "keep_bits": draw_keep_bits(jax.random.fold_in(seeds[6], 71), 0),
        "step_index": jax.random.randint(seeds[5], (1,), 0, 1000000).astype(jnp.int32),
    }


pos_scale = 2.0
neg_scale = 50.0
margin = 0.5

def normalize(values):
    floats = values.astype(jnp.float32)
    radius = jnp.sqrt(lax.optimization_barrier(jnp.sum(floats * floats, axis=1, keepdims=True)) + 1e-06)
    return (floats / radius, radius)

def reference(batch_rows, batch_labels, memory, memory_labels, keep_bits, step_index):
    unit_rows, radius = normalize(batch_rows)
    anchors = unit_rows.astype(jnp.bfloat16)
    memory_keys = normalize(memory)[0].astype(jnp.bfloat16)
    blocks = MEMORY // M_DEV
    key_blocks = memory_keys.reshape(blocks, M_DEV, D)
    label_blocks = memory_labels.reshape(blocks, M_DEV)
    kept_blocks = keep_bits.reshape(blocks, M_DEV)

    def visit(carry, inputs):
        pos_sum, neg_sum, pull, push = carry
        block_keys, block_labels, block_kept = inputs
        scores = lax.dot_general(anchors, block_keys, (((1,), (1,)), ((), ())), preferred_element_type=jnp.float32)
        same_class = batch_labels[:, None] == block_labels[None, :]
        kept_rows = (block_kept > 0)[None, :]
        positive = jnp.logical_and(same_class, kept_rows)
        negative = jnp.logical_and(jnp.logical_not(same_class), kept_rows)
        pos_term = jnp.where(positive, jnp.exp(-pos_scale * (scores - margin)), 0.0)
        neg_term = jnp.where(negative, jnp.exp(neg_scale * (scores - margin)), 0.0)
        pos_sum = pos_sum + lax.optimization_barrier(jnp.sum(pos_term, axis=1))
        neg_sum = neg_sum + lax.optimization_barrier(jnp.sum(neg_term, axis=1))
        pull = pull + jnp.dot(pos_term.astype(jnp.bfloat16), block_keys, preferred_element_type=jnp.float32)
        push = push + jnp.dot(neg_term.astype(jnp.bfloat16), block_keys, preferred_element_type=jnp.float32)
        return ((pos_sum, neg_sum, pull, push), None)
    zeros_row = jnp.zeros((BATCH,), jnp.float32)
    zeros_mat = jnp.zeros((BATCH, D), jnp.float32)
    (pos_sum, neg_sum, pull, push), _ = lax.scan(visit, (zeros_row, zeros_row, zeros_mat, zeros_mat), (key_blocks, label_blocks, kept_blocks))
    anchor_loss = jnp.log(1.0 + pos_sum) / pos_scale + jnp.log(1.0 + neg_sum) / neg_scale
    grad_unit = push / (1.0 + neg_sum)[:, None] - pull / (1.0 + pos_sum)[:, None]
    along = lax.optimization_barrier(jnp.sum(unit_rows * grad_unit, axis=1, keepdims=True))
    grad_batch = (grad_unit - unit_rows * along) / radius
    devices_all = N_GRP * N_DEV
    step_value = step_index[0]
    slot_index = (step_value % (M_DEV // B_DEV)).astype(jnp.int32)
    source = ((jnp.arange(devices_all).astype(jnp.int32) - step_value) % devices_all).astype(jnp.int32)
    moved_rows = anchors.reshape(devices_all, B_DEV, D)[source]
    moved_labels = batch_labels.reshape(devices_all, B_DEV)[source]
    zero_index = jnp.zeros((), jnp.int32)
    new_memory = lax.dynamic_update_slice(memory.reshape(devices_all, M_DEV, D), moved_rows, (zero_index, slot_index * B_DEV, zero_index))
    new_labels = lax.dynamic_update_slice(memory_labels.reshape(devices_all, M_DEV), moved_labels, (zero_index, slot_index * B_DEV))
    return (grad_batch, anchor_loss, new_memory.reshape(MEMORY, D), new_labels.reshape(MEMORY))
```

```python
import functools
import math

import jax
import jax.numpy as jnp
from jax import lax
from jax.experimental import pallas as pl
from jax.experimental.pallas import tpu as pltpu
from jax.sharding import PartitionSpec as P

pos_scale = 2.0
neg_scale = 50.0
margin = 0.5
lanes = 128
log2e = math.log2(math.e)
vmem_bytes = 56 * 1024 * 1024
f32 = jnp.float32
bf16 = jnp.bfloat16


def owner(index, step, count):
    if count & (count - 1) == 0:
        return index ^ step
    return (index - step) % count


def place_of(index, member, count):
    if count & (count - 1) == 0:
        return index ^ member
    return (index - member) % count


def whole(shape):
    return pl.BlockSpec(shape, lambda *_: (0,) * len(shape))


def call(body, outs, *args, flops=0, **kw):
    moved = sum(a.size * a.dtype.itemsize for a in args)
    moved += sum(math.prod(o.shape) * o.dtype.itemsize for o in outs)
    return pl.pallas_call(
        body,
        out_shape=outs,
        compiler_params=pltpu.CompilerParams(vmem_limit_bytes=vmem_bytes),
        cost_estimate=pl.CostEstimate(flops=flops, bytes_accessed=moved, transcendentals=0),
        **kw,
    )(*args)


def shaped(shape, dtype):
    return jax.ShapeDtypeStruct(shape, dtype)


def prepare_kernel(rows_ref, labels_ref, packed_ref, unit_ref, radius_ref):
    rows = rows_ref[...].astype(f32)
    count, width = rows.shape
    radius = jnp.sqrt(jnp.sum(rows * rows, axis=1, keepdims=True) + 1e-06)
    unit = rows / radius
    unit_ref[...] = unit
    radius_ref[...] = jnp.broadcast_to(radius, radius_ref.shape)
    packed_ref[:, :width] = unit.astype(bf16)
    labels = jnp.broadcast_to(labels_ref[...], (count, count))
    across = lax.broadcasted_iota(jnp.int32, (count, count), 1)
    down = lax.broadcasted_iota(jnp.int32, (count, count), 0)
    column = jnp.sum(jnp.where(across == down, labels, 0).astype(f32), axis=1, keepdims=True)
    high = jnp.floor(column * (1.0 / 256.0))
    low = column - high * 256.0
    lane = lax.broadcasted_iota(jnp.int32, (count, lanes), 1)
    digits = jnp.where(lane == 0, high, jnp.where(lane == 1, low, 0.0))
    packed_ref[:, width:] = digits.astype(bf16)


def keys_kernel(memory_ref, keys_ref, turned_ref):
    rows = memory_ref[...].astype(f32)
    radius = jnp.sqrt(jnp.sum(rows * rows, axis=1, keepdims=True) + 1e-06)
    keys = rows / radius
    keys_ref[...] = keys.astype(bf16)
    turned_ref[...] = keys.T.astype(bf16)


def pack_stats(pos, neg):
    rows = pos.shape[0]
    lane = lax.broadcasted_iota(jnp.int32, (rows, lanes), 1)
    parts = []
    for value in (pos, neg):
        high = value.astype(bf16).astype(f32)
        parts += [high, value - high]
    stats = jnp.zeros((rows, lanes), f32)
    for at, part in enumerate(parts):
        stats = jnp.where(lane == at, part, stats)
    return stats


def unpack_stats(stats):
    lane = lax.broadcasted_iota(jnp.int32, stats.shape, 1)
    pos = jnp.sum(jnp.where(lane < 2, stats, 0.0), axis=1, keepdims=True)
    neg = jnp.sum(jnp.where((lane >= 2) & (lane < 4), stats, 0.0), axis=1, keepdims=True)
    return pos, neg


def score_kernel(chunk, rows_ref, keys_ref, turned_ref, labels_ref, keep_ref, out_ref, pos_ref, neg_ref):
    width = keys_ref.shape[1]
    slots = keys_ref.shape[0]
    anchors = rows_ref[:, :width]
    digits = rows_ref[:, width:].astype(f32)
    lane = lax.broadcasted_iota(jnp.int32, digits.shape, 1)
    weight = jnp.where(lane == 0, 256.0, jnp.where(lane == 1, 1.0, 0.0))
    labels = jnp.sum(digits * weight, axis=1, keepdims=True)
    kept = keep_ref[...] > 0
    slot_labels = jnp.where(kept, labels_ref[...], -1).astype(f32)
    neg_shift = jnp.where(kept, -neg_scale * margin * log2e, -1e30)
    pos_sum = jnp.zeros((anchors.shape[0], 1), f32)
    neg_sum = jnp.zeros((anchors.shape[0], 1), f32)
    for start in range(0, slots, chunk):
        part = slice(start, start + chunk)
        scores = jnp.dot(anchors, turned_ref[:, part], preferred_element_type=f32)
        same = labels == slot_labels[:, part]
        slope = jnp.where(same, -pos_scale * log2e, neg_scale * log2e)
        shift = jnp.where(same, pos_scale * margin * log2e, neg_shift[:, part])
        term = jnp.exp2(scores * slope + shift)
        pos = jnp.where(same, term, 0.0)
        neg = jnp.where(same, 0.0, term)
        pos_sum += jnp.sum(pos, axis=1, keepdims=True)
        neg_sum += jnp.sum(neg, axis=1, keepdims=True)
        pos_ref[:, part] = pos.astype(bf16)
        neg_ref[:, part] = neg.astype(bf16)
    push = jnp.dot(neg_ref[...], keys_ref[...], preferred_element_type=f32)
    out_ref[:, :width] = push.astype(out_ref.dtype)
    pull = jnp.dot(pos_ref[...], keys_ref[...], preferred_element_type=f32)
    out_ref[:, width : 2 * width] = pull.astype(out_ref.dtype)
    out_ref[:, 2 * width :] = pack_stats(pos_sum, neg_sum).astype(out_ref.dtype)


def score(rows, first, count, keys, turned, labels, keep, dtype):
    width = keys.shape[1]
    slots = keys.shape[0]
    tile = math.gcd(256, math.gcd(first, count))
    chunk = math.gcd(512, slots)
    columns = 2 * width + lanes
    return call(
        functools.partial(score_kernel, chunk),
        [shaped((count, columns), dtype)],
        rows, keys, turned, labels, keep,
        flops=6 * count * slots * width,
        grid=(count // tile,),
        in_specs=[
            pl.BlockSpec((tile, rows.shape[1]), lambda i: (i + first // tile, 0)),
            whole(keys.shape),
            whole(turned.shape),
            whole(labels.shape),
            whole(keep.shape),
        ],
        out_specs=[pl.BlockSpec((tile, columns), lambda i: (i, 0))],
        scratch_shapes=[pltpu.VMEM((tile, slots), bf16), pltpu.VMEM((tile, slots), bf16)],
    )[0]


def add_kernel(width, held, arrived, refs):
    held_refs, arrived_refs, out_refs = refs[:held], refs[held : held + arrived], refs[held + arrived :]
    rows = out_refs[0].shape[0]
    for block, out_ref in enumerate(out_refs):
        first = block * rows
        total = None
        for group in (held_refs, arrived_refs):
            size = group[0].shape[0]
            for ref in group if group is arrived_refs else [group[first // size]]:
                inside = first % size
                value = ref[inside : inside + rows, :].astype(f32)
                total = value if total is None else total + value
        out_ref[:, : 2 * width] = total[:, : 2 * width].astype(out_ref.dtype)
        pos, neg = unpack_stats(total[:, 2 * width :])
        out_ref[:, 2 * width :] = pack_stats(pos, neg).astype(out_ref.dtype)


def add(width, held, arrived, blocks):
    rows = sum(h.shape[0] for h in held) // blocks
    columns = held[0].shape[1]
    outs = [shaped((rows, columns), f32 if b == 0 else bf16) for b in range(blocks)]

    def body(*refs):
        add_kernel(width, len(held), len(arrived), refs)

    return call(body, outs, *held, *arrived)


def finish_kernel(arrived, *refs):
    held_ref, arrived_refs = refs[0], refs[1 : 1 + arrived]
    unit_ref, radius_ref, grad_ref, loss_ref = refs[1 + arrived :]
    width = unit_ref.shape[1]
    total = held_ref[...]
    for ref in arrived_refs:
        total = total + ref[...].astype(f32)
    pos, neg = unpack_stats(total[:, 2 * width :])
    loss = jnp.log(1.0 + pos) / pos_scale + jnp.log(1.0 + neg) / neg_scale
    grad_unit = total[:, :width] / (1.0 + neg) - total[:, width : 2 * width] / (1.0 + pos)
    unit = unit_ref[...]
    along = jnp.sum(unit * grad_unit, axis=1, keepdims=True)
    grad_ref[...] = (grad_unit - unit * along) / radius_ref[:, :1]
    loss_ref[...] = loss


def per_device(batch_rows, batch_labels, memory, memory_labels, keep_bits, step_index):
    groups = lax.axis_size("grp")
    members = lax.axis_size("dev")
    cores = 2 if members % 2 == 0 else 1
    line = members // cores
    devices_all = groups * members
    my_grp = lax.axis_index("grp")
    my_dev = lax.axis_index("dev")
    count, width = batch_rows.shape
    slots = memory.shape[0]

    def pairs(axis, step):
        if axis == "grp":
            return [(owner(i, step, groups), i) for i in range(groups)]
        out = []
        for z in range(line):
            for c in range(cores):
                source = (owner(z, step, line), c) if axis == "line" else (z, owner(c, step, cores))
                out.append((source[0] * cores + source[1], z * cores + c))
        return out

    def fetch(value, axis, step):
        return lax.ppermute(value, "grp" if axis == "grp" else "dev", pairs(axis, step))

    def hand_back(value, axis, step):
        back = [(b, a) for a, b in pairs(axis, step)]
        return lax.ppermute(value, "grp" if axis == "grp" else "dev", back)

    packed, unit, radius = call(
        prepare_kernel,
        [shaped((count, width + lanes), bf16), shaped((count, width), f32), shaped((count, lanes), f32)],
        batch_rows,
        batch_labels.reshape(1, count),
    )

    block = math.gcd(256, slots)
    keys, turned = call(
        keys_kernel,
        [shaped((slots, width), bf16), shaped((width, slots), bf16)],
        memory,
        grid=(slots // block,),
        in_specs=[pl.BlockSpec((block, width), lambda i: (i, 0))],
        out_specs=[pl.BlockSpec((block, width), lambda i: (i, 0)), pl.BlockSpec((width, block), lambda i: (0, i))],
    )
    label_row = memory_labels.reshape(1, slots)
    keep_row = keep_bits.reshape(1, slots)

    part = jnp.concatenate([packed] + [fetch(packed, "line", s) for s in range(1, line)])
    near = jnp.concatenate([part] + [fetch(part, "grp", s) for s in range(1, groups)])
    halves = [near] + [fetch(near, "core", s) for s in range(1, cores)]
    near_rows = near.shape[0]
    split = near_rows // 2

    sides = (keys, turned, label_row, keep_row)
    early = score(near, 0, split, *sides, f32)
    arrived = [hand_back(score(halves[s], 0, near_rows, *sides, bf16), "core", s) for s in range(1, cores)]
    late = score(near, split, near_rows - split, *sides, f32)

    sums = add(width, [early, late], arrived, groups)
    arrived = [hand_back(sums[s], "grp", s) for s in range(1, groups)]
    sums = add(width, [sums[0]], arrived, line)
    arrived = [hand_back(sums[s], "line", s) for s in range(1, line)]
    grad_batch, loss = call(
        functools.partial(finish_kernel, len(arrived)),
        [shaped((count, width), f32), shaped((count, 1), f32)],
        sums[0], *arrived, unit, radius,
    )

    step_value = step_index[0]
    first_slot = (step_value % (slots // count)) * count
    source = (my_grp * members + my_dev - step_value) % devices_all
    source_grp, source_dev = source // members, source % members
    grp_place = place_of(my_grp, source_grp, groups)
    line_place = place_of(my_dev // cores, source_dev // cores, line)
    core_place = place_of(my_dev % cores, source_dev % cores, cores)
    at = (grp_place * line + line_place) * count
    moved = lax.dynamic_slice_in_dim(halves[0], at, count, 0)
    for s in range(1, cores):
        moved = jnp.where(core_place == s, lax.dynamic_slice_in_dim(halves[s], at, count, 0), moved)
    digits = moved[:, width : width + 2].astype(jnp.int32)
    moved_labels = digits[:, 0] * 256 + digits[:, 1]
    new_memory = lax.dynamic_update_slice_in_dim(memory, moved[:, :width], first_slot, 0)
    new_labels = lax.dynamic_update_slice_in_dim(memory_labels, moved_labels, first_slot, 0)
    return (grad_batch, loss.reshape(count), new_memory, new_labels)


def solution(mesh):
    placed = (
        P(("grp", "dev"), None),
        P(("grp", "dev")),
        P(("grp", "dev"), None),
        P(("grp", "dev")),
        P(("grp", "dev")),
        P(),
    )
    return jax.shard_map(
        per_device,
        mesh=mesh,
        in_specs=placed,
        out_specs=(
            P(("grp", "dev"), None),
            P(("grp", "dev")),
            P(("grp", "dev"), None),
            P(("grp", "dev")),
        ),
        check_vma=False,
    )
```

```python
import functools
import math

import jax
import jax.numpy as jnp
from jax import lax
from jax.experimental import pallas as pl
from jax.experimental.pallas import tpu as pltpu
from jax.sharding import PartitionSpec as P

pos_scale = 2.0
neg_scale = 50.0
margin = 0.5
lanes = 128
log2e = math.log2(math.e)
vmem_bytes = 20 * 1024 * 1024
vmem_terms = 12 * 1024 * 1024
f32 = jnp.float32
bf16 = jnp.bfloat16


def call(body, outs, *args, flops=0, limit=vmem_bytes, **kw):
    moved = sum(a.size * a.dtype.itemsize for a in args)
    moved += sum(math.prod(o.shape) * o.dtype.itemsize for o in outs)
    return pl.pallas_call(
        body,
        out_shape=outs,
        compiler_params=pltpu.CompilerParams(vmem_limit_bytes=limit),
        cost_estimate=pl.CostEstimate(flops=flops, bytes_accessed=moved, transcendentals=0),
        **kw,
    )(*args)


def shaped(shape, dtype):
    return jax.ShapeDtypeStruct(shape, dtype)


def in_vmem(value):
    return pltpu.with_memory_space_constraint(value, pltpu.VMEM)


def prepare_kernel(rows_ref, labels_ref, packed_ref, unit_ref, radius_ref):
    rows = rows_ref[...].astype(f32)
    count, width = rows.shape
    radius = jnp.sqrt(jnp.sum(rows * rows, axis=1, keepdims=True) + 1e-06)
    unit = rows / radius
    unit_ref[...] = unit
    radius_ref[...] = jnp.broadcast_to(radius, radius_ref.shape)
    packed_ref[:, :width] = unit.astype(bf16)
    column = to_column(labels_ref[...].astype(f32))
    high = jnp.floor(column * (1.0 / 256.0))
    low = column - high * 256.0
    lane = lax.broadcasted_iota(jnp.int32, (count, lanes), 1)
    digits = jnp.where(lane == 0, high, jnp.where(lane == 1, low, 0.0))
    packed_ref[:, width:] = digits.astype(bf16)


def diagonal(count):
    across = lax.broadcasted_iota(jnp.int32, (count, count), 1)
    down = lax.broadcasted_iota(jnp.int32, (count, count), 0)
    return across == down


def to_column(row):
    count = row.shape[1]
    spread = jnp.broadcast_to(row, (count, count))
    return jnp.sum(jnp.where(diagonal(count), spread, 0.0), axis=1, keepdims=True)


def to_row(column):
    count = column.shape[0]
    spread = jnp.broadcast_to(column, (count, count))
    return jnp.sum(jnp.where(diagonal(count), spread, 0.0), axis=0, keepdims=True)


def keys_kernel(memory_ref, keys_ref, *copy_refs):
    stored = memory_ref[...]
    rows = stored.astype(f32)
    radius = jnp.sqrt(jnp.sum(rows * rows, axis=1, keepdims=True) + 1e-06)
    keys_ref[...] = (rows / radius).astype(bf16)
    for copy_ref in copy_refs:
        copy_ref[...] = stored


def keys_of(memory, copied):
    slots, width = memory.shape
    block = math.gcd(512, slots)
    spec = pl.BlockSpec((block, width), lambda i: (i, 0))
    return call(
        keys_kernel,
        [shaped((slots, width), bf16)] * (2 if copied else 1),
        memory,
        grid=(slots // block,),
        in_specs=[spec],
        out_specs=[spec] * (2 if copied else 1),
    )


def score_kernel(blocks, sides, chunk, count, *refs):
    rows_refs, keys_refs = refs[:blocks], refs[blocks : blocks + sides]
    label_refs = refs[blocks + sides : blocks + 2 * sides]
    term_refs = refs[blocks + 2 * sides : 2 * blocks + 2 * sides]
    stats_ref = refs[2 * blocks + 2 * sides]
    slots, width = keys_refs[0].shape
    size = rows_refs[0].shape[0]
    anchors = jnp.concatenate([ref[:, :width] for ref in rows_refs], axis=0)
    digits = jnp.concatenate([ref[:, width:] for ref in rows_refs], axis=0).astype(f32)
    lane = lax.broadcasted_iota(jnp.int32, digits.shape, 1)
    weight = jnp.where(lane == 0, 256.0, jnp.where(lane == 1, 1.0, 0.0))
    labels = jnp.sum(digits * weight, axis=1, keepdims=True)
    pos_sum = jnp.zeros((anchors.shape[0], 1), f32)
    neg_sum = jnp.zeros((anchors.shape[0], 1), f32)
    for side in range(sides):
        slot_labels = label_refs[side][...]
        neg_shift = jnp.where(slot_labels < 0.0, -1e30, -neg_scale * margin * log2e)
        for start in range(0, slots, chunk):
            part = slice(start, start + chunk)
            scores = lax.dot_general(
                anchors, keys_refs[side][part, :], (((1,), (1,)), ((), ())), preferred_element_type=f32
            )
            same = labels == slot_labels[:, part]
            slope = jnp.where(same, -pos_scale * log2e, neg_scale * log2e)
            shift = jnp.where(same, pos_scale * margin * log2e, neg_shift[:, part])
            term = jnp.exp2(scores * slope + shift)
            pos_sum += jnp.sum(jnp.where(same, term, 0.0), axis=1, keepdims=True)
            neg_sum += jnp.sum(jnp.where(same, 0.0, term), axis=1, keepdims=True)
            signed = jnp.where(same, -term, term)
            to = slice(side * slots + start, side * slots + start + chunk)
            for block, ref in enumerate(term_refs):
                ref[:, to] = signed[block * size : (block + 1) * size, :]
    for which, total in enumerate((pos_sum, neg_sum)):
        for at in range(blocks * size // count):
            stats_ref[which, at : at + 1, :] = to_row(total[at * count : (at + 1) * count])


def score(blocks, keys, labels, count, placed):
    slots, width = keys[0].shape
    size = blocks[0].shape[0]
    shape = (size, slots * len(keys))
    outs = [placed(shape, f32) for _ in blocks]
    outs.append(shaped((2, len(blocks) * size // count, count), f32))
    return call(
        functools.partial(score_kernel, len(blocks), len(keys), math.gcd(512, slots), count),
        outs,
        *blocks, *[in_vmem(k) for k in keys], *labels,
        flops=2 * size * len(blocks) * slots * len(keys) * width,
    )


def pull_kernel(first, sides, chunk, term_ref, totals_ref, *refs):
    keys_refs, out_ref, weight_ref = refs[:sides], refs[sides], refs[sides + 1]
    slots = keys_refs[0].shape[0]
    size = term_ref.shape[0]
    count = totals_ref.shape[2]
    scales = []
    for which in range(2):
        parts = [to_column(totals_ref[which, first + at : first + at + 1, :]) for at in range(size // count)]
        scales.append(1.0 / (1.0 + jnp.concatenate(parts, axis=0)))
    for start in range(0, slots * sides, chunk):
        part = slice(start, start + chunk)
        term = term_ref[:, part]
        weight = term * jnp.where(term < 0.0, scales[0], scales[1])
        weight_ref[:, part] = weight.astype(bf16)
    total = None
    for side in range(sides):
        part = weight_ref[:, side * slots : (side + 1) * slots]
        term = jnp.dot(part, keys_refs[side][...], preferred_element_type=f32)
        total = term if total is None else total + term
    out_ref[...] = total.astype(out_ref.dtype)


def weighted(term, totals, first, keys, dtype):
    slots, width = keys[0].shape
    size = term.shape[0]
    return call(
        functools.partial(pull_kernel, first, len(keys), math.gcd(512, slots)),
        [shaped((size, width), dtype)],
        term, totals, *[in_vmem(k) for k in keys],
        flops=2 * size * slots * len(keys) * width,
        scratch_shapes=[pltpu.VMEM((size, slots * len(keys)), bf16)],
    )[0]


def finish_kernel(arrived, *refs):
    held_ref, arrived_refs = refs[0], refs[1 : 1 + arrived]
    unit_ref, radius_ref, grad_ref = refs[1 + arrived :]
    total = held_ref[...]
    for ref in arrived_refs:
        total = total + ref[...].astype(f32)
    unit = unit_ref[...]
    along = jnp.sum(unit * total, axis=1, keepdims=True)
    grad_ref[...] = (total - unit * along) / radius_ref[:, :1]


def swapped(value, axis, step):
    shape = value.shape
    cut = shape[:axis] + (shape[axis] // (2 * step), 2, step) + shape[axis + 1 :]
    return jnp.flip(value.reshape(cut), axis + 1).reshape(shape)


def per_device(batch_rows, batch_labels, memory, memory_labels, keep_bits, step_index):
    groups = lax.axis_size("grp")
    members = lax.axis_size("dev")
    cores = 2 if members % 2 == 0 else 1
    line = members // cores
    devices_all = groups * members
    my_grp = lax.axis_index("grp")
    my_dev = lax.axis_index("dev")
    count, width = batch_rows.shape
    slots = memory.shape[0]

    def exchange(value, axis, step):
        if axis == "grp":
            return lax.ppermute(value, "grp", [(i, i ^ step) for i in range(groups)])
        jump = step * cores if axis == "line" else step
        return lax.ppermute(value, "dev", [(i, i ^ jump) for i in range(members)])

    packed, unit, radius = call(
        prepare_kernel,
        [shaped((count, width + lanes), bf16), shaped((count, width), f32), shaped((count, lanes), f32)],
        batch_rows,
        batch_labels.reshape(1, count),
    )

    slot_labels = jnp.where(keep_bits > 0, memory_labels, -1)
    memories = [memory] + [exchange(memory, "core", s) for s in range(1, cores)]
    labels = [slot_labels] + [exchange(slot_labels, "core", s) for s in range(1, cores)]
    labels = [value.astype(f32).reshape(1, slots) for value in labels]
    own_keys, copied = keys_of(memory, True)
    keys = [own_keys] + [keys_of(value, False)[0] for value in memories[1:]]

    part = jnp.concatenate([packed] + [exchange(packed, "line", s) for s in range(1, line)])
    blocks = [part] + [exchange(part, "grp", s) for s in range(1, groups)]
    size = part.shape[0]

    fits = 4 * groups * size * slots * cores <= vmem_terms
    placed = pltpu.VMEM if fits else shaped
    terms, stats = [], []
    for first, last in [(0, 1)] + [(i, min(i + 3, groups)) for i in range(1, groups, 3)]:
        *more, stat = score(blocks[first:last], keys, labels, count, placed)
        terms += more
        stats.append(stat)
    totals = jnp.concatenate(stats, axis=1).reshape(2, groups, line, count)
    for axis, name, extent in ((2, "line", line), (1, "grp", groups)):
        step = 1
        while step < extent:
            totals = totals + swapped(exchange(totals, name, step), axis, step)
            step *= 2
    flat = totals.reshape(2, groups * line, count)
    loss = jnp.log(1.0 + totals[0, 0, 0]) / pos_scale + jnp.log(1.0 + totals[1, 0, 0]) / neg_scale

    arrived = []
    for s in list(range(groups - 1, 0, -1)):
        arrived.append(exchange(weighted(terms[s], flat, s * line, keys, bf16), "grp", s))
    total = weighted(terms[0], flat, 0, keys, f32)
    for value in arrived:
        total = total + value.astype(f32)
    arrived = [exchange(total[s * count : (s + 1) * count].astype(bf16), "line", s) for s in range(1, line)]
    grad_batch = call(
        functools.partial(finish_kernel, len(arrived)),
        [shaped((count, width), f32)],
        total[:count], *arrived, unit, radius,
    )[0]

    step_value = step_index[0]
    first_slot = (step_value % (slots // count)) * count
    crossing = (step_value % cores) if cores > 1 else 0
    target = my_grp * members + (my_dev ^ crossing)
    source = (target - step_value) % devices_all
    source_grp, source_line = source // members, (source % members) // cores
    at = ((my_grp ^ source_grp) * line + ((my_dev // cores) ^ source_line)) * count
    moved = lax.dynamic_slice_in_dim(jnp.concatenate(blocks), at, count, 0)
    if cores > 1:
        moved = jnp.where(crossing > 0, exchange(moved, "core", 1), moved)
    digits = moved[:, width : width + 2].astype(jnp.int32)
    moved_labels = digits[:, 0] * 256 + digits[:, 1]
    new_memory = lax.dynamic_update_slice_in_dim(copied, moved[:, :width], first_slot, 0)
    new_labels = lax.dynamic_update_slice_in_dim(memory_labels, moved_labels, first_slot, 0)
    return (grad_batch, loss, new_memory, new_labels)


def solution(mesh):
    placed = (
        P(("grp", "dev"), None),
        P(("grp", "dev")),
        P(("grp", "dev"), None),
        P(("grp", "dev")),
        P(("grp", "dev")),
        P(),
    )
    return jax.shard_map(
        per_device,
        mesh=mesh,
        in_specs=placed,
        out_specs=(
            P(("grp", "dev"), None),
            P(("grp", "dev")),
            P(("grp", "dev"), None),
            P(("grp", "dev")),
        ),
        check_vma=False,
    )
```

```python
import functools
import math

import jax
import jax.numpy as jnp
from jax import lax
from jax.experimental import pallas as pl
from jax.experimental.pallas import tpu as pltpu
from jax.sharding import PartitionSpec as P

pos_scale = 2.0
neg_scale = 50.0
margin = 0.5
lanes = 128
log2e = math.log2(math.e)
vmem_bytes = 20 * 1024 * 1024
vmem_most = 56 * 1024 * 1024
f32 = jnp.float32
bf16 = jnp.bfloat16


def call(body, outs, *args, flops=0, limit=vmem_bytes, **kw):
    moved = sum(a.size * a.dtype.itemsize for a in args)
    moved += sum(math.prod(o.shape) * o.dtype.itemsize for o in outs)
    return pl.pallas_call(
        body,
        out_shape=outs,
        compiler_params=pltpu.CompilerParams(vmem_limit_bytes=limit),
        cost_estimate=pl.CostEstimate(flops=flops, bytes_accessed=moved, transcendentals=0),
        **kw,
    )(*args)


def shaped(shape, dtype):
    return jax.ShapeDtypeStruct(shape, dtype)


def in_vmem(value):
    return pltpu.with_memory_space_constraint(value, pltpu.VMEM)


def prepare_kernel(rows_ref, labels_ref, stored_ref, keep_ref, packed_ref, unit_ref, radius_ref, slot_ref, copy_ref):
    stored = stored_ref[...]
    slot_ref[...] = jnp.where(keep_ref[...] > 0, stored, -1)
    copy_ref[...] = stored
    rows = rows_ref[...].astype(f32)
    count, width = rows.shape
    radius = jnp.sqrt(jnp.sum(rows * rows, axis=1, keepdims=True) + 1e-06)
    unit = rows / radius
    unit_ref[...] = unit
    radius_ref[...] = jnp.broadcast_to(radius, radius_ref.shape)
    packed_ref[:, :width] = unit.astype(bf16)
    column = to_column(labels_ref[...].astype(f32))
    high = jnp.floor(column * (1.0 / 256.0))
    low = column - high * 256.0
    lane = lax.broadcasted_iota(jnp.int32, (count, lanes), 1)
    digits = jnp.where(lane == 0, high, jnp.where(lane == 1, low, 0.0))
    packed_ref[:, width:] = digits.astype(bf16)


def diagonal(count):
    across = lax.broadcasted_iota(jnp.int32, (count, count), 1)
    down = lax.broadcasted_iota(jnp.int32, (count, count), 0)
    return across == down


def to_column(row):
    count = row.shape[1]
    spread = jnp.broadcast_to(row, (count, count))
    return jnp.sum(jnp.where(diagonal(count), spread, 0.0), axis=1, keepdims=True)


def keys_kernel(memory_ref, keys_ref, *copy_refs):
    stored = memory_ref[...]
    rows = stored.astype(f32)
    radius = jnp.sqrt(jnp.sum(rows * rows, axis=1, keepdims=True) + 1e-06)
    keys_ref[...] = (rows / radius).astype(bf16)
    for copy_ref in copy_refs:
        copy_ref[...] = stored


def keys_of(memory, copied):
    slots, width = memory.shape
    block = math.gcd(512, slots)
    spec = pl.BlockSpec((block, width), lambda i: (i, 0))
    return call(
        keys_kernel,
        [shaped((slots, width), bf16)] * (2 if copied else 1),
        memory,
        grid=(slots // block,),
        in_specs=[spec],
        out_specs=[spec] * (2 if copied else 1),
    )


def pack_sums(values):
    rows = values[0].shape[0]
    lane = lax.broadcasted_iota(jnp.int32, (rows, lanes), 1)
    packed = jnp.zeros((rows, lanes), f32)
    for at, value in enumerate(values):
        high = value.astype(bf16).astype(f32)
        packed = jnp.where(lane == 2 * at, high, packed)
        packed = jnp.where(lane == 2 * at + 1, value - high, packed)
    return packed


def unpack_sums(packed):
    lane = lax.broadcasted_iota(jnp.int32, packed.shape, 1)
    return [
        jnp.sum(jnp.where((lane >= 2 * at) & (lane < 2 * at + 2), packed, 0.0), axis=1, keepdims=True)
        for at in range(4)
    ]


def block_kernel(sides, chunk, rows_ref, *refs):
    keys_refs, label_refs = refs[:sides], refs[sides : 2 * sides]
    out_ref, weight_ref = refs[2 * sides :]
    slots, width = keys_refs[0].shape
    size = rows_ref.shape[0]
    anchors = rows_ref[:, :width]
    digits = rows_ref[:, width:].astype(f32)
    lane = lax.broadcasted_iota(jnp.int32, digits.shape, 1)
    digit = jnp.where(lane == 0, 256.0, jnp.where(lane == 1, 1.0, 0.0))
    labels = jnp.sum(digits * digit, axis=1, keepdims=True)
    pos_sum = jnp.zeros((size, 1), f32)
    neg_sum = jnp.zeros((size, 1), f32)
    for side in range(sides):
        slot_labels = label_refs[side][...].astype(f32)
        neg_shift = jnp.where(slot_labels < 0.0, -1e30, -neg_scale * margin * log2e)
        for start in range(0, slots, chunk):
            part = slice(start, start + chunk)
            scores = lax.dot_general(
                anchors, keys_refs[side][part, :], (((1,), (1,)), ((), ())), preferred_element_type=f32
            )
            same = labels == slot_labels[:, part]
            slope = jnp.where(same, -pos_scale * log2e, neg_scale * log2e)
            shift = jnp.where(same, pos_scale * margin * log2e, neg_shift[:, part])
            term = jnp.exp2(scores * slope + shift)
            pos = jnp.where(same, term, 0.0)
            neg = jnp.where(same, 0.0, term)
            pos_sum += jnp.sum(pos, axis=1, keepdims=True)
            neg_sum += jnp.sum(neg, axis=1, keepdims=True)
            to = slice(side * slots + start, side * slots + start + chunk)
            weight_ref[:size, to] = neg.astype(bf16)
            weight_ref[size:, to] = pos.astype(bf16)
    total = None
    for side in range(sides):
        part = weight_ref[:, side * slots : (side + 1) * slots]
        term = jnp.dot(part, keys_refs[side][...], preferred_element_type=f32)
        total = term if total is None else total + term
    floats = anchors.astype(f32)
    sums = [pos_sum, neg_sum]
    for which in range(2):
        value = total[which * size : (which + 1) * size, :]
        along = jnp.sum(value * floats, axis=1, keepdims=True)
        out_ref[:, which * width : (which + 1) * width] = (value - along * floats).astype(out_ref.dtype)
        sums.append(along)
    out_ref[:, 2 * width :] = pack_sums(sums).astype(out_ref.dtype)


def block_sums(rows, keys, labels, dtype):
    slots, width = keys[0].shape
    size = rows.shape[0]
    return call(
        functools.partial(block_kernel, len(keys), math.gcd(512, slots)),
        [shaped((size, 2 * width + lanes), dtype)],
        rows, *[in_vmem(k) for k in keys], *labels,
        flops=6 * size * slots * len(keys) * width,
        scratch_shapes=[pltpu.VMEM((2 * size, slots * len(keys)), bf16)],
    )[0]


def add_kernel(arrived, *refs):
    in_refs, out_refs = refs[: 1 + arrived], refs[1 + arrived :]
    rows, columns = out_refs[0].shape
    for block, out_ref in enumerate(out_refs):
        part = slice(block * rows, (block + 1) * rows)
        total = in_refs[0][part, :]
        for ref in in_refs[1:]:
            total = total + ref[part, :].astype(f32)
        out_ref[:, : columns - lanes] = total[:, : columns - lanes].astype(out_ref.dtype)
        sums = pack_sums(unpack_sums(total[:, columns - lanes :]))
        out_ref[:, columns - lanes :] = sums.astype(out_ref.dtype)


def add(held, arrived, blocks):
    rows, columns = held.shape
    outs = [shaped((rows // blocks, columns), f32 if b == 0 else bf16) for b in range(blocks)]
    return call(functools.partial(add_kernel, len(arrived)), outs, held, *arrived)


def finish_kernel(arrived, *refs):
    held_ref, arrived_refs = refs[0], refs[1 : 1 + arrived]
    unit_ref, radius_ref, grad_ref, loss_ref = refs[1 + arrived :]
    count, width = unit_ref.shape
    total = held_ref[...]
    for ref in arrived_refs:
        total = total + ref[...].astype(f32)
    pos, neg, push_along, pull_along = unpack_sums(total[:, 2 * width :])
    unit = unit_ref[...]
    anchors = unit.astype(bf16).astype(f32)
    push = total[:, :width] + push_along * anchors
    pull = total[:, width : 2 * width] + pull_along * anchors
    grad_unit = push / (1.0 + neg) - pull / (1.0 + pos)
    along = jnp.sum(unit * grad_unit, axis=1, keepdims=True)
    grad_ref[...] = (grad_unit - unit * along) / radius_ref[:, :1]
    loss = jnp.log(1.0 + pos) / pos_scale + jnp.log(1.0 + neg) / neg_scale
    spread = jnp.broadcast_to(loss, (count, count))
    loss_ref[...] = jnp.sum(jnp.where(diagonal(count), spread, 0.0), axis=0, keepdims=True)


def per_device(batch_rows, batch_labels, memory, memory_labels, keep_bits, step_index):
    groups = lax.axis_size("grp")
    members = lax.axis_size("dev")
    cores = 2 if members % 2 == 0 else 1
    line = members // cores
    devices_all = groups * members
    my_grp = lax.axis_index("grp")
    my_dev = lax.axis_index("dev")
    count, width = batch_rows.shape
    slots = memory.shape[0]

    def exchange(value, axis, step):
        if axis == "grp":
            return lax.ppermute(value, "grp", [(i, i ^ step) for i in range(groups)])
        jump = step * cores if axis == "line" else step
        return lax.ppermute(value, "dev", [(i, i ^ jump) for i in range(members)])

    folded = (slots // lanes, lanes)
    packed, unit, radius, slot_labels, copied_labels = call(
        prepare_kernel,
        [
            shaped((count, width + lanes), bf16),
            shaped((count, width), f32),
            shaped((count, lanes), f32),
            shaped(folded, jnp.int32),
            shaped(folded, jnp.int32),
        ],
        batch_rows, batch_labels.reshape(1, count), memory_labels.reshape(folded), keep_bits.reshape(folded),
        limit=vmem_most,
    )

    labels = [slot_labels] + [exchange(slot_labels, "core", s) for s in range(1, cores)]
    labels = [value.reshape(1, slots) for value in labels]
    memories = [memory] + [exchange(memory, "core", s) for s in range(1, cores)]
    own_keys, copied = keys_of(memory, True)
    keys = [own_keys] + [keys_of(value, False)[0] for value in memories[1:]]

    part = jnp.concatenate([packed] + [exchange(packed, "line", s) for s in range(1, line)])
    blocks = [part] + [exchange(part, "grp", s) for s in range(1, groups)]

    arrived = []
    for s in range(groups - 1, 0, -1):
        sums = block_sums(blocks[s], keys, labels, bf16)
        arrived.append(exchange(sums, "grp", s))
    if groups > 1:
        part, sums = lax.optimization_barrier((part, sums))
    held = block_sums(part, keys, labels, f32)
    held, *parts = add(held, arrived, line)
    arrived = [exchange(value, "line", s) for s, value in enumerate(parts, 1)]
    grad_batch, loss = call(
        functools.partial(finish_kernel, len(arrived)),
        [shaped((count, width), f32), shaped((1, count), f32)],
        held, *arrived, unit, radius,
    )

    step_value = step_index[0]
    first_slot = (step_value % (slots // count)) * count
    crossing = (step_value % cores) if cores > 1 else 0
    target = my_grp * members + (my_dev ^ crossing)
    source = (target - step_value) % devices_all
    source_grp, source_line = source // members, (source % members) // cores
    at = ((my_grp ^ source_grp) * line + ((my_dev // cores) ^ source_line)) * count
    moved = lax.dynamic_slice_in_dim(jnp.concatenate(blocks), at, count, 0)
    if cores > 1:
        moved = jnp.where(crossing > 0, exchange(moved, "core", 1), moved)
    digits = moved[:, width : width + 2].astype(jnp.int32)
    moved_labels = digits[:, 0] * 256 + digits[:, 1]
    new_memory = lax.dynamic_update_slice_in_dim(copied, moved[:, :width], first_slot, 0)
    new_labels = lax.dynamic_update_slice_in_dim(copied_labels.reshape(slots), moved_labels, first_slot, 0)
    return (grad_batch, loss.reshape(count), new_memory, new_labels)


def solution(mesh):
    placed = (
        P(("grp", "dev"), None),
        P(("grp", "dev")),
        P(("grp", "dev"), None),
        P(("grp", "dev")),
        P(("grp", "dev")),
        P(),
    )
    return jax.shard_map(
        per_device,
        mesh=mesh,
        in_specs=placed,
        out_specs=(
            P(("grp", "dev"), None),
            P(("grp", "dev")),
            P(("grp", "dev"), None),
            P(("grp", "dev")),
        ),
        check_vma=False,
    )
```

```python
import functools
import math

import jax
import jax.numpy as jnp
from jax import lax
from jax.experimental import pallas as pl
from jax.experimental.pallas import tpu as pltpu
from jax.sharding import PartitionSpec as P

pos_scale = 2.0
neg_scale = 50.0
margin = 0.5
lanes = 128
log2e = math.log2(math.e)
vmem_bytes = 20 * 1024 * 1024
vmem_most = 56 * 1024 * 1024
f32 = jnp.float32
bf16 = jnp.bfloat16


def call(body, outs, *args, work=0, limit=vmem_bytes, **kw):
    return pl.pallas_call(
        body,
        out_shape=outs,
        compiler_params=pltpu.CompilerParams(vmem_limit_bytes=limit),
        cost_estimate=pl.CostEstimate(flops=work, bytes_accessed=0, transcendentals=0),
        **kw,
    )(*args)


def shaped(shape, dtype):
    return jax.ShapeDtypeStruct(shape, dtype)


def in_vmem(value):
    return pltpu.with_memory_space_constraint(value, pltpu.VMEM)


def prepare_kernel(rows_ref, labels_ref, stored_ref, keep_ref, packed_ref, unit_ref, radius_ref, slot_ref, copy_ref):
    stored = stored_ref[...]
    slot_ref[...] = jnp.where(keep_ref[...] > 0, stored, -1)
    copy_ref[...] = stored
    rows = rows_ref[...].astype(f32)
    count, width = rows.shape
    radius = jnp.sqrt(jnp.sum(rows * rows, axis=1, keepdims=True) + 1e-06)
    unit = rows / radius
    unit_ref[...] = unit
    radius_ref[...] = jnp.broadcast_to(radius, radius_ref.shape)
    packed_ref[:, :width] = unit.astype(bf16)
    column = to_column(labels_ref[...].astype(f32))
    high = jnp.floor(column * (1.0 / 256.0))
    low = column - high * 256.0
    lane = lax.broadcasted_iota(jnp.int32, (count, lanes), 1)
    digits = jnp.where(lane == 0, high, jnp.where(lane == 1, low, 0.0))
    packed_ref[:, width:] = digits.astype(bf16)


def diagonal(count):
    across = lax.broadcasted_iota(jnp.int32, (count, count), 1)
    down = lax.broadcasted_iota(jnp.int32, (count, count), 0)
    return across == down


def to_column(row):
    count = row.shape[1]
    spread = jnp.broadcast_to(row, (count, count))
    return jnp.sum(jnp.where(diagonal(count), spread, 0.0), axis=1, keepdims=True)


def keys_kernel(memory_ref, keys_ref, copy_ref):
    stored = memory_ref[...]
    keys_ref[...] = normalized(stored)
    copy_ref[...] = stored


def normalized(stored):
    rows = stored.astype(f32)
    radius = jnp.sqrt(jnp.sum(rows * rows, axis=1, keepdims=True) + 1e-06)
    return (rows / radius).astype(bf16)


def keys_of(memory):
    slots, width = memory.shape
    block = math.gcd(512, slots)
    spec = pl.BlockSpec((block, width), lambda i: (i, 0))
    return call(
        keys_kernel,
        [shaped((slots, width), bf16)] * 2,
        memory,
        grid=(slots // block,),
        in_specs=[spec],
        out_specs=[spec] * 2,
    )


def join_kernel(blocks, *refs):
    block_refs, out_ref = refs[:blocks], refs[-1]
    size = block_refs[0].shape[0]
    for place, ref in enumerate(block_refs):
        out_ref[place * size : (place + 1) * size, :] = ref[...]


def join(blocks, after):
    size, width = blocks[0].shape
    return call(
        functools.partial(join_kernel, len(blocks)),
        [shaped((size * len(blocks), width), blocks[0].dtype)],
        *blocks, *after,
        in_specs=[pl.BlockSpec(memory_space=pltpu.VMEM)] * len(blocks)
        + [pl.BlockSpec(memory_space=pl.ANY)] * len(after),
    )[0]


def other_keys_kernel(block, memory_ref, rows_ref, keys_ref, same_ref):
    same_ref[...] = rows_ref[...]

    @pl.loop(0, memory_ref.shape[0] // block)
    def _(i):
        part = pl.ds(pl.multiple_of(i * block, block), block)
        keys_ref[part, :] = normalized(memory_ref[part, :])


def other_keys(memory, rows):
    return call(
        functools.partial(other_keys_kernel, math.gcd(256, memory.shape[0])),
        [shaped(memory.shape, bf16), shaped(rows.shape, bf16)],
        memory, rows,
    )


def pick_kernel(groups, count, at_ref, *refs):
    blocks_refs, out_ref = refs[:groups], refs[-1]
    size = blocks_refs[0].shape[0]
    for place, ref in enumerate(blocks_refs):
        inside = at_ref[0] - place * size

        @pl.when((inside >= 0) & (inside < size))
        def _():
            out_ref[...] = ref[pl.ds(pl.multiple_of(inside, count), count), :]


def pick(blocks, at, count, after):
    return call(
        functools.partial(pick_kernel, len(blocks), count),
        [shaped((count, blocks[0].shape[1]), bf16)],
        at.reshape(1), *blocks, *after,
        in_specs=[pl.BlockSpec(memory_space=pltpu.SMEM)]
        + [pl.BlockSpec(memory_space=pltpu.VMEM)] * len(blocks)
        + [pl.BlockSpec(memory_space=pl.ANY)] * len(after),
    )[0]


def patch_kernel(choices, where_ref, stored_ref, labels_ref, *refs):
    moved_refs, (memory_ref, new_labels_ref, rows_ref, sem) = refs[:choices], refs[choices:]
    first = where_ref[0]
    count, width = rows_ref.shape
    moved = moved_refs[0][...]
    for choice in range(1, choices):
        moved = jnp.where(where_ref[1] == choice, moved_refs[choice][...], moved)
    rows_ref[...] = moved[:, :width]
    target = memory_ref.at[pl.ds(pl.multiple_of(first, count), count), :]
    copy = pltpu.make_async_copy(rows_ref, target, sem)
    copy.start()
    digits = moved[:, width:].astype(f32)
    labels = (digits[:, 0:1] * 256.0 + digits[:, 1:2]).astype(jnp.int32)
    new = labels_ref[...]
    slot = lax.broadcasted_iota(jnp.int32, new.shape, 0) * lanes + lax.broadcasted_iota(jnp.int32, new.shape, 1)
    for row in range(count):
        new = jnp.where(slot == first + row, labels[row : row + 1, :], new)
    new_labels_ref[...] = new
    copy.wait()


def patch(stored, labels, choices, where):
    count = choices[0].shape[0]
    width = stored.shape[1]
    return call(
        functools.partial(patch_kernel, len(choices)),
        [shaped(stored.shape, bf16), shaped(labels.shape, jnp.int32)],
        where, stored, labels, *choices,
        in_specs=[pl.BlockSpec(memory_space=pltpu.SMEM), pl.BlockSpec(memory_space=pl.ANY)]
        + [pl.BlockSpec(memory_space=pltpu.VMEM)] * (1 + len(choices)),
        out_specs=[pl.BlockSpec(memory_space=pl.ANY), pl.BlockSpec(memory_space=pltpu.VMEM)],
        scratch_shapes=[pltpu.VMEM((count, width), bf16), pltpu.SemaphoreType.DMA],
        input_output_aliases={1: 0},
    )


def pack_sums(values):
    rows = values[0].shape[0]
    lane = lax.broadcasted_iota(jnp.int32, (rows, lanes), 1)
    packed = jnp.zeros((rows, lanes), f32)
    for at, value in enumerate(values):
        high = value.astype(bf16).astype(f32)
        packed = jnp.where(lane == 2 * at, high, packed)
        packed = jnp.where(lane == 2 * at + 1, value - high, packed)
    return packed


def unpack_sums(packed):
    lane = lax.broadcasted_iota(jnp.int32, packed.shape, 1)
    return [
        jnp.sum(jnp.where((lane >= 2 * at) & (lane < 2 * at + 2), packed, 0.0), axis=1, keepdims=True)
        for at in range(4)
    ]


def block_kernel(sides, chunk, rows_ref, *refs):
    keys_refs, label_refs = refs[:sides], refs[sides : 2 * sides]
    out_ref, weight_ref = refs[-2:]
    slots, width = keys_refs[0].shape
    size = rows_ref.shape[0]
    anchors = rows_ref[:, :width]
    digits = rows_ref[:, width:].astype(f32)
    lane = lax.broadcasted_iota(jnp.int32, digits.shape, 1)
    digit = jnp.where(lane == 0, 256.0, jnp.where(lane == 1, 1.0, 0.0))
    labels = jnp.sum(digits * digit, axis=1, keepdims=True)
    pos_sum = jnp.zeros((size, 1), f32)
    neg_sum = jnp.zeros((size, 1), f32)
    for side in range(sides):
        slot_labels = label_refs[side][...].astype(f32)
        neg_shift = jnp.where(slot_labels < 0.0, -1e30, -neg_scale * margin * log2e)
        for start in range(0, slots, chunk):
            part = slice(start, start + chunk)
            scores = lax.dot_general(
                anchors, keys_refs[side][part, :], (((1,), (1,)), ((), ())), preferred_element_type=f32
            )
            same = labels == slot_labels[:, part]
            slope = jnp.where(same, -pos_scale * log2e, neg_scale * log2e)
            shift = jnp.where(same, pos_scale * margin * log2e, neg_shift[:, part])
            term = jnp.exp2(scores * slope + shift)
            pos = jnp.where(same, term, 0.0)
            neg = jnp.where(same, 0.0, term)
            pos_sum += jnp.sum(pos, axis=1, keepdims=True)
            neg_sum += jnp.sum(neg, axis=1, keepdims=True)
            to = slice(side * slots + start, side * slots + start + chunk)
            weight_ref[:size, to] = neg.astype(bf16)
            weight_ref[size:, to] = pos.astype(bf16)
    total = None
    for side in range(sides):
        part = weight_ref[:, side * slots : (side + 1) * slots]
        term = jnp.dot(part, keys_refs[side][...], preferred_element_type=f32)
        total = term if total is None else total + term
    floats = anchors.astype(f32)
    sums = [pos_sum, neg_sum]
    for which in range(2):
        value = total[which * size : (which + 1) * size, :]
        along = jnp.sum(value * floats, axis=1, keepdims=True)
        out_ref[:, which * width : (which + 1) * width] = (value - along * floats).astype(out_ref.dtype)
        sums.append(along)
    out_ref[:, 2 * width :] = pack_sums(sums).astype(out_ref.dtype)


def block_sums(rows, keys, labels, dtype, after):
    slots, width = keys[0].shape
    size = rows.shape[0]
    return call(
        functools.partial(block_kernel, len(keys), math.gcd(512, slots)),
        [shaped((size, 2 * width + lanes), dtype)],
        rows, *[in_vmem(k) for k in keys], *labels, *after,
        work=12 * size * slots * len(keys) * width,
        in_specs=[pl.BlockSpec(memory_space=pltpu.VMEM)] * (1 + 2 * len(keys))
        + [pl.BlockSpec(memory_space=pl.ANY)] * len(after),
        scratch_shapes=[pltpu.VMEM((2 * size, slots * len(keys)), bf16)],
    )[0]


def add_kernel(arrived, *refs):
    in_refs, out_refs = refs[: 1 + arrived], refs[1 + arrived :]
    rows, columns = out_refs[0].shape
    for block, out_ref in enumerate(out_refs):
        part = slice(block * rows, (block + 1) * rows)
        total = in_refs[0][part, :]
        for ref in in_refs[1:]:
            total = total + ref[part, :].astype(f32)
        out_ref[:, : columns - lanes] = total[:, : columns - lanes].astype(out_ref.dtype)
        sums = pack_sums(unpack_sums(total[:, columns - lanes :]))
        out_ref[:, columns - lanes :] = sums.astype(out_ref.dtype)


def add(held, arrived, blocks):
    rows, columns = held.shape
    outs = [shaped((rows // blocks, columns), f32 if b == 0 else bf16) for b in range(blocks)]
    return call(functools.partial(add_kernel, len(arrived)), outs, held, *arrived)


def finish_kernel(arrived, *refs):
    held_ref, arrived_refs = refs[0], refs[1 : 1 + arrived]
    unit_ref, radius_ref, grad_ref, loss_ref = refs[1 + arrived :]
    count, width = unit_ref.shape
    total = held_ref[...]
    for ref in arrived_refs:
        total = total + ref[...].astype(f32)
    pos, neg, push_along, pull_along = unpack_sums(total[:, 2 * width :])
    unit = unit_ref[...]
    anchors = unit.astype(bf16).astype(f32)
    push = total[:, :width] + push_along * anchors
    pull = total[:, width : 2 * width] + pull_along * anchors
    grad_unit = push / (1.0 + neg) - pull / (1.0 + pos)
    along = jnp.sum(unit * grad_unit, axis=1, keepdims=True)
    grad_ref[...] = (grad_unit - unit * along) / radius_ref[:, :1]
    loss = jnp.log(1.0 + pos) / pos_scale + jnp.log(1.0 + neg) / neg_scale
    spread = jnp.broadcast_to(loss, (count, count))
    loss_ref[...] = jnp.sum(jnp.where(diagonal(count), spread, 0.0), axis=0, keepdims=True)


def per_device(batch_rows, batch_labels, memory, memory_labels, keep_bits, step_index):
    groups = lax.axis_size("grp")
    members = lax.axis_size("dev")
    cores = 2 if members % 2 == 0 else 1
    line = members // cores
    devices_all = groups * members
    my_grp = lax.axis_index("grp")
    my_dev = lax.axis_index("dev")
    count, width = batch_rows.shape
    slots = memory.shape[0]

    def exchange(value, axis, step):
        if axis == "grp":
            return lax.ppermute(value, "grp", [(i, i ^ step) for i in range(groups)])
        jump = step * cores if axis == "line" else step
        return lax.ppermute(value, "dev", [(i, i ^ jump) for i in range(members)])

    folded = (slots // lanes, lanes)
    packed, unit, radius, slot_labels, copied_labels = call(
        prepare_kernel,
        [
            shaped((count, width + lanes), bf16),
            shaped((count, width), f32),
            shaped((count, lanes), f32),
            shaped(folded, jnp.int32),
            shaped(folded, jnp.int32),
        ],
        batch_rows, batch_labels.reshape(1, count), memory_labels.reshape(folded), keep_bits.reshape(folded),
        limit=vmem_most,
    )

    labels = [slot_labels] + [exchange(slot_labels, "core", s) for s in range(1, cores)]
    memories = [memory] + [exchange(memory, "core", s) for s in range(1, cores)]
    own_keys, copied = keys_of(memory)
    keys = [own_keys]

    near = [packed] + [None] * (line - 1)
    for s in range(line - 1, 0, -1):
        near[s] = exchange(packed, "line", s)
    part = join(near, [own_keys, *labels])
    labels = [value.reshape(1, slots) for value in labels]
    blocks = [part] + [None] * (groups - 1)
    for s in range(groups - 1, 1, -1):
        blocks[s] = exchange(part, "grp", s)
    for value in memories[1:]:
        other, part = other_keys(value, part)
        keys.append(other)
    if groups > 1:
        blocks[1] = exchange(part, "grp", 1)

    arrived, after = [], []
    for s in range(groups - 1, 0, -1):
        after = [block_sums(blocks[s], keys, labels, bf16, after)]
        arrived.append(exchange(after[0], "grp", s))
    held = block_sums(part, keys, labels, f32, after)
    sums, *parts = add(held, arrived, line)
    arrived = [exchange(parts[s - 1], "line", s) for s in range(line - 1, 0, -1)]
    grad_batch, loss = call(
        functools.partial(finish_kernel, len(arrived)),
        [shaped((count, width), f32), shaped((1, count), f32)],
        sums, *arrived, unit, radius,
    )

    step_value = step_index[0]
    first_slot = (step_value % (slots // count)) * count
    crossing = step_value % cores
    target = my_grp * members + (my_dev ^ crossing)
    source = (target - step_value) % devices_all
    source_grp, source_line = source // members, (source % members) // cores
    at = ((my_grp ^ source_grp) * line + ((my_dev // cores) ^ source_line)) * count
    moved = pick(blocks, at, count, after)
    choices = [moved] + [exchange(moved, "core", s) for s in range(1, cores)]
    new_memory, new_labels = patch(copied, copied_labels, choices, jnp.stack([first_slot, crossing]))
    return (grad_batch, loss.reshape(count), new_memory, new_labels.reshape(slots))


def solution(mesh):
    placed = (
        P(("grp", "dev"), None),
        P(("grp", "dev")),
        P(("grp", "dev"), None),
        P(("grp", "dev")),
        P(("grp", "dev")),
        P(),
    )
    return jax.shard_map(
        per_device,
        mesh=mesh,
        in_specs=placed,
        out_specs=(
            P(("grp", "dev"), None),
            P(("grp", "dev")),
            P(("grp", "dev"), None),
            P(("grp", "dev")),
        ),
        check_vma=False,
    )
```

```python
import functools
import math

import jax
import jax.numpy as jnp
from jax import lax
from jax.experimental import pallas as pl
from jax.experimental.pallas import tpu as pltpu
from jax.sharding import PartitionSpec as P

pos_scale = 2.0
neg_scale = 50.0
margin = 0.5
lanes = 128
log2e = math.log2(math.e)
vmem_bytes = 20 * 1024 * 1024
vmem_most = 56 * 1024 * 1024
f32 = jnp.float32
bf16 = jnp.bfloat16


def call(body, outs, *args, work=0, limit=vmem_bytes, **kw):
    return pl.pallas_call(
        body,
        out_shape=outs,
        compiler_params=pltpu.CompilerParams(vmem_limit_bytes=limit),
        cost_estimate=pl.CostEstimate(flops=work, bytes_accessed=0, transcendentals=0),
        **kw,
    )(*args)


def shaped(shape, dtype):
    return jax.ShapeDtypeStruct(shape, dtype)


def in_vmem(value):
    return pltpu.with_memory_space_constraint(value, pltpu.VMEM)


def prepare_kernel(rows_ref, labels_ref, stored_ref, keep_ref, packed_ref, unit_ref, radius_ref, slot_ref, copy_ref):
    stored = stored_ref[...]
    slot_ref[...] = jnp.where(keep_ref[...] > 0, stored, -1)
    copy_ref[...] = stored
    rows = rows_ref[...].astype(f32)
    count, width = rows.shape
    radius = jnp.sqrt(jnp.sum(rows * rows, axis=1, keepdims=True) + 1e-06)
    unit = rows / radius
    unit_ref[...] = unit
    radius_ref[...] = jnp.broadcast_to(radius, radius_ref.shape)
    packed_ref[:, :width] = unit.astype(bf16)
    column = to_column(labels_ref[...].astype(f32))
    high = jnp.floor(column * (1.0 / 256.0))
    low = column - high * 256.0
    lane = lax.broadcasted_iota(jnp.int32, (count, lanes), 1)
    digits = jnp.where(lane == 0, high, jnp.where(lane == 1, low, 0.0))
    packed_ref[:, width:] = digits.astype(bf16)


def diagonal(count):
    across = lax.broadcasted_iota(jnp.int32, (count, count), 1)
    down = lax.broadcasted_iota(jnp.int32, (count, count), 0)
    return across == down


def to_column(row):
    count = row.shape[1]
    spread = jnp.broadcast_to(row, (count, count))
    return jnp.sum(jnp.where(diagonal(count), spread, 0.0), axis=1, keepdims=True)


def keys_kernel(memory_ref, keys_ref, *copy_refs):
    stored = memory_ref[...]
    rows = stored.astype(f32)
    radius = jnp.sqrt(jnp.sum(rows * rows, axis=1, keepdims=True) + 1e-06)
    keys_ref[...] = (rows / radius).astype(bf16)
    for copy_ref in copy_refs:
        copy_ref[...] = stored


def keys_of(memory, copies):
    slots, width = memory.shape
    block = math.gcd(512, slots)
    spec = pl.BlockSpec((block, width), lambda i: (i, 0))
    return call(
        keys_kernel,
        [shaped((slots, width), bf16)] * (1 + copies),
        memory,
        grid=(slots // block,),
        in_specs=[spec],
        out_specs=[spec] * (1 + copies),
    )


def join_kernel(blocks, *refs):
    block_refs, out_ref = refs[:blocks], refs[-1]
    size = block_refs[0].shape[0]
    for place, ref in enumerate(block_refs):
        out_ref[place * size : (place + 1) * size, :] = ref[...]


def join(blocks, after):
    size, width = blocks[0].shape
    return call(
        functools.partial(join_kernel, len(blocks)),
        [shaped((size * len(blocks), width), blocks[0].dtype)],
        *blocks, *after,
        in_specs=[pl.BlockSpec(memory_space=pltpu.VMEM)] * len(blocks)
        + [pl.BlockSpec(memory_space=pl.ANY)] * len(after),
    )[0]


def other_keys_kernel(block, memory_ref, rows_ref, keys_ref, same_ref):
    same_ref[...] = rows_ref[...]

    @pl.loop(0, memory_ref.shape[0] // block)
    def _(i):
        part = pl.ds(pl.multiple_of(i * block, block), block)
        keys_ref[part, :] = normalized(memory_ref[part, :])


def other_keys(memory, rows):
    return call(
        functools.partial(other_keys_kernel, math.gcd(256, memory.shape[0])),
        [shaped(memory.shape, bf16), shaped(rows.shape, bf16)],
        memory, rows,
    )


def pick_kernel(groups, count, at_ref, *refs):
    blocks_refs, out_ref = refs[:groups], refs[-1]
    size = blocks_refs[0].shape[0]
    for place, ref in enumerate(blocks_refs):
        inside = at_ref[0] - place * size

        @pl.when((inside >= 0) & (inside < size))
        def _():
            out_ref[...] = ref[pl.ds(pl.multiple_of(inside, count), count), :]


def pick(blocks, at, count, after):
    return call(
        functools.partial(pick_kernel, len(blocks), count),
        [shaped((count, blocks[0].shape[1]), bf16)],
        at.reshape(1), *blocks, *after,
        in_specs=[pl.BlockSpec(memory_space=pltpu.SMEM)]
        + [pl.BlockSpec(memory_space=pltpu.VMEM)] * len(blocks)
        + [pl.BlockSpec(memory_space=pl.ANY)] * len(after),
    )[0]


def patch_kernel(choices, where_ref, stored_ref, labels_ref, *refs):
    moved_refs, (memory_ref, new_labels_ref, rows_ref, sem) = refs[:choices], refs[choices:]
    first = where_ref[0]
    count, width = rows_ref.shape
    moved = moved_refs[0][...]
    for choice in range(1, choices):
        moved = jnp.where(where_ref[1] == choice, moved_refs[choice][...], moved)
    rows_ref[...] = moved[:, :width]
    target = memory_ref.at[pl.ds(pl.multiple_of(first, count), count), :]
    copy = pltpu.make_async_copy(rows_ref, target, sem)
    copy.start()
    digits = moved[:, width:].astype(f32)
    labels = (digits[:, 0:1] * 256.0 + digits[:, 1:2]).astype(jnp.int32)
    new = labels_ref[...]
    slot = lax.broadcasted_iota(jnp.int32, new.shape, 0) * lanes + lax.broadcasted_iota(jnp.int32, new.shape, 1)
    for row in range(count):
        new = jnp.where(slot == first + row, labels[row : row + 1, :], new)
    new_labels_ref[...] = new
    copy.wait()


def patch(stored, labels, choices, where):
    count = choices[0].shape[0]
    width = stored.shape[1]
    return call(
        functools.partial(patch_kernel, len(choices)),
        [shaped(stored.shape, bf16), shaped(labels.shape, jnp.int32)],
        where, stored, labels, *choices,
        in_specs=[pl.BlockSpec(memory_space=pltpu.SMEM), pl.BlockSpec(memory_space=pl.ANY)]
        + [pl.BlockSpec(memory_space=pltpu.VMEM)] * (1 + len(choices)),
        out_specs=[pl.BlockSpec(memory_space=pl.ANY), pl.BlockSpec(memory_space=pltpu.VMEM)],
        scratch_shapes=[pltpu.VMEM((count, width), bf16), pltpu.SemaphoreType.DMA],
        input_output_aliases={1: 0},
    )


def pack_sums(values):
    rows = values[0].shape[0]
    lane = lax.broadcasted_iota(jnp.int32, (rows, lanes), 1)
    packed = jnp.zeros((rows, lanes), f32)
    for at, value in enumerate(values):
        high = value.astype(bf16).astype(f32)
        packed = jnp.where(lane == 2 * at, high, packed)
        packed = jnp.where(lane == 2 * at + 1, value - high, packed)
    return packed


def unpack_sums(packed):
    lane = lax.broadcasted_iota(jnp.int32, packed.shape, 1)
    return [
        jnp.sum(jnp.where((lane >= 2 * at) & (lane < 2 * at + 2), packed, 0.0), axis=1, keepdims=True)
        for at in range(4)
    ]


def block_kernel(sides, chunk, rows_ref, *refs):
    keys_refs, label_refs = refs[:sides], refs[sides : 2 * sides]
    out_ref = refs[-1]
    slots, width = keys_refs[0].shape
    size = rows_ref.shape[0]
    anchors = rows_ref[:, :width]
    digits = rows_ref[:, width:].astype(f32)
    lane = lax.broadcasted_iota(jnp.int32, digits.shape, 1)
    digit = jnp.where(lane == 0, 256.0, jnp.where(lane == 1, 1.0, 0.0))
    labels = jnp.sum(digits * digit, axis=1, keepdims=True)
    pos_sum = jnp.zeros((size, 1), f32)
    neg_sum = jnp.zeros((size, 1), f32)
    total = jnp.zeros((2 * size, width), f32)
    chunks = [(side, slice(at, at + chunk)) for side in range(sides) for at in range(0, slots, chunk)]

    def scores_of(side, part):
        return lax.dot_general(
            anchors, keys_refs[side][part, :], (((1,), (1,)), ((), ())), preferred_element_type=f32
        )

    scores = scores_of(*chunks[0])
    for at, (side, part) in enumerate(chunks):
        following = scores_of(*chunks[at + 1]) if at + 1 < len(chunks) else None
        slot_labels = label_refs[side][:, part].astype(f32)
        neg_shift = jnp.where(slot_labels < 0.0, -1e30, -neg_scale * margin * log2e)
        same = labels == slot_labels
        slope = jnp.where(same, -pos_scale * log2e, neg_scale * log2e)
        shift = jnp.where(same, pos_scale * margin * log2e, neg_shift)
        term = jnp.exp2(scores * slope + shift)
        pos = jnp.where(same, term, 0.0)
        neg = jnp.where(same, 0.0, term)
        pos_sum += jnp.sum(pos, axis=1, keepdims=True)
        neg_sum += jnp.sum(neg, axis=1, keepdims=True)
        weights = jnp.concatenate([neg.astype(bf16), pos.astype(bf16)], axis=0)
        total += jnp.dot(weights, keys_refs[side][part, :], preferred_element_type=f32)
        scores = following
    floats = anchors.astype(f32)
    sums = [pos_sum, neg_sum]
    for which in range(2):
        value = total[which * size : (which + 1) * size, :]
        along = jnp.sum(value * floats, axis=1, keepdims=True)
        out_ref[:, which * width : (which + 1) * width] = (value - along * floats).astype(out_ref.dtype)
        sums.append(along)
    out_ref[:, 2 * width :] = pack_sums(sums).astype(out_ref.dtype)


def block_sums(rows, keys, labels, dtype, after):
    slots, width = keys[0].shape
    size = rows.shape[0]
    return call(
        functools.partial(block_kernel, len(keys), math.gcd(512, slots)),
        [shaped((size, 2 * width + lanes), dtype)],
        rows, *[in_vmem(k) for k in keys], *labels, *after,
        work=12 * size * slots * len(keys) * width,
        in_specs=[pl.BlockSpec(memory_space=pltpu.VMEM)] * (1 + 2 * len(keys))
        + [pl.BlockSpec(memory_space=pl.ANY)] * len(after),
    )[0]


def add_kernel(arrived, *refs):
    in_refs, out_refs = refs[: 1 + arrived], refs[1 + arrived :]
    rows, columns = out_refs[0].shape
    for block, out_ref in enumerate(out_refs):
        part = slice(block * rows, (block + 1) * rows)
        total = in_refs[0][part, :]
        for ref in in_refs[1:]:
            total = total + ref[part, :].astype(f32)
        out_ref[:, : columns - lanes] = total[:, : columns - lanes].astype(out_ref.dtype)
        sums = pack_sums(unpack_sums(total[:, columns - lanes :]))
        out_ref[:, columns - lanes :] = sums.astype(out_ref.dtype)


def add(held, arrived, blocks):
    rows, columns = held.shape
    outs = [shaped((rows // blocks, columns), f32 if b == 0 else bf16) for b in range(blocks)]
    return call(functools.partial(add_kernel, len(arrived)), outs, held, *arrived)


def finish_kernel(arrived, *refs):
    held_ref, arrived_refs = refs[0], refs[1 : 1 + arrived]
    unit_ref, radius_ref, grad_ref, loss_ref = refs[1 + arrived :]
    count, width = unit_ref.shape
    total = held_ref[...]
    for ref in arrived_refs:
        total = total + ref[...].astype(f32)
    pos, neg, push_along, pull_along = unpack_sums(total[:, 2 * width :])
    unit = unit_ref[...]
    anchors = unit.astype(bf16).astype(f32)
    push = total[:, :width] + push_along * anchors
    pull = total[:, width : 2 * width] + pull_along * anchors
    grad_unit = push / (1.0 + neg) - pull / (1.0 + pos)
    along = jnp.sum(unit * grad_unit, axis=1, keepdims=True)
    grad_ref[...] = (grad_unit - unit * along) / radius_ref[:, :1]
    loss = jnp.log(1.0 + pos) / pos_scale + jnp.log(1.0 + neg) / neg_scale
    spread = jnp.broadcast_to(loss, (count, count))
    loss_ref[...] = jnp.sum(jnp.where(diagonal(count), spread, 0.0), axis=0, keepdims=True)


def per_device(batch_rows, batch_labels, memory, memory_labels, keep_bits, step_index):
    groups = lax.axis_size("grp")
    members = lax.axis_size("dev")
    cores = 2 if members % 2 == 0 else 1
    line = members // cores
    devices_all = groups * members
    my_grp = lax.axis_index("grp")
    my_dev = lax.axis_index("dev")
    count, width = batch_rows.shape
    slots = memory.shape[0]

    def exchange(value, axis, step):
        if axis == "grp":
            return lax.ppermute(value, "grp", [(i, i ^ step) for i in range(groups)])
        jump = step * cores if axis == "line" else step
        return lax.ppermute(value, "dev", [(i, i ^ jump) for i in range(members)])

    folded = (slots // lanes, lanes)
    packed, unit, radius, slot_labels, copied_labels = call(
        prepare_kernel,
        [
            shaped((count, width + lanes), bf16),
            shaped((count, width), f32),
            shaped((count, lanes), f32),
            shaped(folded, jnp.int32),
            shaped(folded, jnp.int32),
        ],
        batch_rows, batch_labels.reshape(1, count), memory_labels.reshape(folded), keep_bits.reshape(folded),
        limit=vmem_most,
    )

    labels = [slot_labels] + [exchange(slot_labels, "core", s) for s in range(1, cores)]
    memories = [memory] + [exchange(memory, "core", s) for s in range(1, cores)]
    own_keys, copied = keys_of(memory, 1)
    keys = [own_keys] + [keys_of(value, 0)[0] for value in memories[1:]]

    near = [packed] + [None] * (line - 1)
    for s in range(line - 1, 0, -1):
        near[s] = exchange(packed, "line", s)
    part = join(near, [*keys, *labels])
    labels = [value.reshape(1, slots) for value in labels]
    blocks = [part] + [None] * (groups - 1)
    for s in range(groups - 1, 0, -1):
        blocks[s] = exchange(part, "grp", s)

    arrived, after = [], []
    for s in range(groups - 1, 0, -1):
        after = [block_sums(blocks[s], keys, labels, bf16, after)]
        arrived.append(exchange(after[0], "grp", s))
    held = block_sums(part, keys, labels, f32, after)
    sums, *parts = add(held, arrived, line)
    arrived = [exchange(parts[s - 1], "line", s) for s in range(line - 1, 0, -1)]
    grad_batch, loss = call(
        functools.partial(finish_kernel, len(arrived)),
        [shaped((count, width), f32), shaped((1, count), f32)],
        sums, *arrived, unit, radius,
    )

    step_value = step_index[0]
    first_slot = (step_value % (slots // count)) * count
    crossing = step_value % cores
    target = my_grp * members + (my_dev ^ crossing)
    source = (target - step_value) % devices_all
    source_grp, source_line = source // members, (source % members) // cores
    at = ((my_grp ^ source_grp) * line + ((my_dev // cores) ^ source_line)) * count
    moved = pick(blocks, at, count, after)
    choices = [moved] + [exchange(moved, "core", s) for s in range(1, cores)]
    new_memory, new_labels = patch(copied, copied_labels, choices, jnp.stack([first_slot, crossing]))
    return (grad_batch, loss.reshape(count), new_memory, new_labels.reshape(slots))


def solution(mesh):
    placed = (
        P(("grp", "dev"), None),
        P(("grp", "dev")),
        P(("grp", "dev"), None),
        P(("grp", "dev")),
        P(("grp", "dev")),
        P(),
    )
    return jax.shard_map(
        per_device,
        mesh=mesh,
        in_specs=placed,
        out_specs=(
            P(("grp", "dev"), None),
            P(("grp", "dev")),
            P(("grp", "dev"), None),
            P(("grp", "dev")),
        ),
        check_vma=False,
    )
```

```python
import functools
import math

import jax
import jax.numpy as jnp
from jax import lax
from jax.experimental import pallas as pl
from jax.experimental.pallas import tpu as pltpu
from jax.sharding import PartitionSpec as P

pos_scale = 2.0
neg_scale = 50.0
margin = 0.5
lanes = 128
log2e = math.log2(math.e)
vmem_bytes = 20 * 1024 * 1024
vmem_most = 56 * 1024 * 1024
f32 = jnp.float32
bf16 = jnp.bfloat16


def call(body, outs, *args, work=0, limit=vmem_bytes, **kw):
    return pl.pallas_call(
        body,
        out_shape=outs,
        compiler_params=pltpu.CompilerParams(vmem_limit_bytes=limit),
        cost_estimate=pl.CostEstimate(flops=work, bytes_accessed=0, transcendentals=0),
        **kw,
    )(*args)


def shaped(shape, dtype):
    return jax.ShapeDtypeStruct(shape, dtype)


def in_vmem(value):
    return pltpu.with_memory_space_constraint(value, pltpu.VMEM)


def rounded_up(value, unit):
    return (value + unit - 1) // unit * unit


def blocks_of(width):
    return width // lanes


def rows_as_lanes(parts, rows):
    row = lax.broadcasted_iota(jnp.int32, (rows, lanes), 0)
    out = jnp.zeros((rows, lanes), f32)
    for at, part in enumerate(parts):
        out = jnp.where(row == at, part, out)
    return out


def prepare_kernel(rows_ref, labels_ref, stored_ref, keep_ref, packed_ref, unit_ref, radius_ref, slot_ref, copy_ref):
    stored = stored_ref[...]
    slot_ref[...] = jnp.where(keep_ref[...] > 0, stored, -1)
    copy_ref[...] = stored
    rows = rows_ref[...].astype(f32)
    count, width = rows.shape
    radius = jnp.sqrt(jnp.sum(rows * rows, axis=1, keepdims=True) + 1e-06)
    unit = rows / radius
    unit_ref[...] = unit
    radius_ref[...] = jnp.broadcast_to(radius, radius_ref.shape)
    anchors = unit.astype(bf16)
    for at in range(blocks_of(width)):
        packed_ref[at * count : (at + 1) * count, :] = anchors[:, at * lanes : (at + 1) * lanes]
    row = jnp.concatenate([labels_ref[...].astype(f32), jnp.zeros((1, lanes - count), f32)], axis=1)
    high = jnp.floor(row * (1.0 / 256.0))
    tail = packed_ref.shape[0] - blocks_of(width) * count
    packed_ref[blocks_of(width) * count :, :] = rows_as_lanes([high, row - high * 256.0], tail).astype(bf16)


def diagonal(count):
    across = lax.broadcasted_iota(jnp.int32, (count, count), 1)
    down = lax.broadcasted_iota(jnp.int32, (count, count), 0)
    return across == down


def to_column(row):
    count = row.shape[1]
    spread = jnp.broadcast_to(row, (count, count))
    return jnp.sum(jnp.where(diagonal(count), spread, 0.0), axis=1, keepdims=True)


def to_row(column):
    count = column.shape[0]
    spread = jnp.broadcast_to(column, (count, count))
    return jnp.sum(jnp.where(diagonal(count), spread, 0.0), axis=0, keepdims=True)


def keys_kernel(memory_ref, keys_ref, *copy_refs):
    stored = memory_ref[...]
    rows = stored.astype(f32)
    radius = jnp.sqrt(jnp.sum(rows * rows, axis=1, keepdims=True) + 1e-06)
    keys_ref[...] = (rows / radius).astype(bf16)
    for copy_ref in copy_refs:
        copy_ref[...] = stored


def keys_of(memory, copies):
    slots, width = memory.shape
    block = math.gcd(512, slots)
    spec = pl.BlockSpec((block, width), lambda i: (i, 0))
    return call(
        keys_kernel,
        [shaped((slots, width), bf16)] * (1 + copies),
        memory,
        grid=(slots // block,),
        in_specs=[spec],
        out_specs=[spec] * (1 + copies),
    )


def join_kernel(blocks, *refs):
    block_refs, out_ref = refs[:blocks], refs[-1]
    size = block_refs[0].shape[0]
    for place, ref in enumerate(block_refs):
        out_ref[place * size : (place + 1) * size, :] = ref[...]


def join(blocks, after):
    size, width = blocks[0].shape
    return call(
        functools.partial(join_kernel, len(blocks)),
        [shaped((size * len(blocks), width), blocks[0].dtype)],
        *blocks, *after,
        in_specs=[pl.BlockSpec(memory_space=pltpu.VMEM)] * len(blocks)
        + [pl.BlockSpec(memory_space=pl.ANY)] * len(after),
    )[0]


def other_keys_kernel(block, memory_ref, rows_ref, keys_ref, same_ref):
    same_ref[...] = rows_ref[...]

    @pl.loop(0, memory_ref.shape[0] // block)
    def _(i):
        part = pl.ds(pl.multiple_of(i * block, block), block)
        keys_ref[part, :] = normalized(memory_ref[part, :])


def other_keys(memory, rows):
    return call(
        functools.partial(other_keys_kernel, math.gcd(256, memory.shape[0])),
        [shaped(memory.shape, bf16), shaped(rows.shape, bf16)],
        memory, rows,
    )


def positions(step, count, slots, groups, line, cores):
    first = lax.rem(step, slots // count) * count
    crossing = lax.rem(step, cores)
    members = line * cores
    devices_all = groups * members
    grp = lax.axis_index("grp")
    dev = lax.axis_index("dev")
    target = grp * members + (dev ^ crossing)
    source = lax.rem(target + devices_all - lax.rem(step, devices_all), devices_all)
    source_grp = lax.div(source, members)
    source_line = lax.div(lax.rem(source, members), cores)
    return first, crossing, grp ^ source_grp, lax.div(dev, cores) ^ source_line


def pick_kernel(groups, sizes, step_ref, *refs):
    blocks_refs, out_ref = refs[:groups], refs[-1]
    rows = out_ref.shape[0]
    _, _, grp_place, line_place = positions(step_ref[0], *sizes)
    for place, ref in enumerate(blocks_refs):

        @pl.when(grp_place == place)
        def _():
            out_ref[...] = ref[pl.ds(pl.multiple_of(line_place * rows, 16), rows), :]


def pick(blocks, step, sizes, after):
    line = sizes[3]
    return call(
        functools.partial(pick_kernel, len(blocks), sizes),
        [shaped((blocks[0].shape[0] // line, lanes), bf16)],
        step, *blocks, *after,
        in_specs=[pl.BlockSpec(memory_space=pltpu.SMEM)]
        + [pl.BlockSpec(memory_space=pltpu.VMEM)] * len(blocks)
        + [pl.BlockSpec(memory_space=pl.ANY)] * len(after),
    )[0]


def patch_kernel(choices, sizes, step_ref, stored_ref, labels_ref, *refs):
    moved_refs, (memory_ref, new_labels_ref, rows_ref, sem) = refs[:choices], refs[choices:]
    count, width = rows_ref.shape
    first, crossing, _, _ = positions(step_ref[0], *sizes)
    moved = moved_refs[0][...]
    for choice in range(1, choices):
        moved = jnp.where(crossing == choice, moved_refs[choice][...], moved)
    for at in range(blocks_of(width)):
        rows_ref[:, at * lanes : (at + 1) * lanes] = moved[at * count : (at + 1) * count, :]
    target = memory_ref.at[pl.ds(pl.multiple_of(first, count), count), :]
    copy = pltpu.make_async_copy(rows_ref, target, sem)
    copy.start()
    digits = moved[blocks_of(width) * count :, :].astype(f32)
    row = (digits[0:1, :] * 256.0 + digits[1:2, :]).astype(jnp.int32)
    old = labels_ref[...]
    turned = pltpu.roll(jnp.broadcast_to(row, old.shape), lax.rem(first, lanes), 1)
    slot = lax.broadcasted_iota(jnp.int32, old.shape, 0) * lanes + lax.broadcasted_iota(jnp.int32, old.shape, 1)
    new_labels_ref[...] = jnp.where((slot >= first) & (slot < first + count), turned, old)
    copy.wait()


def patch(stored, labels, choices, step, sizes):
    count, width = sizes[0], stored.shape[1]
    return call(
        functools.partial(patch_kernel, len(choices), sizes),
        [shaped(stored.shape, bf16), shaped(labels.shape, jnp.int32)],
        step, stored, labels, *choices,
        in_specs=[pl.BlockSpec(memory_space=pltpu.SMEM), pl.BlockSpec(memory_space=pl.ANY)]
        + [pl.BlockSpec(memory_space=pltpu.VMEM)] * (1 + len(choices)),
        out_specs=[pl.BlockSpec(memory_space=pl.ANY), pl.BlockSpec(memory_space=pltpu.VMEM)],
        scratch_shapes=[pltpu.VMEM((count, width), bf16), pltpu.SemaphoreType.DMA],
        input_output_aliases={1: 0},
    )


def split_digits(row):
    high = row.astype(bf16).astype(f32)
    return [high, row - high]


def sum_rows(size):
    return rounded_up(8 * (rounded_up(size, lanes) // lanes), 16)


def block_kernel(blocks, sides, chunk, count, *refs):
    rows_refs, keys_refs = refs[:blocks], refs[blocks : blocks + sides]
    label_refs = refs[blocks + sides : blocks + 2 * sides]
    out_refs = refs[-1 - blocks : -1]
    anchors_ref = refs[-1]
    slots, width = keys_refs[0].shape
    parts = blocks_of(width)
    packed = rows_refs[0].shape[0]
    members = packed // (parts * count + 16)
    size = members * count
    columns = []
    for block, ref in enumerate(rows_refs):
        for member in range(members):
            first = member * (parts * count + 16)
            to = block * size + member * count
            for at in range(parts):
                anchors_ref[to : to + count, at * lanes : (at + 1) * lanes] = ref[
                    first + at * count : first + (at + 1) * count, :
                ]
            digits = ref[first + parts * count : first + parts * count + 16, :].astype(f32)
            columns.append(to_column((digits[0:1, :] * 256.0 + digits[1:2, :])[:, :count]))
    labels = jnp.concatenate(columns, axis=0)
    anchors = anchors_ref[...]
    rows = blocks * size
    pos_sum = jnp.zeros((rows, 1), f32)
    neg_sum = jnp.zeros((rows, 1), f32)
    total = None
    chunks = [(side, slice(at, at + chunk)) for side in range(sides) for at in range(0, slots, chunk)]

    def scores_of(side, part):
        return lax.dot_general(
            anchors, keys_refs[side][part, :], (((1,), (1,)), ((), ())), preferred_element_type=f32
        )

    scores = scores_of(*chunks[0])
    for at, (side, part) in enumerate(chunks):
        following = scores_of(*chunks[at + 1]) if at + 1 < len(chunks) else None
        slot_labels = label_refs[side][:, part].astype(f32)
        neg_shift = jnp.where(slot_labels < 0.0, -1e30, -neg_scale * margin * log2e)
        same = labels == slot_labels
        slope = jnp.where(same, -pos_scale * log2e, neg_scale * log2e)
        shift = jnp.where(same, pos_scale * margin * log2e, neg_shift)
        term = jnp.exp2(scores * slope + shift)
        pos = jnp.where(same, term, 0.0)
        neg = jnp.where(same, 0.0, term)
        pos_sum += jnp.sum(pos, axis=1, keepdims=True)
        neg_sum += jnp.sum(neg, axis=1, keepdims=True)
        weights = jnp.concatenate([neg.astype(bf16), pos.astype(bf16)], axis=0)
        more = jnp.dot(weights, keys_refs[side][part, :], preferred_element_type=f32)
        total = more if total is None else total + more
        scores = following
    floats = anchors.astype(f32)
    sums = [pos_sum, neg_sum]
    for which in range(2):
        value = total[which * rows : (which + 1) * rows, :]
        along = jnp.sum(value * floats, axis=1, keepdims=True)
        sums.append(along)
        rest = value - along * floats
        for block, ref in enumerate(out_refs):
            for at in range(parts):
                first = (which * parts + at) * size
                ref[first : first + size, :] = rest[
                    block * size : (block + 1) * size, at * lanes : (at + 1) * lanes
                ].astype(ref.dtype)
    for block, ref in enumerate(out_refs):
        lines = []
        for first in range(0, size, lanes):
            last = min(first + lanes, size)
            for value in sums:
                row = to_row(value[block * size + first : block * size + last])
                if last - first < lanes:
                    row = jnp.concatenate([row, jnp.zeros((1, lanes - last + first), f32)], axis=1)
                lines += split_digits(row)
        first = 2 * parts * size
        ref[first:, :] = rows_as_lanes(lines, ref.shape[0] - first).astype(ref.dtype)


def block_sums(blocks, keys, labels, count, dtype, after):
    slots, width = keys[0].shape
    parts = blocks_of(width)
    size = blocks[0].shape[0] // (parts * count + 16) * count
    return call(
        functools.partial(block_kernel, len(blocks), len(keys), math.gcd(1024, slots), count),
        [shaped((2 * parts * size + sum_rows(size), lanes), dtype)] * len(blocks),
        *blocks, *[in_vmem(k) for k in keys], *labels, *after,
        work=12 * size * len(blocks) * slots * len(keys) * width,
        in_specs=[pl.BlockSpec(memory_space=pltpu.VMEM)] * (len(blocks) + 2 * len(keys))
        + [pl.BlockSpec(memory_space=pl.ANY)] * len(after),
        scratch_shapes=[pltpu.VMEM((len(blocks) * size, width), bf16)],
    )


def add_kernel(arrived, size, count, *refs):
    in_refs, out_refs = refs[: 1 + arrived], refs[-(size // count) :]
    columns = (in_refs[0].shape[0] - sum_rows(size)) // size

    def total(first, rows):
        value = in_refs[0][first : first + rows, :]
        for ref in in_refs[1:]:
            value = value + ref[first : first + rows, :].astype(f32)
        return value

    sums = total(columns * size, sum_rows(size))
    for block, ref in enumerate(out_refs):
        for at in range(columns):
            part = total(at * size + block * count, count)
            ref[at * count : (at + 1) * count, :] = part.astype(ref.dtype)
        group, lane = divmod(block * count, lanes)
        lines = []
        for which in range(4):
            row = 8 * group + 2 * which
            lines += split_digits(sums[row : row + 1, :] + sums[row + 1 : row + 2, :])
        packed = rows_as_lanes(lines, ref.shape[0] - columns * count)
        if lane:
            packed = pltpu.roll(packed, lanes - lane, 1)
        ref[columns * count :, :] = packed.astype(ref.dtype)


def add(held, arrived, size, count, columns, after):
    shape = (columns * count + sum_rows(count), lanes)
    outs = [shaped(shape, f32 if b == 0 else bf16) for b in range(size // count)]
    return call(
        functools.partial(add_kernel, len(arrived), size, count),
        outs,
        held, *arrived, *after,
        in_specs=[pl.BlockSpec(memory_space=pltpu.VMEM)] * (1 + len(arrived))
        + [pl.BlockSpec(memory_space=pl.ANY)] * len(after),
    )


def finish_kernel(arrived, *refs):
    held_ref, arrived_refs = refs[0], refs[1 : 1 + arrived]
    unit_ref, radius_ref, grad_ref, loss_ref = refs[1 + arrived :]
    count, width = unit_ref.shape
    parts = blocks_of(width)
    total = held_ref[...]
    for ref in arrived_refs:
        total = total + ref[...].astype(f32)
    sums = []
    for which in range(4):
        row = 2 * parts * count + 2 * which
        sums.append((total[row : row + 1, :] + total[row + 1 : row + 2, :])[:, :count])
    pos, neg = sums[:2]
    loss_ref[...] = jnp.log(1.0 + pos) / pos_scale + jnp.log(1.0 + neg) / neg_scale
    pos, neg, push_along, pull_along = [to_column(row) for row in sums]
    unit = unit_ref[...]
    anchors = unit.astype(bf16).astype(f32)
    push, pull = [
        jnp.concatenate([total[(first + at) * count : (first + at + 1) * count, :] for at in range(parts)], axis=1)
        for first in (0, parts)
    ]
    push = push + push_along * anchors
    pull = pull + pull_along * anchors
    grad_unit = push / (1.0 + neg) - pull / (1.0 + pos)
    along = jnp.sum(unit * grad_unit, axis=1, keepdims=True)
    grad_ref[...] = (grad_unit - unit * along) / radius_ref[:, :1]


def per_device(batch_rows, batch_labels, memory, memory_labels, keep_bits, step_index):
    groups = lax.axis_size("grp")
    members = lax.axis_size("dev")
    cores = 2 if members % 2 == 0 else 1
    line = members // cores
    count, width = batch_rows.shape
    slots = memory.shape[0]

    def exchange(value, axis, step):
        if axis == "grp":
            return lax.ppermute(value, "grp", [(i, i ^ step) for i in range(groups)])
        jump = step * cores if axis == "line" else step
        return lax.ppermute(value, "dev", [(i, i ^ jump) for i in range(members)])

    folded = (slots // lanes, lanes)
    parts = blocks_of(width)
    packed, unit, radius, slot_labels, copied_labels = call(
        prepare_kernel,
        [
            pltpu.VMEM((parts * count + 16, lanes), bf16),
            pltpu.VMEM((count, width), f32),
            pltpu.VMEM((count, lanes), f32),
            pltpu.VMEM(folded, jnp.int32),
            pltpu.VMEM(folded, jnp.int32),
        ],
        batch_rows, batch_labels.reshape(1, count), memory_labels.reshape(folded), keep_bits.reshape(folded),
        limit=vmem_most,
    )

    labels = [slot_labels] + [exchange(slot_labels, "core", s) for s in range(1, cores)]
    memories = [memory] + [exchange(memory, "core", s) for s in range(1, cores)]
    own_keys, copied = keys_of(memory, 1)
    keys = [own_keys] + [keys_of(value, 0)[0] for value in memories[1:]]

    near = [packed] + [None] * (line - 1)
    for s in range(line - 1, 0, -1):
        near[s] = exchange(packed, "line", s)
    part = join(near, [*keys, *labels])
    labels = [value.reshape(1, slots) for value in labels]
    blocks = [part] + [None] * (groups - 1)
    for s in range(groups - 1, 0, -1):
        blocks[s] = exchange(part, "grp", s)

    size = count * line
    arrived, after = [], []
    places = list(range(groups - 1, 0, -1))
    while places:
        now = places[:1] if not after else places[:2]
        places = places[len(now) :]
        after = block_sums([blocks[s] for s in now], keys, labels, count, bf16, after)
        arrived += [exchange(value, "grp", s) for s, value in zip(now, after)]
    held = block_sums([part], keys, labels, count, f32, after)[0]
    sizes = (count, slots, groups, line, cores)
    moved = pick(blocks, step_index, sizes, after)
    choices = [moved] + [exchange(moved, "core", s) for s in range(1, cores)]

    sums, *others = add(held, arrived, size, count, 2 * parts, choices)
    arrived = [exchange(others[s - 1], "line", s) for s in range(line - 1, 0, -1)]
    grad_batch, loss = call(
        functools.partial(finish_kernel, len(arrived)),
        [shaped((count, width), f32), shaped((1, count), f32)],
        sums, *arrived, unit, radius,
    )

    new_memory, new_labels = patch(copied, copied_labels, choices, step_index, sizes)
    return (grad_batch, loss.reshape(count), new_memory, new_labels.reshape(slots))


def solution(mesh):
    placed = (
        P(("grp", "dev"), None),
        P(("grp", "dev")),
        P(("grp", "dev"), None),
        P(("grp", "dev")),
        P(("grp", "dev")),
        P(),
    )
    return jax.shard_map(
        per_device,
        mesh=mesh,
        in_specs=placed,
        out_specs=(
            P(("grp", "dev"), None),
            P(("grp", "dev")),
            P(("grp", "dev"), None),
            P(("grp", "dev")),
        ),
        check_vma=False,
    )
```

```python
import functools
import math

import jax
import jax.numpy as jnp
from jax import lax
from jax.experimental import pallas as pl
from jax.experimental.pallas import tpu as pltpu
from jax.sharding import PartitionSpec as P

pos_scale = 2.0
neg_scale = 50.0
margin = 0.5
lanes = 128
log2e = math.log2(math.e)
vmem_bytes = 20 * 1024 * 1024
vmem_most = 56 * 1024 * 1024
f32 = jnp.float32
bf16 = jnp.bfloat16


def call(body, outs, *args, work=0, limit=vmem_bytes, **kw):
    return pl.pallas_call(
        body,
        out_shape=outs,
        compiler_params=pltpu.CompilerParams(vmem_limit_bytes=limit),
        cost_estimate=pl.CostEstimate(flops=work, bytes_accessed=0, transcendentals=0),
        **kw,
    )(*args)


def shaped(shape, dtype):
    return jax.ShapeDtypeStruct(shape, dtype)


def in_vmem(value):
    return pltpu.with_memory_space_constraint(value, pltpu.VMEM)


def rounded_up(value, unit):
    return (value + unit - 1) // unit * unit


def blocks_of(width):
    return width // lanes


def rows_as_lanes(parts, rows):
    row = lax.broadcasted_iota(jnp.int32, (rows, lanes), 0)
    out = jnp.zeros((rows, lanes), f32)
    for at, part in enumerate(parts):
        out = jnp.where(row == at, part, out)
    return out


def prepare_kernel(rows_ref, labels_ref, stored_ref, keep_ref, step_ref, *refs):
    packed_ref, unit_ref, radius_ref, slot_ref, copy_ref, step_out_ref = refs
    step_out_ref[...] = jnp.broadcast_to(step_ref[...], step_out_ref.shape)
    stored = stored_ref[...]
    slot_ref[...] = jnp.where(keep_ref[...] > 0, stored, -1)
    copy_ref[...] = stored
    rows = rows_ref[...].astype(f32)
    count, width = rows.shape
    radius = jnp.sqrt(jnp.sum(rows * rows, axis=1, keepdims=True) + 1e-06)
    unit = rows / radius
    unit_ref[...] = unit
    radius_ref[...] = jnp.broadcast_to(radius, radius_ref.shape)
    anchors = unit.astype(bf16)
    for at in range(blocks_of(width)):
        packed_ref[at * count : (at + 1) * count, :] = anchors[:, at * lanes : (at + 1) * lanes]
    row = jnp.concatenate([labels_ref[...].astype(f32), jnp.zeros((1, lanes - count), f32)], axis=1)
    high = jnp.floor(row * (1.0 / 256.0))
    tail = packed_ref.shape[0] - blocks_of(width) * count
    packed_ref[blocks_of(width) * count :, :] = rows_as_lanes([high, row - high * 256.0], tail).astype(bf16)


def diagonal(count):
    across = lax.broadcasted_iota(jnp.int32, (count, count), 1)
    down = lax.broadcasted_iota(jnp.int32, (count, count), 0)
    return across == down


def to_column(row):
    count = row.shape[1]
    spread = jnp.broadcast_to(row, (count, count))
    return jnp.sum(jnp.where(diagonal(count), spread, 0.0), axis=1, keepdims=True)


def to_row(column):
    count = column.shape[0]
    spread = jnp.broadcast_to(column, (count, count))
    return jnp.sum(jnp.where(diagonal(count), spread, 0.0), axis=0, keepdims=True)


def keys_kernel(memory_ref, keys_ref, *copy_refs):
    stored = memory_ref[...]
    rows = stored.astype(f32)
    radius = jnp.sqrt(jnp.sum(rows * rows, axis=1, keepdims=True) + 1e-06)
    keys_ref[...] = (rows / radius).astype(bf16)
    for copy_ref in copy_refs:
        copy_ref[...] = stored


def keys_of(memory, copies, place):
    slots, width = memory.shape
    block = math.gcd(512, slots)
    spec = pl.BlockSpec((block, width), lambda i: (i, 0))
    return call(
        keys_kernel,
        [shaped((slots, width), bf16)] * (1 + copies),
        pltpu.with_memory_space_constraint(memory, place),
        grid=(slots // block,),
        in_specs=[spec],
        out_specs=[spec] * (1 + copies),
    )


def join_kernel(blocks, *refs):
    block_refs, out_ref = refs[:blocks], refs[-1]
    size = block_refs[0].shape[0]
    for place, ref in enumerate(block_refs):
        out_ref[place * size : (place + 1) * size, :] = ref[...]


def join(blocks, after):
    size, width = blocks[0].shape
    return call(
        functools.partial(join_kernel, len(blocks)),
        [shaped((size * len(blocks), width), blocks[0].dtype)],
        *blocks, *after,
        in_specs=[pl.BlockSpec(memory_space=pltpu.VMEM)] * len(blocks)
        + [pl.BlockSpec(memory_space=pl.ANY)] * len(after),
    )[0]


def other_keys_kernel(block, memory_ref, rows_ref, keys_ref, same_ref):
    same_ref[...] = rows_ref[...]

    @pl.loop(0, memory_ref.shape[0] // block)
    def _(i):
        part = pl.ds(pl.multiple_of(i * block, block), block)
        keys_ref[part, :] = normalized(memory_ref[part, :])


def other_keys(memory, rows):
    return call(
        functools.partial(other_keys_kernel, math.gcd(256, memory.shape[0])),
        [shaped(memory.shape, bf16), shaped(rows.shape, bf16)],
        memory, rows,
    )


def positions(step, count, slots, groups, line, cores):
    first = lax.rem(step, slots // count) * count
    crossing = lax.rem(step, cores)
    members = line * cores
    devices_all = groups * members
    grp = lax.axis_index("grp")
    dev = lax.axis_index("dev")
    target = grp * members + (dev ^ crossing)
    source = lax.rem(target + devices_all - lax.rem(step, devices_all), devices_all)
    source_grp = lax.div(source, members)
    source_line = lax.div(lax.rem(source, members), cores)
    return first, crossing, grp ^ source_grp, lax.div(dev, cores) ^ source_line


def read_step(step_ref, scalar_ref, sem):
    copy = pltpu.make_async_copy(step_ref, scalar_ref, sem)
    copy.start()
    copy.wait()
    return scalar_ref[0, 0]


def pick_kernel(groups, sizes, step_ref, *refs):
    blocks_refs, (out_ref, scalar_ref, sem) = refs[:groups], refs[-3:]
    rows = out_ref.shape[0]
    _, _, grp_place, line_place = positions(read_step(step_ref, scalar_ref, sem), *sizes)
    for place, ref in enumerate(blocks_refs):

        @pl.when(grp_place == place)
        def _():
            out_ref[...] = ref[pl.ds(pl.multiple_of(line_place * rows, 16), rows), :]


def pick(blocks, step, sizes, after):
    line = sizes[3]
    return call(
        functools.partial(pick_kernel, len(blocks), sizes),
        [shaped((blocks[0].shape[0] // line, lanes), bf16)],
        step, *blocks, *after,
        in_specs=[pl.BlockSpec(memory_space=pl.ANY)]
        + [pl.BlockSpec(memory_space=pltpu.VMEM)] * len(blocks)
        + [pl.BlockSpec(memory_space=pl.ANY)] * len(after),
        scratch_shapes=[pltpu.SMEM((8, lanes), jnp.int32), pltpu.SemaphoreType.DMA],
    )[0]


def patch_kernel(choices, sizes, step_ref, stored_ref, labels_ref, *refs):
    moved_refs, (memory_ref, new_labels_ref, rows_ref, scalar_ref, sem) = refs[:choices], refs[choices:]
    count, width = rows_ref.shape
    first, crossing, _, _ = positions(read_step(step_ref, scalar_ref, sem), *sizes)
    moved = moved_refs[0][...]
    for choice in range(1, choices):
        moved = jnp.where(crossing == choice, moved_refs[choice][...], moved)
    for at in range(blocks_of(width)):
        rows_ref[:, at * lanes : (at + 1) * lanes] = moved[at * count : (at + 1) * count, :]
    target = memory_ref.at[pl.ds(pl.multiple_of(first, count), count), :]
    copy = pltpu.make_async_copy(rows_ref, target, sem)
    copy.start()
    digits = moved[blocks_of(width) * count :, :].astype(f32)
    row = (digits[0:1, :] * 256.0 + digits[1:2, :]).astype(jnp.int32)
    old = labels_ref[...]
    turned = pltpu.roll(jnp.broadcast_to(row, old.shape), lax.rem(first, lanes), 1)
    slot = lax.broadcasted_iota(jnp.int32, old.shape, 0) * lanes + lax.broadcasted_iota(jnp.int32, old.shape, 1)
    new_labels_ref[...] = jnp.where((slot >= first) & (slot < first + count), turned, old)
    copy.wait()


def patch(stored, labels, choices, step, sizes):
    count, width = sizes[0], stored.shape[1]
    return call(
        functools.partial(patch_kernel, len(choices), sizes),
        [shaped(stored.shape, bf16), shaped(labels.shape, jnp.int32)],
        step, stored, labels, *choices,
        in_specs=[pl.BlockSpec(memory_space=pl.ANY)] * 2
        + [pl.BlockSpec(memory_space=pltpu.VMEM)] * (1 + len(choices)),
        out_specs=[pl.BlockSpec(memory_space=pl.ANY), pl.BlockSpec(memory_space=pltpu.VMEM)],
        scratch_shapes=[
            pltpu.VMEM((count, width), bf16),
            pltpu.SMEM((8, lanes), jnp.int32),
            pltpu.SemaphoreType.DMA,
        ],
        input_output_aliases={1: 0},
    )


def split_digits(row):
    high = row.astype(bf16).astype(f32)
    return [high, row - high]


def sum_rows(size):
    return rounded_up(8 * (rounded_up(size, lanes) // lanes), 16)


def block_kernel(blocks, sides, chunk, count, *refs):
    rows_refs, keys_refs = refs[:blocks], refs[blocks : blocks + sides]
    label_refs = refs[blocks + sides : blocks + 2 * sides]
    out_refs = refs[-1 - blocks : -1]
    anchors_ref = refs[-1]
    slots, width = keys_refs[0].shape
    parts = blocks_of(width)
    packed = rows_refs[0].shape[0]
    members = packed // (parts * count + 16)
    size = members * count
    columns = []
    for block, ref in enumerate(rows_refs):
        for member in range(members):
            first = member * (parts * count + 16)
            to = block * size + member * count
            for at in range(parts):
                anchors_ref[to : to + count, at * lanes : (at + 1) * lanes] = ref[
                    first + at * count : first + (at + 1) * count, :
                ]
            digits = ref[first + parts * count : first + parts * count + 16, :].astype(f32)
            columns.append(to_column((digits[0:1, :] * 256.0 + digits[1:2, :])[:, :count]))
    labels = jnp.concatenate(columns, axis=0)
    anchors = anchors_ref[...]
    rows = blocks * size
    pos_sum = jnp.zeros((rows, 1), f32)
    neg_sum = jnp.zeros((rows, 1), f32)
    total = None
    chunks = [(side, slice(at, at + chunk)) for side in range(sides) for at in range(0, slots, chunk)]

    def scores_of(side, part):
        return lax.dot_general(
            anchors, keys_refs[side][part, :], (((1,), (1,)), ((), ())), preferred_element_type=f32
        )

    scores = scores_of(*chunks[0])
    for at, (side, part) in enumerate(chunks):
        following = scores_of(*chunks[at + 1]) if at + 1 < len(chunks) else None
        slot_labels = label_refs[side][:, part].astype(f32)
        neg_shift = jnp.where(slot_labels < 0.0, -1e30, -neg_scale * margin * log2e)
        same = labels == slot_labels
        slope = jnp.where(same, -pos_scale * log2e, neg_scale * log2e)
        shift = jnp.where(same, pos_scale * margin * log2e, neg_shift)
        term = jnp.exp2(scores * slope + shift)
        pos = jnp.where(same, term, 0.0)
        neg = jnp.where(same, 0.0, term)
        pos_sum += jnp.sum(pos, axis=1, keepdims=True)
        neg_sum += jnp.sum(neg, axis=1, keepdims=True)
        weights = jnp.concatenate([neg.astype(bf16), pos.astype(bf16)], axis=0)
        more = jnp.dot(weights, keys_refs[side][part, :], preferred_element_type=f32)
        total = more if total is None else total + more
        scores = following
    floats = anchors.astype(f32)
    sums = [pos_sum, neg_sum]
    for which in range(2):
        value = total[which * rows : (which + 1) * rows, :]
        along = jnp.sum(value * floats, axis=1, keepdims=True)
        sums.append(along)
        rest = value - along * floats
        for block, ref in enumerate(out_refs):
            for at in range(parts):
                first = (which * parts + at) * size
                ref[first : first + size, :] = rest[
                    block * size : (block + 1) * size, at * lanes : (at + 1) * lanes
                ].astype(ref.dtype)
    for block, ref in enumerate(out_refs):
        lines = []
        for first in range(0, size, lanes):
            last = min(first + lanes, size)
            for value in sums:
                row = to_row(value[block * size + first : block * size + last])
                if last - first < lanes:
                    row = jnp.concatenate([row, jnp.zeros((1, lanes - last + first), f32)], axis=1)
                lines += split_digits(row)
        first = 2 * parts * size
        ref[first:, :] = rows_as_lanes(lines, ref.shape[0] - first).astype(ref.dtype)


def block_sums(blocks, keys, labels, count, dtype, after):
    slots, width = keys[0].shape
    parts = blocks_of(width)
    size = blocks[0].shape[0] // (parts * count + 16) * count
    return call(
        functools.partial(block_kernel, len(blocks), len(keys), math.gcd(1024, slots), count),
        [shaped((2 * parts * size + sum_rows(size), lanes), dtype)] * len(blocks),
        *blocks, *[in_vmem(k) for k in keys], *labels, *after,
        work=12 * size * len(blocks) * slots * len(keys) * width,
        in_specs=[pl.BlockSpec(memory_space=pltpu.VMEM)] * (len(blocks) + 2 * len(keys))
        + [pl.BlockSpec(memory_space=pl.ANY)] * len(after),
        scratch_shapes=[pltpu.VMEM((len(blocks) * size, width), bf16)],
    )


def add_kernel(arrived, size, count, *refs):
    in_refs, out_refs = refs[: 1 + arrived], refs[-(size // count) :]
    columns = (in_refs[0].shape[0] - sum_rows(size)) // size

    def total(first, rows):
        value = in_refs[0][first : first + rows, :]
        for ref in in_refs[1:]:
            value = value + ref[first : first + rows, :].astype(f32)
        return value

    sums = total(columns * size, sum_rows(size))
    for block, ref in enumerate(out_refs):
        for at in range(columns):
            part = total(at * size + block * count, count)
            ref[at * count : (at + 1) * count, :] = part.astype(ref.dtype)
        group, lane = divmod(block * count, lanes)
        lines = []
        for which in range(4):
            row = 8 * group + 2 * which
            lines += split_digits(sums[row : row + 1, :] + sums[row + 1 : row + 2, :])
        packed = rows_as_lanes(lines, ref.shape[0] - columns * count)
        if lane:
            packed = pltpu.roll(packed, lanes - lane, 1)
        ref[columns * count :, :] = packed.astype(ref.dtype)


def add(held, arrived, size, count, columns, after):
    shape = (columns * count + sum_rows(count), lanes)
    outs = [shaped(shape, f32 if b == 0 else bf16) for b in range(size // count)]
    return call(
        functools.partial(add_kernel, len(arrived), size, count),
        outs,
        held, *arrived, *after,
        in_specs=[pl.BlockSpec(memory_space=pltpu.VMEM)] * (1 + len(arrived))
        + [pl.BlockSpec(memory_space=pl.ANY)] * len(after),
    )


def finish_kernel(arrived, *refs):
    held_ref, arrived_refs = refs[0], refs[1 : 1 + arrived]
    unit_ref, radius_ref, grad_ref, loss_ref = refs[1 + arrived :]
    count, width = unit_ref.shape
    parts = blocks_of(width)
    total = held_ref[...]
    for ref in arrived_refs:
        total = total + ref[...].astype(f32)
    sums = []
    for which in range(4):
        row = 2 * parts * count + 2 * which
        sums.append((total[row : row + 1, :] + total[row + 1 : row + 2, :])[:, :count])
    pos, neg = sums[:2]
    loss_ref[...] = jnp.log(1.0 + pos) / pos_scale + jnp.log(1.0 + neg) / neg_scale
    pos, neg, push_along, pull_along = [to_column(row) for row in sums]
    unit = unit_ref[...]
    anchors = unit.astype(bf16).astype(f32)
    push, pull = [
        jnp.concatenate([total[(first + at) * count : (first + at + 1) * count, :] for at in range(parts)], axis=1)
        for first in (0, parts)
    ]
    push = push + push_along * anchors
    pull = pull + pull_along * anchors
    grad_unit = push / (1.0 + neg) - pull / (1.0 + pos)
    along = jnp.sum(unit * grad_unit, axis=1, keepdims=True)
    grad_ref[...] = (grad_unit - unit * along) / radius_ref[:, :1]


def per_device(batch_rows, batch_labels, memory, memory_labels, keep_bits, step_index):
    groups = lax.axis_size("grp")
    members = lax.axis_size("dev")
    cores = 2 if members % 2 == 0 else 1
    line = members // cores
    count, width = batch_rows.shape
    slots = memory.shape[0]

    def exchange(value, axis, step):
        if axis == "grp":
            return lax.ppermute(value, "grp", [(i, i ^ step) for i in range(groups)])
        jump = step * cores if axis == "line" else step
        return lax.ppermute(value, "dev", [(i, i ^ jump) for i in range(members)])

    folded = (slots // lanes, lanes)
    parts = blocks_of(width)
    packed, unit, radius, slot_labels, copied_labels, step = call(
        prepare_kernel,
        [
            pltpu.VMEM((parts * count + 16, lanes), bf16),
            pltpu.VMEM((count, width), f32),
            pltpu.VMEM((count, lanes), f32),
            pltpu.VMEM(folded, jnp.int32),
            pltpu.VMEM(folded, jnp.int32),
            pltpu.VMEM((8, lanes), jnp.int32),
        ],
        batch_rows, batch_labels.reshape(1, count), memory_labels.reshape(folded), keep_bits.reshape(folded),
        step_index.reshape(1, 1),
        limit=vmem_most,
    )

    labels = [slot_labels] + [exchange(slot_labels, "core", s) for s in range(1, cores)]
    memories = [memory] + [exchange(memory, "core", s) for s in range(1, cores)]
    own_keys, copied = keys_of(memory, 1, pltpu.HBM)
    keys = [own_keys] + [keys_of(value, 0, pltpu.VMEM)[0] for value in memories[1:]]

    near = [packed] + [None] * (line - 1)
    for s in range(line - 1, 0, -1):
        near[s] = exchange(packed, "line", s)
    part = join(near, [own_keys, *labels])
    labels = [value.reshape(1, slots) for value in labels]
    blocks = [part] + [None] * (groups - 1)
    for s in range(groups - 1, 0, -1):
        blocks[s] = exchange(part if s == groups - 1 else later, "grp", s)
        if s == groups - 1:
            later = join([part], keys[1:])

    size = count * line
    arrived, after = [], []
    places = list(range(groups - 1, 0, -1))
    while places:
        now = places[:1] if not after else places[:2]
        places = places[len(now) :]
        after = block_sums([blocks[s] for s in now], keys, labels, count, bf16, after)
        arrived += [exchange(value, "grp", s) for s, value in zip(now, after)]
    held = block_sums([part], keys, labels, count, f32, after)[0]
    sizes = (count, slots, groups, line, cores)
    moved = pick(blocks, step, sizes, after)
    choices = [moved] + [exchange(moved, "core", s) for s in range(1, cores)]

    sums, *others = add(held, arrived, size, count, 2 * parts, choices)
    arrived = [exchange(others[s - 1], "line", s) for s in range(line - 1, 0, -1)]
    grad_batch, loss = call(
        functools.partial(finish_kernel, len(arrived)),
        [shaped((count, width), f32), shaped((1, count), f32)],
        sums, *arrived, unit, radius,
    )

    new_memory, new_labels = patch(copied, copied_labels, choices, step, sizes)
    return (grad_batch, loss.reshape(count), new_memory, new_labels.reshape(slots))


def solution(mesh):
    placed = (
        P(("grp", "dev"), None),
        P(("grp", "dev")),
        P(("grp", "dev"), None),
        P(("grp", "dev")),
        P(("grp", "dev")),
        P(),
    )
    return jax.shard_map(
        per_device,
        mesh=mesh,
        in_specs=placed,
        out_specs=(
            P(("grp", "dev"), None),
            P(("grp", "dev")),
            P(("grp", "dev"), None),
            P(("grp", "dev")),
        ),
        check_vma=False,
    )
```

```python
import functools
import math

import jax
import jax.numpy as jnp
from jax import lax
from jax.experimental import pallas as pl
from jax.experimental.pallas import tpu as pltpu
from jax.sharding import PartitionSpec as P

pos_scale = 2.0
neg_scale = 50.0
margin = 0.5
lanes = 128
log2e = math.log2(math.e)
vmem_bytes = 20 * 1024 * 1024
vmem_most = 56 * 1024 * 1024
f32 = jnp.float32
bf16 = jnp.bfloat16


def call(body, outs, *args, work=0, limit=vmem_bytes, **kw):
    return pl.pallas_call(
        body,
        out_shape=outs,
        compiler_params=pltpu.CompilerParams(vmem_limit_bytes=limit),
        cost_estimate=pl.CostEstimate(flops=work, bytes_accessed=0, transcendentals=0),
        **kw,
    )(*args)


def shaped(shape, dtype):
    return jax.ShapeDtypeStruct(shape, dtype)


def in_vmem(value):
    return pltpu.with_memory_space_constraint(value, pltpu.VMEM)


def rounded_up(value, unit):
    return (value + unit - 1) // unit * unit


def blocks_of(width):
    return width // lanes


def rows_as_lanes(parts, rows):
    row = lax.broadcasted_iota(jnp.int32, (rows, lanes), 0)
    out = jnp.zeros((rows, lanes), f32)
    for at, part in enumerate(parts):
        out = jnp.where(row == at, part, out)
    return out


def prepare_kernel(rows_ref, labels_ref, stored_ref, keep_ref, packed_ref, unit_ref, radius_ref, slot_ref, copy_ref):
    stored = stored_ref[...]
    slot_ref[...] = jnp.where(keep_ref[...] > 0, stored, -1)
    copy_ref[...] = stored
    rows = rows_ref[...].astype(f32)
    count, width = rows.shape
    radius = jnp.sqrt(jnp.sum(rows * rows, axis=1, keepdims=True) + 1e-06)
    unit = rows / radius
    unit_ref[...] = unit
    radius_ref[...] = jnp.broadcast_to(radius, radius_ref.shape)
    anchors = unit.astype(bf16)
    for at in range(blocks_of(width)):
        packed_ref[at * count : (at + 1) * count, :] = anchors[:, at * lanes : (at + 1) * lanes]
    row = jnp.concatenate([labels_ref[...].astype(f32), jnp.zeros((1, lanes - count), f32)], axis=1)
    high = jnp.floor(row * (1.0 / 256.0))
    tail = packed_ref.shape[0] - blocks_of(width) * count
    packed_ref[blocks_of(width) * count :, :] = rows_as_lanes([high, row - high * 256.0], tail).astype(bf16)


def diagonal(count):
    across = lax.broadcasted_iota(jnp.int32, (count, count), 1)
    down = lax.broadcasted_iota(jnp.int32, (count, count), 0)
    return across == down


def to_column(row):
    count = row.shape[1]
    spread = jnp.broadcast_to(row, (count, count))
    return jnp.sum(jnp.where(diagonal(count), spread, 0.0), axis=1, keepdims=True)


def to_row(column):
    count = column.shape[0]
    spread = jnp.broadcast_to(column, (count, count))
    return jnp.sum(jnp.where(diagonal(count), spread, 0.0), axis=0, keepdims=True)


def keys_kernel(memory_ref, keys_ref):
    rows = memory_ref[...].astype(f32)
    radius = jnp.sqrt(jnp.sum(rows * rows, axis=1, keepdims=True) + 1e-06)
    keys_ref[...] = (rows / radius).astype(bf16)


def keys_of(memory, place):
    slots, width = memory.shape
    block = math.gcd(512, slots)
    spec = pl.BlockSpec((block, width), lambda i: (i, 0))
    return call(
        keys_kernel,
        [shaped((slots, width), bf16)],
        pltpu.with_memory_space_constraint(memory, place),
        grid=(slots // block,),
        in_specs=[spec],
        out_specs=[spec],
    )[0]


def join_kernel(blocks, *refs):
    block_refs, out_ref = refs[:blocks], refs[-1]
    size = block_refs[0].shape[0]
    for place, ref in enumerate(block_refs):
        out_ref[place * size : (place + 1) * size, :] = ref[...]


def join(blocks, after):
    size, width = blocks[0].shape
    return call(
        functools.partial(join_kernel, len(blocks)),
        [shaped((size * len(blocks), width), blocks[0].dtype)],
        *blocks, *after,
        in_specs=[pl.BlockSpec(memory_space=pltpu.VMEM)] * len(blocks)
        + [pl.BlockSpec(memory_space=pl.ANY)] * len(after),
    )[0]


def other_keys_kernel(block, memory_ref, rows_ref, keys_ref, same_ref):
    same_ref[...] = rows_ref[...]

    @pl.loop(0, memory_ref.shape[0] // block)
    def _(i):
        part = pl.ds(pl.multiple_of(i * block, block), block)
        keys_ref[part, :] = normalized(memory_ref[part, :])


def other_keys(memory, rows):
    return call(
        functools.partial(other_keys_kernel, math.gcd(256, memory.shape[0])),
        [shaped(memory.shape, bf16), shaped(rows.shape, bf16)],
        memory, rows,
    )


def positions(step, count, slots, groups, line, cores):
    first = lax.rem(step, slots // count) * count
    crossing = lax.rem(step, cores)
    members = line * cores
    devices_all = groups * members
    grp = lax.axis_index("grp")
    dev = lax.axis_index("dev")
    target = grp * members + (dev ^ crossing)
    source = lax.rem(target + devices_all - lax.rem(step, devices_all), devices_all)
    source_grp = lax.div(source, members)
    source_line = lax.div(lax.rem(source, members), cores)
    return first, crossing, grp ^ source_grp, lax.div(dev, cores) ^ source_line


def pick_kernel(groups, sizes, step_ref, *refs):
    blocks_refs, out_ref = refs[:groups], refs[-1]
    rows = out_ref.shape[0]
    _, _, grp_place, line_place = positions(step_ref[0], *sizes)
    for place, ref in enumerate(blocks_refs):

        @pl.when(grp_place == place)
        def _():
            out_ref[...] = ref[pl.ds(pl.multiple_of(line_place * rows, 16), rows), :]


def pick(blocks, step, sizes, after):
    line = sizes[3]
    return call(
        functools.partial(pick_kernel, len(blocks), sizes),
        [shaped((blocks[0].shape[0] // line, lanes), bf16)],
        step, *blocks, *after,
        in_specs=[pl.BlockSpec(memory_space=pltpu.SMEM)]
        + [pl.BlockSpec(memory_space=pltpu.VMEM)] * len(blocks)
        + [pl.BlockSpec(memory_space=pl.ANY)] * len(after),
    )[0]


def patch_kernel(choices, sizes, step_ref, stored_ref, labels_ref, *refs):
    moved_refs, (memory_ref, new_labels_ref, rows_ref, sem) = refs[:choices], refs[choices:]
    count, width = rows_ref.shape
    first, crossing, _, _ = positions(step_ref[0], *sizes)
    moved = moved_refs[0][...]
    for choice in range(1, choices):
        moved = jnp.where(crossing == choice, moved_refs[choice][...], moved)
    for at in range(blocks_of(width)):
        rows_ref[:, at * lanes : (at + 1) * lanes] = moved[at * count : (at + 1) * count, :]
    target = memory_ref.at[pl.ds(pl.multiple_of(first, count), count), :]
    copy = pltpu.make_async_copy(rows_ref, target, sem)
    copy.start()
    digits = moved[blocks_of(width) * count :, :].astype(f32)
    row = (digits[0:1, :] * 256.0 + digits[1:2, :]).astype(jnp.int32)
    old = labels_ref[...]
    turned = pltpu.roll(jnp.broadcast_to(row, old.shape), lax.rem(first, lanes), 1)
    slot = lax.broadcasted_iota(jnp.int32, old.shape, 0) * lanes + lax.broadcasted_iota(jnp.int32, old.shape, 1)
    new_labels_ref[...] = jnp.where((slot >= first) & (slot < first + count), turned, old)
    copy.wait()


def patch(stored, labels, choices, step, sizes):
    count, width = sizes[0], stored.shape[1]
    return call(
        functools.partial(patch_kernel, len(choices), sizes),
        [shaped(stored.shape, bf16), shaped(labels.shape, jnp.int32)],
        step, stored, labels, *choices,
        in_specs=[pl.BlockSpec(memory_space=pltpu.SMEM), pl.BlockSpec(memory_space=pl.ANY)]
        + [pl.BlockSpec(memory_space=pltpu.VMEM)] * (1 + len(choices)),
        out_specs=[pl.BlockSpec(memory_space=pl.ANY), pl.BlockSpec(memory_space=pltpu.VMEM)],
        scratch_shapes=[pltpu.VMEM((count, width), bf16), pltpu.SemaphoreType.DMA],
        input_output_aliases={1: 0},
    )


def split_digits(row):
    high = row.astype(bf16).astype(f32)
    return [high, row - high]


def sum_rows(size):
    return rounded_up(8 * (rounded_up(size, lanes) // lanes), 16)


def block_kernel(blocks, sides, chunk, count, copies, *refs):
    if copies:
        source_ref, target_ref, sem = refs[blocks + 2 * sides], refs[-3], refs[-1]
        copy = pltpu.make_async_copy(source_ref, target_ref, sem)
        copy.start()
        refs = refs[:-3] + refs[-2:-1]
    rows_refs, keys_refs = refs[:blocks], refs[blocks : blocks + sides]
    label_refs = refs[blocks + sides : blocks + 2 * sides]
    out_refs = refs[-1 - blocks : -1]
    anchors_ref = refs[-1]
    slots, width = keys_refs[0].shape
    parts = blocks_of(width)
    packed = rows_refs[0].shape[0]
    members = packed // (parts * count + 16)
    size = members * count
    columns = []
    for block, ref in enumerate(rows_refs):
        for member in range(members):
            first = member * (parts * count + 16)
            to = block * size + member * count
            for at in range(parts):
                anchors_ref[to : to + count, at * lanes : (at + 1) * lanes] = ref[
                    first + at * count : first + (at + 1) * count, :
                ]
            digits = ref[first + parts * count : first + parts * count + 16, :].astype(f32)
            columns.append(to_column((digits[0:1, :] * 256.0 + digits[1:2, :])[:, :count]))
    labels = jnp.concatenate(columns, axis=0)
    anchors = anchors_ref[...]
    rows = blocks * size
    pos_sum = jnp.zeros((rows, 1), f32)
    neg_sum = jnp.zeros((rows, 1), f32)
    total = None
    chunks = [(side, slice(at, at + chunk)) for side in range(sides) for at in range(0, slots, chunk)]

    def scores_of(side, part):
        return lax.dot_general(
            anchors, keys_refs[side][part, :], (((1,), (1,)), ((), ())), preferred_element_type=f32
        )

    scores = scores_of(*chunks[0])
    for at, (side, part) in enumerate(chunks):
        following = scores_of(*chunks[at + 1]) if at + 1 < len(chunks) else None
        slot_labels = label_refs[side][:, part].astype(f32)
        neg_shift = jnp.where(slot_labels < 0.0, -1e30, -neg_scale * margin * log2e)
        same = labels == slot_labels
        slope = jnp.where(same, -pos_scale * log2e, neg_scale * log2e)
        shift = jnp.where(same, pos_scale * margin * log2e, neg_shift)
        term = jnp.exp2(scores * slope + shift)
        pos = jnp.where(same, term, 0.0)
        neg = jnp.where(same, 0.0, term)
        pos_sum += jnp.sum(pos, axis=1, keepdims=True)
        neg_sum += jnp.sum(neg, axis=1, keepdims=True)
        weights = jnp.concatenate([neg.astype(bf16), pos.astype(bf16)], axis=0)
        more = jnp.dot(weights, keys_refs[side][part, :], preferred_element_type=f32)
        total = more if total is None else total + more
        scores = following
    floats = anchors.astype(f32)
    sums = [pos_sum, neg_sum]
    for which in range(2):
        value = total[which * rows : (which + 1) * rows, :]
        along = jnp.sum(value * floats, axis=1, keepdims=True)
        sums.append(along)
        rest = value - along * floats
        for block, ref in enumerate(out_refs):
            for at in range(parts):
                first = (which * parts + at) * size
                ref[first : first + size, :] = rest[
                    block * size : (block + 1) * size, at * lanes : (at + 1) * lanes
                ].astype(ref.dtype)
    for block, ref in enumerate(out_refs):
        lines = []
        for first in range(0, size, lanes):
            last = min(first + lanes, size)
            for value in sums:
                row = to_row(value[block * size + first : block * size + last])
                if last - first < lanes:
                    row = jnp.concatenate([row, jnp.zeros((1, lanes - last + first), f32)], axis=1)
                lines += split_digits(row)
        first = 2 * parts * size
        ref[first:, :] = rows_as_lanes(lines, ref.shape[0] - first).astype(ref.dtype)
    if copies:
        copy.wait()


def block_sums(blocks, keys, labels, count, dtype, after, copied=()):
    slots, width = keys[0].shape
    parts = blocks_of(width)
    size = blocks[0].shape[0] // (parts * count + 16) * count
    anywhere = pl.BlockSpec(memory_space=pl.ANY)
    vmem = pl.BlockSpec(memory_space=pltpu.VMEM)
    return call(
        functools.partial(block_kernel, len(blocks), len(keys), math.gcd(1024, slots), count, len(copied)),
        [shaped((2 * parts * size + sum_rows(size), lanes), dtype)] * len(blocks)
        + [shaped(value.shape, value.dtype) for value in copied],
        *blocks, *[in_vmem(k) for k in keys], *labels, *copied, *after,
        work=12 * size * len(blocks) * slots * len(keys) * width,
        in_specs=[vmem] * (len(blocks) + 2 * len(keys)) + [anywhere] * (len(copied) + len(after)),
        out_specs=[vmem] * len(blocks) + [anywhere] * len(copied),
        scratch_shapes=[pltpu.VMEM((len(blocks) * size, width), bf16)]
        + [pltpu.SemaphoreType.DMA] * len(copied),
    )


def add_kernel(arrived, size, count, *refs):
    in_refs, out_refs = refs[: 1 + arrived], refs[-(size // count) :]
    columns = (in_refs[0].shape[0] - sum_rows(size)) // size

    def total(first, rows):
        value = in_refs[0][first : first + rows, :]
        for ref in in_refs[1:]:
            value = value + ref[first : first + rows, :].astype(f32)
        return value

    sums = total(columns * size, sum_rows(size))
    for block, ref in enumerate(out_refs):
        for at in range(columns):
            part = total(at * size + block * count, count)
            ref[at * count : (at + 1) * count, :] = part.astype(ref.dtype)
        group, lane = divmod(block * count, lanes)
        lines = []
        for which in range(4):
            row = 8 * group + 2 * which
            lines += split_digits(sums[row : row + 1, :] + sums[row + 1 : row + 2, :])
        packed = rows_as_lanes(lines, ref.shape[0] - columns * count)
        if lane:
            packed = pltpu.roll(packed, lanes - lane, 1)
        ref[columns * count :, :] = packed.astype(ref.dtype)


def add(held, arrived, size, count, columns, after):
    shape = (columns * count + sum_rows(count), lanes)
    outs = [shaped(shape, f32 if b == 0 else bf16) for b in range(size // count)]
    return call(
        functools.partial(add_kernel, len(arrived), size, count),
        outs,
        held, *arrived, *after,
        in_specs=[pl.BlockSpec(memory_space=pltpu.VMEM)] * (1 + len(arrived))
        + [pl.BlockSpec(memory_space=pl.ANY)] * len(after),
    )


def finish_kernel(arrived, *refs):
    held_ref, arrived_refs = refs[0], refs[1 : 1 + arrived]
    unit_ref, radius_ref, grad_ref, loss_ref = refs[1 + arrived :]
    count, width = unit_ref.shape
    parts = blocks_of(width)
    total = held_ref[...]
    for ref in arrived_refs:
        total = total + ref[...].astype(f32)
    sums = []
    for which in range(4):
        row = 2 * parts * count + 2 * which
        sums.append((total[row : row + 1, :] + total[row + 1 : row + 2, :])[:, :count])
    pos, neg = sums[:2]
    loss_ref[...] = jnp.log(1.0 + pos) / pos_scale + jnp.log(1.0 + neg) / neg_scale
    pos, neg, push_along, pull_along = [to_column(row) for row in sums]
    unit = unit_ref[...]
    anchors = unit.astype(bf16).astype(f32)
    push, pull = [
        jnp.concatenate([total[(first + at) * count : (first + at + 1) * count, :] for at in range(parts)], axis=1)
        for first in (0, parts)
    ]
    push = push + push_along * anchors
    pull = pull + pull_along * anchors
    grad_unit = push / (1.0 + neg) - pull / (1.0 + pos)
    along = jnp.sum(unit * grad_unit, axis=1, keepdims=True)
    grad_ref[...] = (grad_unit - unit * along) / radius_ref[:, :1]


def per_device(batch_rows, batch_labels, memory, memory_labels, keep_bits, step_index):
    groups = lax.axis_size("grp")
    members = lax.axis_size("dev")
    cores = 2 if members % 2 == 0 else 1
    line = members // cores
    count, width = batch_rows.shape
    slots = memory.shape[0]

    def exchange(value, axis, step):
        if axis == "grp":
            return lax.ppermute(value, "grp", [(i, i ^ step) for i in range(groups)])
        jump = step * cores if axis == "line" else step
        return lax.ppermute(value, "dev", [(i, i ^ jump) for i in range(members)])

    folded = (slots // lanes, lanes)
    parts = blocks_of(width)
    packed, unit, radius, slot_labels, copied_labels = call(
        prepare_kernel,
        [
            pltpu.VMEM((parts * count + 16, lanes), bf16),
            pltpu.VMEM((count, width), f32),
            pltpu.VMEM((count, lanes), f32),
            pltpu.VMEM(folded, jnp.int32),
            pltpu.VMEM(folded, jnp.int32),
        ],
        batch_rows, batch_labels.reshape(1, count), memory_labels.reshape(folded), keep_bits.reshape(folded),
        limit=vmem_most,
    )

    labels = [slot_labels] + [exchange(slot_labels, "core", s) for s in range(1, cores)]
    memories = [memory] + [exchange(memory, "core", s) for s in range(1, cores)]
    keys = [keys_of(memory, pltpu.HBM)] + [keys_of(value, pltpu.VMEM) for value in memories[1:]]

    near = [packed] + [None] * (line - 1)
    for s in range(line - 1, 0, -1):
        near[s] = exchange(packed, "line", s)
    part = join(near, [keys[0], *labels])
    labels = [value.reshape(1, slots) for value in labels]
    blocks = [part] + [None] * (groups - 1)
    for s in range(groups - 1, 0, -1):
        blocks[s] = exchange(part if s == groups - 1 else later, "grp", s)
        if s == groups - 1:
            later = join([part], keys[1:])

    size = count * line
    arrived, after = [], []
    places = list(range(groups - 1, 0, -1))
    while places:
        now = places[:1] if not after else places[:2]
        places = places[len(now) :]
        after = block_sums([blocks[s] for s in now], keys, labels, count, bf16, after)
        arrived += [exchange(value, "grp", s) for s, value in zip(now, after)]
    held, copied = block_sums([part], keys, labels, count, f32, after, [memory])
    sizes = (count, slots, groups, line, cores)
    moved = pick(blocks, step_index, sizes, after)
    choices = [moved] + [exchange(moved, "core", s) for s in range(1, cores)]

    sums, *others = add(held, arrived, size, count, 2 * parts, choices)
    arrived = [exchange(others[s - 1], "line", s) for s in range(line - 1, 0, -1)]
    grad_batch, loss = call(
        functools.partial(finish_kernel, len(arrived)),
        [shaped((count, width), f32), shaped((1, count), f32)],
        sums, *arrived, unit, radius,
    )

    new_memory, new_labels = patch(copied, copied_labels, choices, step_index, sizes)
    return (grad_batch, loss.reshape(count), new_memory, new_labels.reshape(slots))


def solution(mesh):
    placed = (
        P(("grp", "dev"), None),
        P(("grp", "dev")),
        P(("grp", "dev"), None),
        P(("grp", "dev")),
        P(("grp", "dev")),
        P(),
    )
    return jax.shard_map(
        per_device,
        mesh=mesh,
        in_specs=placed,
        out_specs=(
            P(("grp", "dev"), None),
            P(("grp", "dev")),
            P(("grp", "dev"), None),
            P(("grp", "dev")),
        ),
        check_vma=False,
    )
```

```python
import functools
import math

import jax
import jax.numpy as jnp
from jax import lax
from jax.experimental import pallas as pl
from jax.experimental.pallas import tpu as pltpu
from jax.sharding import PartitionSpec as P

pos_scale = 2.0
neg_scale = 50.0
margin = 0.5
lanes = 128
log2e = math.log2(math.e)
vmem_bytes = 20 * 1024 * 1024
vmem_most = 56 * 1024 * 1024
f32 = jnp.float32
bf16 = jnp.bfloat16


def call(body, outs, *args, work=0, limit=vmem_bytes, **kw):
    return pl.pallas_call(
        body,
        out_shape=outs,
        compiler_params=pltpu.CompilerParams(vmem_limit_bytes=limit),
        cost_estimate=pl.CostEstimate(flops=work, bytes_accessed=0, transcendentals=0),
        **kw,
    )(*args)


def shaped(shape, dtype):
    return jax.ShapeDtypeStruct(shape, dtype)


def in_vmem(value):
    return pltpu.with_memory_space_constraint(value, pltpu.VMEM)


def rounded_up(value, unit):
    return (value + unit - 1) // unit * unit


def blocks_of(width):
    return width // lanes


def rows_as_lanes(parts, rows):
    row = lax.broadcasted_iota(jnp.int32, (rows, lanes), 0)
    out = jnp.zeros((rows, lanes), f32)
    for at, part in enumerate(parts):
        out = jnp.where(row == at, part, out)
    return out


def prepare_kernel(rows_ref, labels_ref, stored_ref, keep_ref, packed_ref, unit_ref, radius_ref, slot_ref, copy_ref):
    stored = stored_ref[...]
    slot_ref[...] = jnp.where(keep_ref[...] > 0, stored, -1)
    copy_ref[...] = stored
    rows = rows_ref[...].astype(f32)
    count, width = rows.shape
    radius = jnp.sqrt(jnp.sum(rows * rows, axis=1, keepdims=True) + 1e-06)
    unit = rows / radius
    unit_ref[...] = unit
    radius_ref[...] = jnp.broadcast_to(radius, radius_ref.shape)
    anchors = unit.astype(bf16)
    row = jnp.concatenate([labels_ref[...].astype(f32), jnp.zeros((1, lanes - count), f32)], axis=1)
    high = jnp.floor(row * (1.0 / 256.0))
    digits = rows_as_lanes([high, row - high * 256.0], 16).astype(bf16)
    size = blocks_of(width) * count
    for first in range(0, packed_ref.shape[0], size + 16):
        for at in range(blocks_of(width)):
            part = slice(first + at * count, first + (at + 1) * count)
            packed_ref[part, :] = anchors[:, at * lanes : (at + 1) * lanes]
        packed_ref[first + size : first + size + 16, :] = digits


def diagonal(count):
    across = lax.broadcasted_iota(jnp.int32, (count, count), 1)
    down = lax.broadcasted_iota(jnp.int32, (count, count), 0)
    return across == down


def to_column(row):
    count = row.shape[1]
    spread = jnp.broadcast_to(row, (count, count))
    return jnp.sum(jnp.where(diagonal(count), spread, 0.0), axis=1, keepdims=True)


def to_row(column):
    count = column.shape[0]
    spread = jnp.broadcast_to(column, (count, count))
    return jnp.sum(jnp.where(diagonal(count), spread, 0.0), axis=0, keepdims=True)


def keys_kernel(memory_ref, keys_ref):
    rows = memory_ref[...].astype(f32)
    radius = jnp.sqrt(jnp.sum(rows * rows, axis=1, keepdims=True) + 1e-06)
    keys_ref[...] = (rows / radius).astype(bf16)


def keys_of(memory, place):
    slots, width = memory.shape
    block = math.gcd(512, slots)
    spec = pl.BlockSpec((block, width), lambda i: (i, 0))
    return call(
        keys_kernel,
        [shaped((slots, width), bf16)],
        pltpu.with_memory_space_constraint(memory, place),
        grid=(slots // block,),
        in_specs=[spec],
        out_specs=[spec],
    )[0]


def join_kernel(blocks, *refs):
    block_refs, out_ref = refs[:blocks], refs[-1]
    size = block_refs[0].shape[0]
    for place, ref in enumerate(block_refs):
        out_ref[place * size : (place + 1) * size, :] = ref[...]


def join(blocks, after):
    size, width = blocks[0].shape
    return call(
        functools.partial(join_kernel, len(blocks)),
        [shaped((size * len(blocks), width), blocks[0].dtype)],
        *blocks, *after,
        in_specs=[pl.BlockSpec(memory_space=pltpu.VMEM)] * len(blocks)
        + [pl.BlockSpec(memory_space=pl.ANY)] * len(after),
    )[0]


def other_keys_kernel(block, memory_ref, rows_ref, keys_ref, same_ref):
    same_ref[...] = rows_ref[...]

    @pl.loop(0, memory_ref.shape[0] // block)
    def _(i):
        part = pl.ds(pl.multiple_of(i * block, block), block)
        keys_ref[part, :] = normalized(memory_ref[part, :])


def other_keys(memory, rows):
    return call(
        functools.partial(other_keys_kernel, math.gcd(256, memory.shape[0])),
        [shaped(memory.shape, bf16), shaped(rows.shape, bf16)],
        memory, rows,
    )


def positions(step, count, slots, groups, line, cores):
    first = lax.rem(step, slots // count) * count
    crossing = lax.rem(step, cores)
    members = line * cores
    devices_all = groups * members
    grp = lax.axis_index("grp")
    dev = lax.axis_index("dev")
    target = grp * members + (dev ^ crossing)
    source = lax.rem(target + devices_all - lax.rem(step, devices_all), devices_all)
    source_grp = lax.div(source, members)
    source_line = lax.div(lax.rem(source, members), cores)
    return first, crossing, grp ^ source_grp, source_line


def pick_kernel(groups, sizes, step_ref, *refs):
    blocks_refs, out_ref = refs[:groups], refs[-1]
    rows = out_ref.shape[0]
    _, _, grp_place, line_place = positions(step_ref[0], *sizes)
    for place, ref in enumerate(blocks_refs):

        @pl.when(grp_place == place)
        def _():
            out_ref[...] = ref[pl.ds(pl.multiple_of(line_place * rows, 16), rows), :]


def pick(blocks, step, sizes, after):
    line = sizes[3]
    return call(
        functools.partial(pick_kernel, len(blocks), sizes),
        [shaped((blocks[0].shape[0] // line, lanes), bf16)],
        step, *blocks, *after,
        in_specs=[pl.BlockSpec(memory_space=pltpu.SMEM)]
        + [pl.BlockSpec(memory_space=pltpu.VMEM)] * len(blocks)
        + [pl.BlockSpec(memory_space=pl.ANY)] * len(after),
    )[0]


def patch_kernel(choices, sizes, step_ref, stored_ref, labels_ref, *refs):
    moved_refs, (memory_ref, new_labels_ref, rows_ref, sem) = refs[:choices], refs[choices:]
    count, width = rows_ref.shape
    first, crossing, _, _ = positions(step_ref[0], *sizes)
    moved = moved_refs[0][...]
    for choice in range(1, choices):
        moved = jnp.where(crossing == choice, moved_refs[choice][...], moved)
    for at in range(blocks_of(width)):
        rows_ref[:, at * lanes : (at + 1) * lanes] = moved[at * count : (at + 1) * count, :]
    target = memory_ref.at[pl.ds(pl.multiple_of(first, count), count), :]
    copy = pltpu.make_async_copy(rows_ref, target, sem)
    copy.start()
    digits = moved[blocks_of(width) * count :, :].astype(f32)
    row = (digits[0:1, :] * 256.0 + digits[1:2, :]).astype(jnp.int32)
    old = labels_ref[...]
    turned = pltpu.roll(jnp.broadcast_to(row, old.shape), lax.rem(first, lanes), 1)
    slot = lax.broadcasted_iota(jnp.int32, old.shape, 0) * lanes + lax.broadcasted_iota(jnp.int32, old.shape, 1)
    new_labels_ref[...] = jnp.where((slot >= first) & (slot < first + count), turned, old)
    copy.wait()


def patch(stored, labels, choices, step, sizes):
    count, width = sizes[0], stored.shape[1]
    return call(
        functools.partial(patch_kernel, len(choices), sizes),
        [shaped(stored.shape, bf16), shaped(labels.shape, jnp.int32)],
        step, stored, labels, *choices,
        in_specs=[pl.BlockSpec(memory_space=pltpu.SMEM), pl.BlockSpec(memory_space=pl.ANY)]
        + [pl.BlockSpec(memory_space=pltpu.VMEM)] * (1 + len(choices)),
        out_specs=[pl.BlockSpec(memory_space=pl.ANY), pl.BlockSpec(memory_space=pltpu.VMEM)],
        scratch_shapes=[pltpu.VMEM((count, width), bf16), pltpu.SemaphoreType.DMA],
        input_output_aliases={1: 0},
    )


def split_digits(row):
    high = row.astype(bf16).astype(f32)
    return [high, row - high]


def sum_rows(size):
    return rounded_up(8 * (rounded_up(size, lanes) // lanes), 16)


def block_kernel(blocks, sides, chunk, count, copies, *refs):
    if copies:
        source_ref, target_ref, sem = refs[blocks + 2 * sides], refs[-3], refs[-1]
        copy = pltpu.make_async_copy(source_ref, target_ref, sem)
        copy.start()
        refs = refs[:-3] + refs[-2:-1]
    rows_refs, keys_refs = refs[:blocks], refs[blocks : blocks + sides]
    label_refs = refs[blocks + sides : blocks + 2 * sides]
    out_refs = refs[-1 - blocks : -1]
    anchors_ref = refs[-1]
    slots, width = keys_refs[0].shape
    parts = blocks_of(width)
    packed = rows_refs[0].shape[0]
    members = packed // (parts * count + 16)
    size = members * count
    columns = []
    for block, ref in enumerate(rows_refs):
        for member in range(members):
            first = member * (parts * count + 16)
            to = block * size + member * count
            for at in range(parts):
                anchors_ref[to : to + count, at * lanes : (at + 1) * lanes] = ref[
                    first + at * count : first + (at + 1) * count, :
                ]
            digits = ref[first + parts * count : first + parts * count + 16, :].astype(f32)
            columns.append(to_column((digits[0:1, :] * 256.0 + digits[1:2, :])[:, :count]))
    labels = jnp.concatenate(columns, axis=0)
    anchors = anchors_ref[...]
    rows = blocks * size
    pos_sum = jnp.zeros((rows, 1), f32)
    neg_sum = jnp.zeros((rows, 1), f32)
    total = None
    chunks = [(side, slice(at, at + chunk)) for side in range(sides) for at in range(0, slots, chunk)]

    def scores_of(side, part):
        return lax.dot_general(
            anchors, keys_refs[side][part, :], (((1,), (1,)), ((), ())), preferred_element_type=f32
        )

    scores = scores_of(*chunks[0])
    for at, (side, part) in enumerate(chunks):
        following = scores_of(*chunks[at + 1]) if at + 1 < len(chunks) else None
        slot_labels = label_refs[side][:, part].astype(f32)
        neg_shift = jnp.where(slot_labels < 0.0, -1e30, -neg_scale * margin * log2e)
        same = labels == slot_labels
        slope = jnp.where(same, -pos_scale * log2e, neg_scale * log2e)
        shift = jnp.where(same, pos_scale * margin * log2e, neg_shift)
        term = jnp.exp2(scores * slope + shift)
        pos = jnp.where(same, term, 0.0)
        neg = jnp.where(same, 0.0, term)
        pos_sum += jnp.sum(pos, axis=1, keepdims=True)
        neg_sum += jnp.sum(neg, axis=1, keepdims=True)
        weights = jnp.concatenate([neg.astype(bf16), pos.astype(bf16)], axis=0)
        more = jnp.dot(weights, keys_refs[side][part, :], preferred_element_type=f32)
        total = more if total is None else total + more
        scores = following
    floats = anchors.astype(f32)
    sums = [pos_sum, neg_sum]
    for which in range(2):
        value = total[which * rows : (which + 1) * rows, :]
        along = jnp.sum(value * floats, axis=1, keepdims=True)
        sums.append(along)
        rest = value - along * floats
        for block, ref in enumerate(out_refs):
            for at in range(parts):
                first = (which * parts + at) * size
                ref[first : first + size, :] = rest[
                    block * size : (block + 1) * size, at * lanes : (at + 1) * lanes
                ].astype(ref.dtype)
    for block, ref in enumerate(out_refs):
        lines = []
        for first in range(0, size, lanes):
            last = min(first + lanes, size)
            for value in sums:
                row = to_row(value[block * size + first : block * size + last])
                if last - first < lanes:
                    row = jnp.concatenate([row, jnp.zeros((1, lanes - last + first), f32)], axis=1)
                lines += split_digits(row)
        first = 2 * parts * size
        ref[first:, :] = rows_as_lanes(lines, ref.shape[0] - first).astype(ref.dtype)
    if copies:
        copy.wait()


def block_sums(blocks, keys, labels, count, dtype, after, copied=()):
    slots, width = keys[0].shape
    parts = blocks_of(width)
    size = blocks[0].shape[0] // (parts * count + 16) * count
    anywhere = pl.BlockSpec(memory_space=pl.ANY)
    vmem = pl.BlockSpec(memory_space=pltpu.VMEM)
    return call(
        functools.partial(block_kernel, len(blocks), len(keys), math.gcd(1024, slots), count, len(copied)),
        [shaped((2 * parts * size + sum_rows(size), lanes), dtype)] * len(blocks)
        + [shaped(value.shape, value.dtype) for value in copied],
        *blocks, *[in_vmem(k) for k in keys], *labels, *copied, *after,
        work=12 * size * len(blocks) * slots * len(keys) * width,
        in_specs=[vmem] * (len(blocks) + 2 * len(keys)) + [anywhere] * (len(copied) + len(after)),
        out_specs=[vmem] * len(blocks) + [anywhere] * len(copied),
        scratch_shapes=[pltpu.VMEM((len(blocks) * size, width), bf16)]
        + [pltpu.SemaphoreType.DMA] * len(copied),
    )


def add_kernel(arrived, size, count, *refs):
    in_refs, out_ref = refs[: 1 + arrived], refs[-1]
    columns = (in_refs[0].shape[0] - sum_rows(size)) // size

    def total(first, rows):
        value = in_refs[0][first : first + rows, :]
        for ref in in_refs[1:]:
            value = value + ref[first : first + rows, :].astype(f32)
        return value

    sums = total(columns * size, sum_rows(size))
    tail = sum_rows(count)
    for block in range(size // count):
        base = block * (columns * count + tail)
        for at in range(columns):
            part = total(at * size + block * count, count)
            out_ref[base + at * count : base + (at + 1) * count, :] = part.astype(bf16)
        group, lane = divmod(block * count, lanes)
        lines = []
        for which in range(4):
            row = 8 * group + 2 * which
            lines += split_digits(sums[row : row + 1, :] + sums[row + 1 : row + 2, :])
        packed = rows_as_lanes(lines, tail)
        if lane:
            packed = pltpu.roll(packed, lanes - lane, 1)
        base += columns * count
        out_ref[base : base + tail, :] = packed.astype(bf16)


def add(held, arrived, size, count, columns, after):
    blocks = size // count
    return call(
        functools.partial(add_kernel, len(arrived), size, count),
        [shaped((blocks * (columns * count + sum_rows(count)), lanes), bf16)],
        held, *arrived, *after,
        in_specs=[pl.BlockSpec(memory_space=pltpu.VMEM)] * (1 + len(arrived))
        + [pl.BlockSpec(memory_space=pl.ANY)] * len(after),
    )[0]


def finish_kernel(sums_ref, unit_ref, radius_ref, grad_ref, loss_ref):
    count, width = unit_ref.shape
    parts = blocks_of(width)
    rows = 2 * parts * count + sum_rows(count)
    total = sums_ref[:rows, :].astype(f32)
    for first in range(rows, sums_ref.shape[0], rows):
        total = total + sums_ref[first : first + rows, :].astype(f32)
    sums = []
    for which in range(4):
        row = 2 * parts * count + 2 * which
        sums.append((total[row : row + 1, :] + total[row + 1 : row + 2, :])[:, :count])
    pos, neg = sums[:2]
    loss_ref[...] = jnp.log(1.0 + pos) / pos_scale + jnp.log(1.0 + neg) / neg_scale
    pos, neg, push_along, pull_along = [to_column(row) for row in sums]
    unit = unit_ref[...]
    anchors = unit.astype(bf16).astype(f32)
    push, pull = [
        jnp.concatenate([total[(first + at) * count : (first + at + 1) * count, :] for at in range(parts)], axis=1)
        for first in (0, parts)
    ]
    push = push + push_along * anchors
    pull = pull + pull_along * anchors
    grad_unit = push / (1.0 + neg) - pull / (1.0 + pos)
    along = jnp.sum(unit * grad_unit, axis=1, keepdims=True)
    grad_ref[...] = (grad_unit - unit * along) / radius_ref[:, :1]


def per_device(batch_rows, batch_labels, memory, memory_labels, keep_bits, step_index):
    groups = lax.axis_size("grp")
    members = lax.axis_size("dev")
    cores = 2 if members % 2 == 0 else 1
    line = members // cores
    count, width = batch_rows.shape
    slots = memory.shape[0]

    def along_line(value):
        members_of = [[at * cores + core for at in range(line)] for core in range(cores)]
        return lax.all_to_all(value, "dev", 0, 0, axis_index_groups=members_of, tiled=True)

    def exchange(value, axis, step):
        if axis == "grp":
            return lax.ppermute(value, "grp", [(i, i ^ step) for i in range(groups)])
        return lax.ppermute(value, "dev", [(i, i ^ step) for i in range(members)])

    folded = (slots // lanes, lanes)
    parts = blocks_of(width)
    packed, unit, radius, slot_labels, copied_labels = call(
        prepare_kernel,
        [
            pltpu.VMEM((line * (parts * count + 16), lanes), bf16),
            pltpu.VMEM((count, width), f32),
            pltpu.VMEM((count, lanes), f32),
            pltpu.VMEM(folded, jnp.int32),
            pltpu.VMEM(folded, jnp.int32),
        ],
        batch_rows, batch_labels.reshape(1, count), memory_labels.reshape(folded), keep_bits.reshape(folded),
        limit=vmem_most,
    )

    labels = [slot_labels] + [exchange(slot_labels, "core", s) for s in range(1, cores)]
    memories = [memory] + [exchange(memory, "core", s) for s in range(1, cores)]
    keys = [keys_of(memory, pltpu.HBM)] + [keys_of(value, pltpu.VMEM) for value in memories[1:]]

    part = join([along_line(packed)], labels)
    labels = [value.reshape(1, slots) for value in labels]
    blocks = [part] + [None] * (groups - 1)
    for s in range(groups - 1, 0, -1):
        blocks[s] = exchange(part if s == groups - 1 else later, "grp", s)
        if s == groups - 1:
            later = join([part], keys)

    size = count * line
    arrived, after = [], []
    places = list(range(groups - 1, 0, -1))
    while places:
        now = places[:1] if not after else places[:2]
        places = places[len(now) :]
        after = block_sums([blocks[s] for s in now], keys, labels, count, bf16, after)
        arrived += [exchange(value, "grp", s) for s, value in zip(now, after)]
    held, copied = block_sums([part], keys, labels, count, f32, after, [memory])
    sizes = (count, slots, groups, line, cores)
    moved = pick(blocks, step_index, sizes, after)
    choices = [moved] + [exchange(moved, "core", s) for s in range(1, cores)]

    sums = along_line(add(held, arrived, size, count, 2 * parts, choices))
    grad_batch, loss = call(
        finish_kernel,
        [shaped((count, width), f32), shaped((1, count), f32)],
        sums, unit, radius,
    )

    new_memory, new_labels = patch(copied, copied_labels, choices, step_index, sizes)
    return (grad_batch, loss.reshape(count), new_memory, new_labels.reshape(slots))


def solution(mesh):
    placed = (
        P(("grp", "dev"), None),
        P(("grp", "dev")),
        P(("grp", "dev"), None),
        P(("grp", "dev")),
        P(("grp", "dev")),
        P(),
    )
    return jax.shard_map(
        per_device,
        mesh=mesh,
        in_specs=placed,
        out_specs=(
            P(("grp", "dev"), None),
            P(("grp", "dev")),
            P(("grp", "dev"), None),
            P(("grp", "dev")),
        ),
        check_vma=False,
    )
```

```python
import functools
import math

import jax
import jax.numpy as jnp
from jax import lax
from jax.experimental import pallas as pl
from jax.experimental.pallas import tpu as pltpu
from jax.sharding import PartitionSpec as P

pos_scale = 2.0
neg_scale = 50.0
margin = 0.5
lanes = 128
log2e = math.log2(math.e)
vmem_bytes = 20 * 1024 * 1024
vmem_most = 56 * 1024 * 1024
f32 = jnp.float32
bf16 = jnp.bfloat16


def call(body, outs, *args, work=0, limit=vmem_bytes, **kw):
    return pl.pallas_call(
        body,
        out_shape=outs,
        compiler_params=pltpu.CompilerParams(vmem_limit_bytes=limit),
        cost_estimate=pl.CostEstimate(flops=work, bytes_accessed=0, transcendentals=0),
        **kw,
    )(*args)


def shaped(shape, dtype):
    return jax.ShapeDtypeStruct(shape, dtype)


def in_vmem(value):
    return pltpu.with_memory_space_constraint(value, pltpu.VMEM)


def rounded_up(value, unit):
    return (value + unit - 1) // unit * unit


def blocks_of(width):
    return width // lanes


def rows_as_lanes(parts, rows):
    row = lax.broadcasted_iota(jnp.int32, (rows, lanes), 0)
    out = jnp.zeros((rows, lanes), f32)
    for at, part in enumerate(parts):
        out = jnp.where(row == at, part, out)
    return out


def prepare_kernel(rows_ref, labels_ref, stored_ref, keep_ref, packed_ref, unit_ref, radius_ref, slot_ref, copy_ref):
    stored = stored_ref[...]
    slot_ref[...] = jnp.where(keep_ref[...] > 0, stored, -1)
    copy_ref[...] = stored
    rows = rows_ref[...].astype(f32)
    count, width = rows.shape
    radius = jnp.sqrt(jnp.sum(rows * rows, axis=1, keepdims=True) + 1e-06)
    unit = rows / radius
    unit_ref[...] = unit
    radius_ref[...] = jnp.broadcast_to(radius, radius_ref.shape)
    anchors = unit.astype(bf16)
    for at in range(blocks_of(width)):
        packed_ref[at * count : (at + 1) * count, :] = anchors[:, at * lanes : (at + 1) * lanes]
    row = jnp.concatenate([labels_ref[...].astype(f32), jnp.zeros((1, lanes - count), f32)], axis=1)
    high = jnp.floor(row * (1.0 / 256.0))
    tail = packed_ref.shape[0] - blocks_of(width) * count
    packed_ref[blocks_of(width) * count :, :] = rows_as_lanes([high, row - high * 256.0], tail).astype(bf16)


def diagonal(count):
    across = lax.broadcasted_iota(jnp.int32, (count, count), 1)
    down = lax.broadcasted_iota(jnp.int32, (count, count), 0)
    return across == down


def to_column(row):
    count = row.shape[1]
    spread = jnp.broadcast_to(row, (count, count))
    return jnp.sum(jnp.where(diagonal(count), spread, 0.0), axis=1, keepdims=True)


def to_row(column):
    count = column.shape[0]
    spread = jnp.broadcast_to(column, (count, count))
    return jnp.sum(jnp.where(diagonal(count), spread, 0.0), axis=0, keepdims=True)


def keys_kernel(memory_ref, *refs):
    keys_ref = refs[-1]
    rows = memory_ref[...].astype(f32)
    radius = jnp.sqrt(jnp.sum(rows * rows, axis=1, keepdims=True) + 1e-06)
    keys_ref[...] = (rows / radius).astype(bf16)


def keys_of(memory, place, after):
    slots, width = memory.shape
    block = math.gcd(512, slots)
    spec = pl.BlockSpec((block, width), lambda i: (i, 0))
    return call(
        keys_kernel,
        [shaped((slots, width), bf16)],
        pltpu.with_memory_space_constraint(memory, place), *after,
        work=64 * slots * width * width,
        grid=(slots // block,),
        in_specs=[spec] + [pl.BlockSpec(memory_space=pl.ANY)] * len(after),
        out_specs=[spec],
    )[0]


def join_kernel(blocks, *refs):
    block_refs, out_ref = refs[:blocks], refs[-1]
    size = block_refs[0].shape[0]
    for place, ref in enumerate(block_refs):
        out_ref[place * size : (place + 1) * size, :] = ref[...]


def join(blocks, after):
    size, width = blocks[0].shape
    return call(
        functools.partial(join_kernel, len(blocks)),
        [shaped((size * len(blocks), width), blocks[0].dtype)],
        *blocks, *after,
        in_specs=[pl.BlockSpec(memory_space=pltpu.VMEM)] * len(blocks)
        + [pl.BlockSpec(memory_space=pl.ANY)] * len(after),
    )[0]


def other_keys_kernel(block, memory_ref, rows_ref, keys_ref, same_ref):
    same_ref[...] = rows_ref[...]

    @pl.loop(0, memory_ref.shape[0] // block)
    def _(i):
        part = pl.ds(pl.multiple_of(i * block, block), block)
        keys_ref[part, :] = normalized(memory_ref[part, :])


def other_keys(memory, rows):
    return call(
        functools.partial(other_keys_kernel, math.gcd(256, memory.shape[0])),
        [shaped(memory.shape, bf16), shaped(rows.shape, bf16)],
        memory, rows,
    )


def positions(step, count, slots, groups, line, cores):
    first = lax.rem(step, slots // count) * count
    crossing = lax.rem(step, cores)
    members = line * cores
    devices_all = groups * members
    grp = lax.axis_index("grp")
    dev = lax.axis_index("dev")
    target = grp * members + (dev ^ crossing)
    source = lax.rem(target + devices_all - lax.rem(step, devices_all), devices_all)
    source_grp = lax.div(source, members)
    source_line = lax.div(lax.rem(source, members), cores)
    return first, crossing, grp ^ source_grp, lax.div(dev, cores) ^ source_line


def pick_kernel(groups, sizes, step_ref, *refs):
    blocks_refs, out_ref = refs[:groups], refs[-1]
    rows = out_ref.shape[0]
    _, _, grp_place, line_place = positions(step_ref[0], *sizes)
    for place, ref in enumerate(blocks_refs):

        @pl.when(grp_place == place)
        def _():
            out_ref[...] = ref[pl.ds(pl.multiple_of(line_place * rows, 16), rows), :]


def pick(blocks, step, sizes, after):
    line = sizes[3]
    return call(
        functools.partial(pick_kernel, len(blocks), sizes),
        [shaped((blocks[0].shape[0] // line, lanes), bf16)],
        step, *blocks, *after,
        in_specs=[pl.BlockSpec(memory_space=pltpu.SMEM)]
        + [pl.BlockSpec(memory_space=pltpu.VMEM)] * len(blocks)
        + [pl.BlockSpec(memory_space=pl.ANY)] * len(after),
    )[0]


def patch_kernel(choices, sizes, step_ref, stored_ref, labels_ref, *refs):
    moved_refs, (memory_ref, new_labels_ref, rows_ref, sem) = refs[:choices], refs[choices:]
    count, width = rows_ref.shape
    first, crossing, _, _ = positions(step_ref[0], *sizes)
    moved = moved_refs[0][...]
    for choice in range(1, choices):
        moved = jnp.where(crossing == choice, moved_refs[choice][...], moved)
    for at in range(blocks_of(width)):
        rows_ref[:, at * lanes : (at + 1) * lanes] = moved[at * count : (at + 1) * count, :]
    target = memory_ref.at[pl.ds(pl.multiple_of(first, count), count), :]
    copy = pltpu.make_async_copy(rows_ref, target, sem)
    copy.start()
    digits = moved[blocks_of(width) * count :, :].astype(f32)
    row = (digits[0:1, :] * 256.0 + digits[1:2, :]).astype(jnp.int32)
    old = labels_ref[...]
    turned = pltpu.roll(jnp.broadcast_to(row, old.shape), lax.rem(first, lanes), 1)
    slot = lax.broadcasted_iota(jnp.int32, old.shape, 0) * lanes + lax.broadcasted_iota(jnp.int32, old.shape, 1)
    new_labels_ref[...] = jnp.where((slot >= first) & (slot < first + count), turned, old)
    copy.wait()


def patch(stored, labels, choices, step, sizes):
    count, width = sizes[0], stored.shape[1]
    return call(
        functools.partial(patch_kernel, len(choices), sizes),
        [shaped(stored.shape, bf16), shaped(labels.shape, jnp.int32)],
        step, stored, labels, *choices,
        in_specs=[pl.BlockSpec(memory_space=pltpu.SMEM), pl.BlockSpec(memory_space=pl.ANY)]
        + [pl.BlockSpec(memory_space=pltpu.VMEM)] * (1 + len(choices)),
        out_specs=[pl.BlockSpec(memory_space=pl.ANY), pl.BlockSpec(memory_space=pltpu.VMEM)],
        scratch_shapes=[pltpu.VMEM((count, width), bf16), pltpu.SemaphoreType.DMA],
        input_output_aliases={1: 0},
    )


def split_digits(row):
    high = row.astype(bf16).astype(f32)
    return [high, row - high]


def sum_rows(size):
    return rounded_up(8 * (rounded_up(size, lanes) // lanes), 16)


def block_kernel(blocks, sides, chunk, count, copies, *refs):
    if copies:
        source_ref, target_ref, sem = refs[blocks + 2 * sides], refs[-3], refs[-1]
        copy = pltpu.make_async_copy(source_ref, target_ref, sem)
        copy.start()
        refs = refs[:-3] + refs[-2:-1]
    rows_refs, keys_refs = refs[:blocks], refs[blocks : blocks + sides]
    label_refs = refs[blocks + sides : blocks + 2 * sides]
    out_refs = refs[-1 - blocks : -1]
    anchors_ref = refs[-1]
    slots, width = keys_refs[0].shape
    parts = blocks_of(width)
    packed = rows_refs[0].shape[0]
    members = packed // (parts * count + 16)
    size = members * count
    columns = []
    for block, ref in enumerate(rows_refs):
        for member in range(members):
            first = member * (parts * count + 16)
            to = block * size + member * count
            for at in range(parts):
                anchors_ref[to : to + count, at * lanes : (at + 1) * lanes] = ref[
                    first + at * count : first + (at + 1) * count, :
                ]
            digits = ref[first + parts * count : first + parts * count + 16, :].astype(f32)
            columns.append(to_column((digits[0:1, :] * 256.0 + digits[1:2, :])[:, :count]))
    labels = jnp.concatenate(columns, axis=0)
    anchors = anchors_ref[...]
    rows = blocks * size
    pos_sum = jnp.zeros((rows, 1), f32)
    neg_sum = jnp.zeros((rows, 1), f32)
    total = None
    chunks = [(side, slice(at, at + chunk)) for side in range(sides) for at in range(0, slots, chunk)]

    def scores_of(side, part):
        return lax.dot_general(
            anchors, keys_refs[side][part, :], (((1,), (1,)), ((), ())), preferred_element_type=f32
        )

    scores = scores_of(*chunks[0])
    for at, (side, part) in enumerate(chunks):
        following = scores_of(*chunks[at + 1]) if at + 1 < len(chunks) else None
        slot_labels = label_refs[side][:, part].astype(f32)
        neg_shift = jnp.where(slot_labels < 0.0, -1e30, -neg_scale * margin * log2e)
        same = labels == slot_labels
        slope = jnp.where(same, -pos_scale * log2e, neg_scale * log2e)
        shift = jnp.where(same, pos_scale * margin * log2e, neg_shift)
        term = jnp.exp2(scores * slope + shift)
        pos = jnp.where(same, term, 0.0)
        neg = jnp.where(same, 0.0, term)
        pos_sum += jnp.sum(pos, axis=1, keepdims=True)
        neg_sum += jnp.sum(neg, axis=1, keepdims=True)
        weights = jnp.concatenate([neg.astype(bf16), pos.astype(bf16)], axis=0)
        more = jnp.dot(weights, keys_refs[side][part, :], preferred_element_type=f32)
        total = more if total is None else total + more
        scores = following
    floats = anchors.astype(f32)
    sums = [pos_sum, neg_sum]
    for which in range(2):
        value = total[which * rows : (which + 1) * rows, :]
        along = jnp.sum(value * floats, axis=1, keepdims=True)
        sums.append(along)
        rest = value - along * floats
        for block, ref in enumerate(out_refs):
            for at in range(parts):
                first = (which * parts + at) * size
                ref[first : first + size, :] = rest[
                    block * size : (block + 1) * size, at * lanes : (at + 1) * lanes
                ].astype(ref.dtype)
    for block, ref in enumerate(out_refs):
        lines = []
        for first in range(0, size, lanes):
            last = min(first + lanes, size)
            for value in sums:
                row = to_row(value[block * size + first : block * size + last])
                if last - first < lanes:
                    row = jnp.concatenate([row, jnp.zeros((1, lanes - last + first), f32)], axis=1)
                lines += split_digits(row)
        first = 2 * parts * size
        ref[first:, :] = rows_as_lanes(lines, ref.shape[0] - first).astype(ref.dtype)
    if copies:
        copy.wait()


def block_sums(blocks, keys, labels, count, dtype, after, copied=()):
    slots, width = keys[0].shape
    parts = blocks_of(width)
    size = blocks[0].shape[0] // (parts * count + 16) * count
    anywhere = pl.BlockSpec(memory_space=pl.ANY)
    vmem = pl.BlockSpec(memory_space=pltpu.VMEM)
    return call(
        functools.partial(block_kernel, len(blocks), len(keys), math.gcd(512, slots), count, len(copied)),
        [shaped((2 * parts * size + sum_rows(size), lanes), dtype)] * len(blocks)
        + [shaped(value.shape, value.dtype) for value in copied],
        *blocks, *[in_vmem(k) for k in keys], *labels, *copied, *after,
        work=12 * size * len(blocks) * slots * len(keys) * width,
        in_specs=[vmem] * (len(blocks) + 2 * len(keys)) + [anywhere] * (len(copied) + len(after)),
        out_specs=[vmem] * len(blocks) + [anywhere] * len(copied),
        scratch_shapes=[pltpu.VMEM((len(blocks) * size, width), bf16)]
        + [pltpu.SemaphoreType.DMA] * len(copied),
    )


def add_kernel(arrived, size, count, *refs):
    in_refs, out_refs = refs[: 1 + arrived], refs[-(size // count) :]
    columns = (in_refs[0].shape[0] - sum_rows(size)) // size

    def total(first, rows):
        value = in_refs[0][first : first + rows, :]
        for ref in in_refs[1:]:
            value = value + ref[first : first + rows, :].astype(f32)
        return value

    sums = total(columns * size, sum_rows(size))
    for block, ref in enumerate(out_refs):
        for at in range(columns):
            part = total(at * size + block * count, count)
            ref[at * count : (at + 1) * count, :] = part.astype(ref.dtype)
        group, lane = divmod(block * count, lanes)
        lines = []
        for which in range(4):
            row = 8 * group + 2 * which
            lines += split_digits(sums[row : row + 1, :] + sums[row + 1 : row + 2, :])
        packed = rows_as_lanes(lines, ref.shape[0] - columns * count)
        if lane:
            packed = pltpu.roll(packed, lanes - lane, 1)
        ref[columns * count :, :] = packed.astype(ref.dtype)


def add(held, arrived, size, count, columns, after):
    shape = (columns * count + sum_rows(count), lanes)
    outs = [shaped(shape, f32 if b == 0 else bf16) for b in range(size // count)]
    return call(
        functools.partial(add_kernel, len(arrived), size, count),
        outs,
        held, *arrived, *after,
        in_specs=[pl.BlockSpec(memory_space=pltpu.VMEM)] * (1 + len(arrived))
        + [pl.BlockSpec(memory_space=pl.ANY)] * len(after),
    )


def finish_kernel(arrived, *refs):
    held_ref, arrived_refs = refs[0], refs[1 : 1 + arrived]
    unit_ref, radius_ref, grad_ref, loss_ref = refs[1 + arrived :]
    count, width = unit_ref.shape
    parts = blocks_of(width)
    total = held_ref[...]
    for ref in arrived_refs:
        total = total + ref[...].astype(f32)
    sums = []
    for which in range(4):
        row = 2 * parts * count + 2 * which
        sums.append((total[row : row + 1, :] + total[row + 1 : row + 2, :])[:, :count])
    pos, neg = sums[:2]
    loss_ref[...] = jnp.log(1.0 + pos) / pos_scale + jnp.log(1.0 + neg) / neg_scale
    pos, neg, push_along, pull_along = [to_column(row) for row in sums]
    unit = unit_ref[...]
    anchors = unit.astype(bf16).astype(f32)
    push, pull = [
        jnp.concatenate([total[(first + at) * count : (first + at + 1) * count, :] for at in range(parts)], axis=1)
        for first in (0, parts)
    ]
    push = push + push_along * anchors
    pull = pull + pull_along * anchors
    grad_unit = push / (1.0 + neg) - pull / (1.0 + pos)
    along = jnp.sum(unit * grad_unit, axis=1, keepdims=True)
    grad_ref[...] = (grad_unit - unit * along) / radius_ref[:, :1]


def per_device(batch_rows, batch_labels, memory, memory_labels, keep_bits, step_index):
    groups = lax.axis_size("grp")
    members = lax.axis_size("dev")
    cores = 2 if members % 2 == 0 else 1
    line = members // cores
    count, width = batch_rows.shape
    slots = memory.shape[0]

    def exchange(value, axis, step):
        if axis == "grp":
            return lax.ppermute(value, "grp", [(i, i ^ step) for i in range(groups)])
        jump = step * cores if axis == "line" else step
        return lax.ppermute(value, "dev", [(i, i ^ jump) for i in range(members)])

    folded = (slots // lanes, lanes)
    parts = blocks_of(width)
    packed, unit, radius, slot_labels, copied_labels = call(
        prepare_kernel,
        [
            pltpu.VMEM((parts * count + 16, lanes), bf16),
            pltpu.VMEM((count, width), f32),
            pltpu.VMEM((count, lanes), f32),
            pltpu.VMEM(folded, jnp.int32),
            pltpu.VMEM(folded, jnp.int32),
        ],
        batch_rows, batch_labels.reshape(1, count), memory_labels.reshape(folded), keep_bits.reshape(folded),
        limit=vmem_most,
    )

    labels = [slot_labels] + [exchange(slot_labels, "core", s) for s in range(1, cores)]
    memories = [memory] + [exchange(memory, "core", s) for s in range(1, cores)]

    near = [packed] + [None] * (line - 1)
    for s in range(line - 1, 0, -1):
        near[s] = exchange(packed, "line", s)
    part = join(near, labels)
    labels = [value.reshape(1, slots) for value in labels]
    blocks = [part] + [None] * (groups - 1)
    for s in range(groups - 1, 0, -1):
        blocks[s] = exchange(part, "grp", s)
    keys = [keys_of(memory, pltpu.HBM, [part])] + [keys_of(value, pltpu.VMEM, [part]) for value in memories[1:]]

    size = count * line
    arrived, after = [], []
    places = list(range(groups - 1, 0, -1))
    while places:
        now = places[:1] if not after else places[:2]
        places = places[len(now) :]
        after = block_sums([blocks[s] for s in now], keys, labels, count, bf16, after)
        arrived += [exchange(value, "grp", s) for s, value in zip(now, after)]
    held, copied = block_sums([part], keys, labels, count, f32, after, [memory])
    sizes = (count, slots, groups, line, cores)
    moved = pick(blocks, step_index, sizes, after)
    choices = [moved] + [exchange(moved, "core", s) for s in range(1, cores)]

    sums, *others = add(held, arrived, size, count, 2 * parts, choices)
    arrived = [exchange(others[s - 1], "line", s) for s in range(line - 1, 0, -1)]
    grad_batch, loss = call(
        functools.partial(finish_kernel, len(arrived)),
        [shaped((count, width), f32), shaped((1, count), f32)],
        sums, *arrived, unit, radius,
    )

    new_memory, new_labels = patch(copied, copied_labels, choices, step_index, sizes)
    return (grad_batch, loss.reshape(count), new_memory, new_labels.reshape(slots))


def solution(mesh):
    placed = (
        P(("grp", "dev"), None),
        P(("grp", "dev")),
        P(("grp", "dev"), None),
        P(("grp", "dev")),
        P(("grp", "dev")),
        P(),
    )
    return jax.shard_map(
        per_device,
        mesh=mesh,
        in_specs=placed,
        out_specs=(
            P(("grp", "dev"), None),
            P(("grp", "dev")),
            P(("grp", "dev"), None),
            P(("grp", "dev")),
        ),
        check_vma=False,
    )
```

```python
import functools
import math

import jax
import jax.numpy as jnp
from jax import lax
from jax.experimental import pallas as pl
from jax.experimental.pallas import tpu as pltpu
from jax.sharding import PartitionSpec as P

pos_scale = 2.0
neg_scale = 50.0
margin = 0.5
lanes = 128
log2e = math.log2(math.e)
vmem_bytes = 20 * 1024 * 1024
vmem_most = 56 * 1024 * 1024
f32 = jnp.float32
bf16 = jnp.bfloat16


def call(body, outs, *args, work=0, limit=vmem_bytes, **kw):
    return pl.pallas_call(
        body,
        out_shape=outs,
        compiler_params=pltpu.CompilerParams(vmem_limit_bytes=limit),
        cost_estimate=pl.CostEstimate(flops=work, bytes_accessed=0, transcendentals=0),
        **kw,
    )(*args)


def shaped(shape, dtype):
    return jax.ShapeDtypeStruct(shape, dtype)


def in_vmem(value):
    return pltpu.with_memory_space_constraint(value, pltpu.VMEM)


def rounded_up(value, unit):
    return (value + unit - 1) // unit * unit


def blocks_of(width):
    return width // lanes


def rows_as_lanes(parts, rows):
    row = lax.broadcasted_iota(jnp.int32, (rows, lanes), 0)
    out = jnp.zeros((rows, lanes), f32)
    for at, part in enumerate(parts):
        out = jnp.where(row == at, part, out)
    return out


def prepare_kernel(rows_ref, labels_ref, stored_ref, keep_ref, packed_ref, unit_ref, radius_ref, slot_ref, copy_ref):
    stored = stored_ref[...]
    slot_ref[...] = jnp.where(keep_ref[...] > 0, stored, -1)
    copy_ref[...] = stored
    rows = rows_ref[...].astype(f32)
    count, width = rows.shape
    radius = jnp.sqrt(jnp.sum(rows * rows, axis=1, keepdims=True) + 1e-06)
    unit = rows / radius
    unit_ref[...] = unit
    radius_ref[...] = jnp.broadcast_to(radius, radius_ref.shape)
    anchors = unit.astype(bf16)
    for at in range(blocks_of(width)):
        packed_ref[at * count : (at + 1) * count, :] = anchors[:, at * lanes : (at + 1) * lanes]
    row = jnp.concatenate([labels_ref[...].astype(f32), jnp.zeros((1, lanes - count), f32)], axis=1)
    high = jnp.floor(row * (1.0 / 256.0))
    tail = packed_ref.shape[0] - blocks_of(width) * count
    packed_ref[blocks_of(width) * count :, :] = rows_as_lanes([high, row - high * 256.0], tail).astype(bf16)


def diagonal(count):
    across = lax.broadcasted_iota(jnp.int32, (count, count), 1)
    down = lax.broadcasted_iota(jnp.int32, (count, count), 0)
    return across == down


def to_column(row):
    count = row.shape[1]
    spread = jnp.broadcast_to(row, (count, count))
    return jnp.sum(jnp.where(diagonal(count), spread, 0.0), axis=1, keepdims=True)


def to_row(column):
    count = column.shape[0]
    spread = jnp.broadcast_to(column, (count, count))
    return jnp.sum(jnp.where(diagonal(count), spread, 0.0), axis=0, keepdims=True)


def keys_kernel(memory_ref, *refs):
    keys_ref = refs[-1]
    rows = memory_ref[...].astype(f32)
    radius = jnp.sqrt(jnp.sum(rows * rows, axis=1, keepdims=True) + 1e-06)
    keys_ref[...] = (rows / radius).astype(bf16)


def keys_of(memory, place, after):
    slots, width = memory.shape
    block = math.gcd(512, slots)
    spec = pl.BlockSpec((block, width), lambda i: (i, 0))
    return call(
        keys_kernel,
        [shaped((slots, width), bf16)],
        pltpu.with_memory_space_constraint(memory, place), *after,
        work=64 * slots * width * width,
        grid=(slots // block,),
        in_specs=[spec] + [pl.BlockSpec(memory_space=pl.ANY)] * len(after),
        out_specs=[spec],
    )[0]


def join_kernel(blocks, *refs):
    block_refs, out_ref = refs[:blocks], refs[-1]
    first = 0
    for ref in block_refs:
        out_ref[first : first + ref.shape[0], :] = ref[...]
        first += ref.shape[0]


def join(blocks, after):
    rows = sum(block.shape[0] for block in blocks)
    return call(
        functools.partial(join_kernel, len(blocks)),
        [shaped((rows, blocks[0].shape[1]), blocks[0].dtype)],
        *blocks, *after,
        in_specs=[pl.BlockSpec(memory_space=pltpu.VMEM)] * len(blocks)
        + [pl.BlockSpec(memory_space=pl.ANY)] * len(after),
    )[0]


def positions(step, count, slots, groups, line, cores):
    first = lax.rem(step, slots // count) * count
    crossing = lax.rem(step, cores)
    members = line * cores
    devices_all = groups * members
    grp = lax.axis_index("grp")
    dev = lax.axis_index("dev")
    target = grp * members + (dev ^ crossing)
    source = lax.rem(target + devices_all - lax.rem(step, devices_all), devices_all)
    source_grp = lax.div(source, members)
    source_line = lax.div(lax.rem(source, members), cores)
    step = lax.div(dev, cores) ^ source_line
    return first, crossing, grp ^ source_grp, lax.rem(line - step, line)


def pick_kernel(groups, sizes, step_ref, *refs):
    blocks_refs, out_ref = refs[:groups], refs[-1]
    rows = out_ref.shape[0]
    _, _, grp_place, line_place = positions(step_ref[0], *sizes)
    for place, ref in enumerate(blocks_refs):

        @pl.when(grp_place == place)
        def _():
            out_ref[...] = ref[pl.ds(pl.multiple_of(line_place * rows, 16), rows), :]


def pick(blocks, step, sizes, after):
    line = sizes[3]
    return call(
        functools.partial(pick_kernel, len(blocks), sizes),
        [shaped((blocks[0].shape[0] // line, lanes), bf16)],
        step, *blocks, *after,
        in_specs=[pl.BlockSpec(memory_space=pltpu.SMEM)]
        + [pl.BlockSpec(memory_space=pltpu.VMEM)] * len(blocks)
        + [pl.BlockSpec(memory_space=pl.ANY)] * len(after),
    )[0]


def patch_kernel(choices, sizes, step_ref, stored_ref, labels_ref, *refs):
    moved_refs, (memory_ref, new_labels_ref, rows_ref, sem) = refs[:choices], refs[choices:]
    count, width = rows_ref.shape
    first, crossing, _, _ = positions(step_ref[0], *sizes)
    moved = moved_refs[0][...]
    for choice in range(1, choices):
        moved = jnp.where(crossing == choice, moved_refs[choice][...], moved)
    for at in range(blocks_of(width)):
        rows_ref[:, at * lanes : (at + 1) * lanes] = moved[at * count : (at + 1) * count, :]
    target = memory_ref.at[pl.ds(pl.multiple_of(first, count), count), :]
    copy = pltpu.make_async_copy(rows_ref, target, sem)
    copy.start()
    digits = moved[blocks_of(width) * count :, :].astype(f32)
    row = (digits[0:1, :] * 256.0 + digits[1:2, :]).astype(jnp.int32)
    old = labels_ref[...]
    turned = pltpu.roll(jnp.broadcast_to(row, old.shape), lax.rem(first, lanes), 1)
    slot = lax.broadcasted_iota(jnp.int32, old.shape, 0) * lanes + lax.broadcasted_iota(jnp.int32, old.shape, 1)
    new_labels_ref[...] = jnp.where((slot >= first) & (slot < first + count), turned, old)
    copy.wait()


def patch(stored, labels, choices, step, sizes):
    count, width = sizes[0], stored.shape[1]
    return call(
        functools.partial(patch_kernel, len(choices), sizes),
        [shaped(stored.shape, bf16), shaped(labels.shape, jnp.int32)],
        step, stored, labels, *choices,
        in_specs=[pl.BlockSpec(memory_space=pltpu.SMEM), pl.BlockSpec(memory_space=pl.ANY)]
        + [pl.BlockSpec(memory_space=pltpu.VMEM)] * (1 + len(choices)),
        out_specs=[pl.BlockSpec(memory_space=pl.ANY), pl.BlockSpec(memory_space=pltpu.VMEM)],
        scratch_shapes=[pltpu.VMEM((count, width), bf16), pltpu.SemaphoreType.DMA],
        input_output_aliases={1: 0},
    )


def split_digits(row):
    high = row.astype(bf16).astype(f32)
    return [high, row - high]


def sum_rows(size):
    return rounded_up(8 * (rounded_up(size, lanes) // lanes), 16)


def block_kernel(blocks, sides, chunk, count, copies, *refs):
    if copies:
        source_ref, target_ref, sem = refs[blocks + 2 * sides], refs[-3], refs[-1]
        copy = pltpu.make_async_copy(source_ref, target_ref, sem)
        copy.start()
        refs = refs[:-3] + refs[-2:-1]
    rows_refs, keys_refs = refs[:blocks], refs[blocks : blocks + sides]
    label_refs = refs[blocks + sides : blocks + 2 * sides]
    out_refs = refs[-1 - blocks : -1]
    anchors_ref = refs[-1]
    slots, width = keys_refs[0].shape
    parts = blocks_of(width)
    packed = rows_refs[0].shape[0]
    members = packed // (parts * count + 16)
    size = members * count
    columns = []
    for block, ref in enumerate(rows_refs):
        for member in range(members):
            first = member * (parts * count + 16)
            to = block * size + member * count
            for at in range(parts):
                anchors_ref[to : to + count, at * lanes : (at + 1) * lanes] = ref[
                    first + at * count : first + (at + 1) * count, :
                ]
            digits = ref[first + parts * count : first + parts * count + 16, :].astype(f32)
            columns.append(to_column((digits[0:1, :] * 256.0 + digits[1:2, :])[:, :count]))
    labels = jnp.concatenate(columns, axis=0)
    anchors = anchors_ref[...]
    rows = blocks * size
    pos_sum = jnp.zeros((rows, 1), f32)
    neg_sum = jnp.zeros((rows, 1), f32)
    total = None
    chunks = [(side, slice(at, at + chunk)) for side in range(sides) for at in range(0, slots, chunk)]

    def scores_of(side, part):
        return lax.dot_general(
            anchors, keys_refs[side][part, :], (((1,), (1,)), ((), ())), preferred_element_type=f32
        )

    scores = scores_of(*chunks[0])
    for at, (side, part) in enumerate(chunks):
        following = scores_of(*chunks[at + 1]) if at + 1 < len(chunks) else None
        slot_labels = label_refs[side][:, part].astype(f32)
        neg_shift = jnp.where(slot_labels < 0.0, -1e30, -neg_scale * margin * log2e)
        same = labels == slot_labels
        slope = jnp.where(same, -pos_scale * log2e, neg_scale * log2e)
        shift = jnp.where(same, pos_scale * margin * log2e, neg_shift)
        term = jnp.exp2(scores * slope + shift)
        pos = jnp.where(same, term, 0.0)
        neg = jnp.where(same, 0.0, term)
        pos_sum += jnp.sum(pos, axis=1, keepdims=True)
        neg_sum += jnp.sum(neg, axis=1, keepdims=True)
        weights = jnp.concatenate([neg.astype(bf16), pos.astype(bf16)], axis=0)
        more = jnp.dot(weights, keys_refs[side][part, :], preferred_element_type=f32)
        total = more if total is None else total + more
        scores = following
    floats = anchors.astype(f32)
    sums = [pos_sum, neg_sum]
    for which in range(2):
        value = total[which * rows : (which + 1) * rows, :]
        along = jnp.sum(value * floats, axis=1, keepdims=True)
        sums.append(along)
        rest = value - along * floats
        for block, ref in enumerate(out_refs):
            for at in range(parts):
                first = (which * parts + at) * size
                ref[first : first + size, :] = rest[
                    block * size : (block + 1) * size, at * lanes : (at + 1) * lanes
                ].astype(ref.dtype)
    for block, ref in enumerate(out_refs):
        lines = []
        for first in range(0, size, lanes):
            last = min(first + lanes, size)
            for value in sums:
                row = to_row(value[block * size + first : block * size + last])
                if last - first < lanes:
                    row = jnp.concatenate([row, jnp.zeros((1, lanes - last + first), f32)], axis=1)
                lines += split_digits(row)
        first = 2 * parts * size
        ref[first:, :] = rows_as_lanes(lines, ref.shape[0] - first).astype(ref.dtype)
    if copies:
        copy.wait()


def block_sums(blocks, keys, labels, count, dtype, after, copied=()):
    slots, width = keys[0].shape
    parts = blocks_of(width)
    size = blocks[0].shape[0] // (parts * count + 16) * count
    anywhere = pl.BlockSpec(memory_space=pl.ANY)
    vmem = pl.BlockSpec(memory_space=pltpu.VMEM)
    return call(
        functools.partial(block_kernel, len(blocks), len(keys), math.gcd(1024, slots), count, len(copied)),
        [shaped((2 * parts * size + sum_rows(size), lanes), dtype)] * len(blocks)
        + [shaped(value.shape, value.dtype) for value in copied],
        *blocks, *[in_vmem(k) for k in keys], *labels, *copied, *after,
        work=12 * size * len(blocks) * slots * len(keys) * width,
        in_specs=[vmem] * (len(blocks) + 2 * len(keys)) + [anywhere] * (len(copied) + len(after)),
        out_specs=[vmem] * len(blocks) + [anywhere] * len(copied),
        scratch_shapes=[pltpu.VMEM((len(blocks) * size, width), bf16)]
        + [pltpu.SemaphoreType.DMA] * len(copied),
    )


def add_kernel(arrived, size, count, *refs):
    in_refs, out_refs = refs[: 1 + arrived], refs[-(size // count) :]
    columns = (in_refs[0].shape[0] - sum_rows(size)) // size

    def total(first, rows):
        value = in_refs[0][first : first + rows, :]
        for ref in in_refs[1:]:
            value = value + ref[first : first + rows, :].astype(f32)
        return value

    sums = total(columns * size, sum_rows(size))
    for block, ref in enumerate(out_refs):
        for at in range(columns):
            part = total(at * size + block * count, count)
            ref[at * count : (at + 1) * count, :] = part.astype(ref.dtype)
        group, lane = divmod(block * count, lanes)
        lines = []
        for which in range(4):
            row = 8 * group + 2 * which
            lines += split_digits(sums[row : row + 1, :] + sums[row + 1 : row + 2, :])
        packed = rows_as_lanes(lines, ref.shape[0] - columns * count)
        if lane:
            packed = pltpu.roll(packed, lanes - lane, 1)
        ref[columns * count :, :] = packed.astype(ref.dtype)


def add(held, arrived, size, count, columns, after):
    shape = (columns * count + sum_rows(count), lanes)
    outs = [shaped(shape, f32 if b == 0 else bf16) for b in range(size // count)]
    return call(
        functools.partial(add_kernel, len(arrived), size, count),
        outs,
        held, *arrived, *after,
        in_specs=[pl.BlockSpec(memory_space=pltpu.VMEM)] * (1 + len(arrived))
        + [pl.BlockSpec(memory_space=pl.ANY)] * len(after),
    )


def finish_kernel(arrived, *refs):
    held_ref, arrived_refs = refs[0], refs[1 : 1 + arrived]
    unit_ref, radius_ref, grad_ref, loss_ref = refs[1 + arrived :]
    count, width = unit_ref.shape
    parts = blocks_of(width)
    total = held_ref[...]
    for ref in arrived_refs:
        total = total + ref[...].astype(f32)
    sums = []
    for which in range(4):
        row = 2 * parts * count + 2 * which
        sums.append((total[row : row + 1, :] + total[row + 1 : row + 2, :])[:, :count])
    pos, neg = sums[:2]
    loss_ref[...] = jnp.log(1.0 + pos) / pos_scale + jnp.log(1.0 + neg) / neg_scale
    pos, neg, push_along, pull_along = [to_column(row) for row in sums]
    unit = unit_ref[...]
    anchors = unit.astype(bf16).astype(f32)
    push, pull = [
        jnp.concatenate([total[(first + at) * count : (first + at + 1) * count, :] for at in range(parts)], axis=1)
        for first in (0, parts)
    ]
    push = push + push_along * anchors
    pull = pull + pull_along * anchors
    grad_unit = push / (1.0 + neg) - pull / (1.0 + pos)
    along = jnp.sum(unit * grad_unit, axis=1, keepdims=True)
    grad_ref[...] = (grad_unit - unit * along) / radius_ref[:, :1]


def per_device(batch_rows, batch_labels, memory, memory_labels, keep_bits, step_index):
    groups = lax.axis_size("grp")
    members = lax.axis_size("dev")
    cores = 2 if members % 2 == 0 else 1
    line = members // cores
    count, width = batch_rows.shape
    slots = memory.shape[0]

    def exchange(value, axis, step):
        if axis == "grp":
            return lax.ppermute(value, "grp", [(i, i ^ step) for i in range(groups)])
        jump = step * cores if axis == "line" else step
        return lax.ppermute(value, "dev", [(i, i ^ jump) for i in range(members)])

    folded = (slots // lanes, lanes)
    parts = blocks_of(width)
    packed, unit, radius, slot_labels, copied_labels = call(
        prepare_kernel,
        [
            pltpu.VMEM((parts * count + 16, lanes), bf16),
            pltpu.VMEM((count, width), f32),
            pltpu.VMEM((count, lanes), f32),
            pltpu.VMEM(folded, jnp.int32),
            pltpu.VMEM(folded, jnp.int32),
        ],
        batch_rows, batch_labels.reshape(1, count), memory_labels.reshape(folded), keep_bits.reshape(folded),
        limit=vmem_most,
    )

    labels = [slot_labels] + [exchange(slot_labels, "core", s) for s in range(1, cores)]
    memories = [memory] + [exchange(memory, "core", s) for s in range(1, cores)]

    part = packed
    for s in range(line - 1, 0, -1):
        part = join([part, exchange(packed, "line", s)], labels if s == 1 else [])
    labels = [value.reshape(1, slots) for value in labels]
    blocks = [part] + [None] * (groups - 1)
    for s in range(groups - 1, 0, -1):
        blocks[s] = exchange(part, "grp", s)
    keys = [keys_of(memory, pltpu.HBM, [part])] + [keys_of(value, pltpu.VMEM, [part]) for value in memories[1:]]

    size = count * line
    arrived, after = [], []
    places = list(range(groups - 1, 0, -1))
    while places:
        now = places[:1] if not after else places[:2]
        places = places[len(now) :]
        after = block_sums([blocks[s] for s in now], keys, labels, count, bf16, after)
        arrived += [exchange(value, "grp", s) for s, value in zip(now, after)]
    held, copied = block_sums([part], keys, labels, count, f32, after, [memory])
    sizes = (count, slots, groups, line, cores)
    moved = pick(blocks, step_index, sizes, after)
    choices = [moved] + [exchange(moved, "core", s) for s in range(1, cores)]

    sums, *others = add(held, arrived, size, count, 2 * parts, choices)
    arrived = [exchange(value, "line", line - at) for at, value in enumerate(others, 1)]
    grad_batch, loss = call(
        functools.partial(finish_kernel, len(arrived)),
        [shaped((count, width), f32), shaped((1, count), f32)],
        sums, *arrived, unit, radius,
    )

    new_memory, new_labels = patch(copied, copied_labels, choices, step_index, sizes)
    return (grad_batch, loss.reshape(count), new_memory, new_labels.reshape(slots))


def solution(mesh):
    placed = (
        P(("grp", "dev"), None),
        P(("grp", "dev")),
        P(("grp", "dev"), None),
        P(("grp", "dev")),
        P(("grp", "dev")),
        P(),
    )
    return jax.shard_map(
        per_device,
        mesh=mesh,
        in_specs=placed,
        out_specs=(
            P(("grp", "dev"), None),
            P(("grp", "dev")),
            P(("grp", "dev"), None),
            P(("grp", "dev")),
        ),
        check_vma=False,
    )
```

```python
import functools
import math

import jax
import jax.numpy as jnp
from jax import lax
from jax.experimental import pallas as pl
from jax.experimental.pallas import tpu as pltpu
from jax.sharding import PartitionSpec as P

pos_scale = 2.0
neg_scale = 50.0
margin = 0.5
lanes = 128
log2e = math.log2(math.e)
vmem_bytes = 20 * 1024 * 1024
vmem_most = 56 * 1024 * 1024
f32 = jnp.float32
bf16 = jnp.bfloat16


def call(body, outs, *args, work=0, limit=vmem_bytes, **kw):
    return pl.pallas_call(
        body,
        out_shape=outs,
        compiler_params=pltpu.CompilerParams(vmem_limit_bytes=limit),
        cost_estimate=pl.CostEstimate(flops=work, bytes_accessed=0, transcendentals=0),
        **kw,
    )(*args)


def shaped(shape, dtype):
    return jax.ShapeDtypeStruct(shape, dtype)


def in_vmem(value):
    return pltpu.with_memory_space_constraint(value, pltpu.VMEM)


def rounded_up(value, unit):
    return (value + unit - 1) // unit * unit


def blocks_of(width):
    return width // lanes


def rows_as_lanes(parts, rows):
    row = lax.broadcasted_iota(jnp.int32, (rows, lanes), 0)
    out = jnp.zeros((rows, lanes), f32)
    for at, part in enumerate(parts):
        out = jnp.where(row == at, part, out)
    return out


def prepare_kernel(rows_ref, labels_ref, stored_ref, keep_ref, packed_ref, unit_ref, radius_ref, slot_ref, copy_ref):
    stored = stored_ref[...]
    slot_ref[...] = jnp.where(keep_ref[...] > 0, stored, -1)
    copy_ref[...] = stored
    rows = rows_ref[...].astype(f32)
    count, width = rows.shape
    radius = jnp.sqrt(jnp.sum(rows * rows, axis=1, keepdims=True) + 1e-06)
    unit = rows / radius
    unit_ref[...] = unit
    radius_ref[...] = jnp.broadcast_to(radius, radius_ref.shape)
    anchors = unit.astype(bf16)
    for at in range(blocks_of(width)):
        packed_ref[at * count : (at + 1) * count, :] = anchors[:, at * lanes : (at + 1) * lanes]
    row = jnp.concatenate([labels_ref[...].astype(f32), jnp.zeros((1, lanes - count), f32)], axis=1)
    high = jnp.floor(row * (1.0 / 256.0))
    tail = packed_ref.shape[0] - blocks_of(width) * count
    packed_ref[blocks_of(width) * count :, :] = rows_as_lanes([high, row - high * 256.0], tail).astype(bf16)


def diagonal(count):
    across = lax.broadcasted_iota(jnp.int32, (count, count), 1)
    down = lax.broadcasted_iota(jnp.int32, (count, count), 0)
    return across == down


def to_column(row):
    count = row.shape[1]
    spread = jnp.broadcast_to(row, (count, count))
    return jnp.sum(jnp.where(diagonal(count), spread, 0.0), axis=1, keepdims=True)


def to_row(column):
    count = column.shape[0]
    spread = jnp.broadcast_to(column, (count, count))
    return jnp.sum(jnp.where(diagonal(count), spread, 0.0), axis=0, keepdims=True)


def keys_kernel(memory_ref, *refs):
    keys_ref = refs[-1]
    rows = memory_ref[...].astype(f32)
    radius = jnp.sqrt(jnp.sum(rows * rows, axis=1, keepdims=True) + 1e-06)
    keys_ref[...] = (rows / radius).astype(bf16)


def keys_of(memory, place, after):
    slots, width = memory.shape
    block = math.gcd(512, slots)
    spec = pl.BlockSpec((block, width), lambda i: (i, 0))
    return call(
        keys_kernel,
        [shaped((slots, width), bf16)],
        pltpu.with_memory_space_constraint(memory, place), *after,
        work=64 * slots * width * width,
        grid=(slots // block,),
        in_specs=[spec] + [pl.BlockSpec(memory_space=pl.ANY)] * len(after),
        out_specs=[spec],
    )[0]


def join_kernel(blocks, *refs):
    block_refs, out_ref = refs[:blocks], refs[-1]
    first = 0
    for ref in block_refs:
        out_ref[first : first + ref.shape[0], :] = ref[...]
        first += ref.shape[0]


def join(blocks, after):
    rows = sum(block.shape[0] for block in blocks)
    return call(
        functools.partial(join_kernel, len(blocks)),
        [shaped((rows, blocks[0].shape[1]), blocks[0].dtype)],
        *blocks, *after,
        in_specs=[pl.BlockSpec(memory_space=pltpu.VMEM)] * len(blocks)
        + [pl.BlockSpec(memory_space=pl.ANY)] * len(after),
    )[0]


def positions(step, count, slots, groups, line, cores):
    first = lax.rem(step, slots // count) * count
    crossing = lax.rem(step, cores)
    members = line * cores
    devices_all = groups * members
    grp = lax.axis_index("grp")
    dev = lax.axis_index("dev")
    target = grp * members + (dev ^ crossing)
    source = lax.rem(target + devices_all - lax.rem(step, devices_all), devices_all)
    source_grp = lax.div(source, members)
    source_line = lax.div(lax.rem(source, members), cores)
    step = lax.div(dev, cores) ^ source_line
    return first, crossing, grp ^ source_grp, lax.rem(line - step, line)


def pick_kernel(groups, sizes, step_ref, *refs):
    blocks_refs, out_ref = refs[:groups], refs[-1]
    rows = out_ref.shape[0]
    _, _, grp_place, line_place = positions(step_ref[0], *sizes)
    for place, ref in enumerate(blocks_refs):

        @pl.when(grp_place == place)
        def _():
            out_ref[...] = ref[pl.ds(pl.multiple_of(line_place * rows, 16), rows), :]


def pick(blocks, step, sizes, after):
    line = sizes[3]
    return call(
        functools.partial(pick_kernel, len(blocks), sizes),
        [shaped((blocks[0].shape[0] // line, lanes), bf16)],
        step, *blocks, *after,
        in_specs=[pl.BlockSpec(memory_space=pltpu.SMEM)]
        + [pl.BlockSpec(memory_space=pltpu.VMEM)] * len(blocks)
        + [pl.BlockSpec(memory_space=pl.ANY)] * len(after),
    )[0]


def patch_kernel(choices, sizes, step_ref, stored_ref, labels_ref, *refs):
    moved_refs, (memory_ref, new_labels_ref, rows_ref, sem) = refs[:choices], refs[choices:]
    count, width = rows_ref.shape
    first, crossing, _, _ = positions(step_ref[0], *sizes)
    moved = moved_refs[0][...]
    for choice in range(1, choices):
        moved = jnp.where(crossing == choice, moved_refs[choice][...], moved)
    for at in range(blocks_of(width)):
        rows_ref[:, at * lanes : (at + 1) * lanes] = moved[at * count : (at + 1) * count, :]
    target = memory_ref.at[pl.ds(pl.multiple_of(first, count), count), :]
    copy = pltpu.make_async_copy(rows_ref, target, sem)
    copy.start()
    digits = moved[blocks_of(width) * count :, :].astype(f32)
    row = (digits[0:1, :] * 256.0 + digits[1:2, :]).astype(jnp.int32)
    old = labels_ref[...]
    turned = pltpu.roll(jnp.broadcast_to(row, old.shape), lax.rem(first, lanes), 1)
    slot = lax.broadcasted_iota(jnp.int32, old.shape, 0) * lanes + lax.broadcasted_iota(jnp.int32, old.shape, 1)
    new_labels_ref[...] = jnp.where((slot >= first) & (slot < first + count), turned, old)
    copy.wait()


def patch(stored, labels, choices, step, sizes):
    count, width = sizes[0], stored.shape[1]
    return call(
        functools.partial(patch_kernel, len(choices), sizes),
        [shaped(stored.shape, bf16), shaped(labels.shape, jnp.int32)],
        step, stored, labels, *choices,
        in_specs=[pl.BlockSpec(memory_space=pltpu.SMEM), pl.BlockSpec(memory_space=pl.ANY)]
        + [pl.BlockSpec(memory_space=pltpu.VMEM)] * (1 + len(choices)),
        out_specs=[pl.BlockSpec(memory_space=pl.ANY), pl.BlockSpec(memory_space=pltpu.VMEM)],
        scratch_shapes=[pltpu.VMEM((count, width), bf16), pltpu.SemaphoreType.DMA],
        input_output_aliases={1: 0},
    )


def split_digits(row):
    high = row.astype(bf16).astype(f32)
    return [high, row - high]


def sum_rows(size):
    return rounded_up(8 * (rounded_up(size, lanes) // lanes), 16)


def block_kernel(blocks, sides, unit, count, copies, scratch, *refs):
    if copies:
        source_ref, target_ref, sem = refs[blocks + 2 * sides], refs[-scratch - 1], refs[-1]
        copy = pltpu.make_async_copy(source_ref, target_ref, sem)
        copy.start()
        refs = refs[: -scratch - 1] + refs[-scratch : -1]
        scratch -= 1
    rows_refs, keys_refs = refs[:blocks], refs[blocks : blocks + sides]
    label_refs = refs[blocks + sides : blocks + 2 * sides]
    out_refs = refs[-scratch - blocks : -scratch]
    anchors_ref, labels_ref, total_ref, pos_ref, neg_ref = refs[-scratch:-4]
    scores_refs, weight_refs = refs[-4:-2], refs[-2:]
    slots, width = keys_refs[0].shape
    parts = blocks_of(width)
    packed = rows_refs[0].shape[0]
    members = packed // (parts * count + 16)
    size = members * count
    columns = []
    for block, ref in enumerate(rows_refs):
        for member in range(members):
            first = member * (parts * count + 16)
            to = block * size + member * count
            for at in range(parts):
                anchors_ref[to : to + count, at * lanes : (at + 1) * lanes] = ref[
                    first + at * count : first + (at + 1) * count, :
                ]
            digits = ref[first + parts * count : first + parts * count + 16, :].astype(f32)
            columns.append(to_column((digits[0:1, :] * 256.0 + digits[1:2, :])[:, :count]))
    rows = blocks * size
    labels_ref[...] = jnp.broadcast_to(jnp.concatenate(columns, axis=0), labels_ref.shape)
    pos_ref[...] = jnp.zeros_like(pos_ref)
    neg_ref[...] = jnp.zeros_like(neg_ref)
    anchors = anchors_ref[...]
    units = [(side, at) for side in range(sides) for at in range(0, slots, unit)]
    quarter = rows // 4

    def score_unit(at):
        side, first = units[at]
        scores_refs[at % 2][...] = lax.dot_general(
            anchors, keys_refs[side][first : first + unit, :], (((1,), (1,)), ((), ())), preferred_element_type=f32
        )

    def term_unit(at, which):
        side, first = units[at]
        part = slice(which * quarter, (which + 1) * quarter)
        weights_ref = weight_refs[at // 2 % 2]
        wanted = labels_ref[part, :]
        pos_sum, neg_sum = pos_ref[part, :], neg_ref[part, :]
        for piece in range(0, unit, lanes):
            slot_labels = label_refs[side][:, first + piece : first + piece + lanes].astype(f32)
            neg_shift = jnp.where(slot_labels < 0.0, -1e30, -neg_scale * margin * log2e)
            same = wanted == slot_labels
            slope = jnp.where(same, -pos_scale * log2e, neg_scale * log2e)
            shift = jnp.where(same, pos_scale * margin * log2e, neg_shift)
            term = jnp.exp2(scores_refs[at % 2][part, piece : piece + lanes] * slope + shift)
            pos = jnp.where(same, term, 0.0)
            neg = jnp.where(same, 0.0, term)
            pos_sum += pos
            neg_sum += neg
            to = slice(at % 2 * unit + piece, at % 2 * unit + piece + lanes)
            weights_ref[part, to] = neg.astype(bf16)
            weights_ref[rows + which * quarter : rows + (which + 1) * quarter, to] = pos.astype(bf16)
        pos_ref[part, :] = pos_sum
        neg_ref[part, :] = neg_sum

    def weigh_half(pair, half):
        side, first = units[2 * pair]
        part = slice(half * (width // 2), (half + 1) * (width // 2))
        more = jnp.dot(
            weight_refs[pair % 2][...], keys_refs[side][first : first + 2 * unit, part], preferred_element_type=f32
        )
        total_ref[:, part] = more if pair == 0 else total_ref[:, part] + more

    score_unit(0)
    for at in range(len(units)):
        term_unit(at, 0)
        if at + 1 < len(units):
            score_unit(at + 1)
        term_unit(at, 1)
        term_unit(at, 2)
        if at >= 2:
            weigh_half(at // 2 - 1, at % 2)
        term_unit(at, 3)
    weigh_half(len(units) // 2 - 1, 0)
    weigh_half(len(units) // 2 - 1, 1)
    total = total_ref[...]
    pos_sum = jnp.sum(pos_ref[...], axis=1, keepdims=True)
    neg_sum = jnp.sum(neg_ref[...], axis=1, keepdims=True)
    floats = anchors.astype(f32)
    sums = [pos_sum, neg_sum]
    for which in range(2):
        value = total[which * rows : (which + 1) * rows, :]
        along = jnp.sum(value * floats, axis=1, keepdims=True)
        sums.append(along)
        rest = value - along * floats
        for block, ref in enumerate(out_refs):
            for at in range(parts):
                first = (which * parts + at) * size
                ref[first : first + size, :] = rest[
                    block * size : (block + 1) * size, at * lanes : (at + 1) * lanes
                ].astype(ref.dtype)
    for block, ref in enumerate(out_refs):
        lines = []
        for first in range(0, size, lanes):
            last = min(first + lanes, size)
            for value in sums:
                row = to_row(value[block * size + first : block * size + last])
                if last - first < lanes:
                    row = jnp.concatenate([row, jnp.zeros((1, lanes - last + first), f32)], axis=1)
                lines += split_digits(row)
        first = 2 * parts * size
        ref[first:, :] = rows_as_lanes(lines, ref.shape[0] - first).astype(ref.dtype)
    if copies:
        copy.wait()


def block_sums(blocks, keys, labels, count, dtype, after, copied=()):
    slots, width = keys[0].shape
    parts = blocks_of(width)
    size = blocks[0].shape[0] // (parts * count + 16) * count
    rows = len(blocks) * size
    unit = math.gcd(256, slots // 2)
    anywhere = pl.BlockSpec(memory_space=pl.ANY)
    vmem = pl.BlockSpec(memory_space=pltpu.VMEM)
    return call(
        functools.partial(block_kernel, len(blocks), len(keys), unit, count, len(copied), 9 + len(copied)),
        [shaped((2 * parts * size + sum_rows(size), lanes), dtype)] * len(blocks)
        + [shaped(value.shape, value.dtype) for value in copied],
        *blocks, *[in_vmem(k) for k in keys], *labels, *copied, *after,
        work=12 * size * len(blocks) * slots * len(keys) * width,
        in_specs=[vmem] * (len(blocks) + 2 * len(keys)) + [anywhere] * (len(copied) + len(after)),
        out_specs=[vmem] * len(blocks) + [anywhere] * len(copied),
        scratch_shapes=[
            pltpu.VMEM((rows, width), bf16),
            pltpu.VMEM((rows, lanes), f32),
            pltpu.VMEM((2 * rows, width), f32),
            pltpu.VMEM((rows, lanes), f32),
            pltpu.VMEM((rows, lanes), f32),
            pltpu.VMEM((rows, unit), f32),
            pltpu.VMEM((rows, unit), f32),
            pltpu.VMEM((2 * rows, 2 * unit), bf16),
            pltpu.VMEM((2 * rows, 2 * unit), bf16),
        ]
        + [pltpu.SemaphoreType.DMA] * len(copied),
    )


def add_kernel(arrived, size, count, *refs):
    in_refs, out_refs = refs[: 1 + arrived], refs[-(size // count) :]
    columns = (in_refs[0].shape[0] - sum_rows(size)) // size

    def total(first, rows):
        value = in_refs[0][first : first + rows, :]
        for ref in in_refs[1:]:
            value = value + ref[first : first + rows, :].astype(f32)
        return value

    sums = total(columns * size, sum_rows(size))
    for block, ref in enumerate(out_refs):
        for at in range(columns):
            part = total(at * size + block * count, count)
            ref[at * count : (at + 1) * count, :] = part.astype(ref.dtype)
        group, lane = divmod(block * count, lanes)
        lines = []
        for which in range(4):
            row = 8 * group + 2 * which
            lines += split_digits(sums[row : row + 1, :] + sums[row + 1 : row + 2, :])
        packed = rows_as_lanes(lines, ref.shape[0] - columns * count)
        if lane:
            packed = pltpu.roll(packed, lanes - lane, 1)
        ref[columns * count :, :] = packed.astype(ref.dtype)


def add(held, arrived, size, count, columns, after):
    shape = (columns * count + sum_rows(count), lanes)
    outs = [shaped(shape, f32 if b == 0 else bf16) for b in range(size // count)]
    return call(
        functools.partial(add_kernel, len(arrived), size, count),
        outs,
        held, *arrived, *after,
        in_specs=[pl.BlockSpec(memory_space=pltpu.VMEM)] * (1 + len(arrived))
        + [pl.BlockSpec(memory_space=pl.ANY)] * len(after),
    )


def finish_kernel(arrived, *refs):
    held_ref, arrived_refs = refs[0], refs[1 : 1 + arrived]
    unit_ref, radius_ref, grad_ref, loss_ref = refs[1 + arrived :]
    count, width = unit_ref.shape
    parts = blocks_of(width)
    total = held_ref[...]
    for ref in arrived_refs:
        total = total + ref[...].astype(f32)
    sums = []
    for which in range(4):
        row = 2 * parts * count + 2 * which
        sums.append((total[row : row + 1, :] + total[row + 1 : row + 2, :])[:, :count])
    pos, neg = sums[:2]
    loss_ref[...] = jnp.log(1.0 + pos) / pos_scale + jnp.log(1.0 + neg) / neg_scale
    pos, neg, push_along, pull_along = [to_column(row) for row in sums]
    unit = unit_ref[...]
    anchors = unit.astype(bf16).astype(f32)
    push, pull = [
        jnp.concatenate([total[(first + at) * count : (first + at + 1) * count, :] for at in range(parts)], axis=1)
        for first in (0, parts)
    ]
    push = push + push_along * anchors
    pull = pull + pull_along * anchors
    grad_unit = push / (1.0 + neg) - pull / (1.0 + pos)
    along = jnp.sum(unit * grad_unit, axis=1, keepdims=True)
    grad_ref[...] = (grad_unit - unit * along) / radius_ref[:, :1]


def per_device(batch_rows, batch_labels, memory, memory_labels, keep_bits, step_index):
    groups = lax.axis_size("grp")
    members = lax.axis_size("dev")
    cores = 2 if members % 2 == 0 else 1
    line = members // cores
    count, width = batch_rows.shape
    slots = memory.shape[0]

    def exchange(value, axis, step):
        if axis == "grp":
            return lax.ppermute(value, "grp", [(i, i ^ step) for i in range(groups)])
        jump = step * cores if axis == "line" else step
        return lax.ppermute(value, "dev", [(i, i ^ jump) for i in range(members)])

    folded = (slots // lanes, lanes)
    parts = blocks_of(width)
    packed, unit, radius, slot_labels, copied_labels = call(
        prepare_kernel,
        [
            pltpu.VMEM((parts * count + 16, lanes), bf16),
            pltpu.VMEM((count, width), f32),
            pltpu.VMEM((count, lanes), f32),
            pltpu.VMEM(folded, jnp.int32),
            pltpu.VMEM(folded, jnp.int32),
        ],
        batch_rows, batch_labels.reshape(1, count), memory_labels.reshape(folded), keep_bits.reshape(folded),
        limit=vmem_most,
    )

    labels = [slot_labels] + [exchange(slot_labels, "core", s) for s in range(1, cores)]
    memories = [memory] + [exchange(memory, "core", s) for s in range(1, cores)]

    part = packed
    for s in range(line - 1, 0, -1):
        part = join([part, exchange(packed, "line", s)], labels if s == 1 else [])
    labels = [value.reshape(1, slots) for value in labels]
    blocks = [part] + [None] * (groups - 1)
    for s in range(groups - 1, 0, -1):
        blocks[s] = exchange(part, "grp", s)
    keys = [keys_of(memory, pltpu.HBM, [part])] + [keys_of(value, pltpu.VMEM, [part]) for value in memories[1:]]

    size = count * line
    arrived, after = [], []
    places = list(range(groups - 1, 0, -1))
    while places:
        now = places[:1] if not after else places[:2]
        places = places[len(now) :]
        after = block_sums([blocks[s] for s in now], keys, labels, count, bf16, after)
        arrived += [exchange(value, "grp", s) for s, value in zip(now, after)]
    held, copied = block_sums([part], keys, labels, count, f32, after, [memory])
    sizes = (count, slots, groups, line, cores)
    moved = pick(blocks, step_index, sizes, after)
    choices = [moved] + [exchange(moved, "core", s) for s in range(1, cores)]

    sums, *others = add(held, arrived, size, count, 2 * parts, choices)
    arrived = [exchange(value, "line", line - at) for at, value in enumerate(others, 1)]
    grad_batch, loss = call(
        functools.partial(finish_kernel, len(arrived)),
        [shaped((count, width), f32), shaped((1, count), f32)],
        sums, *arrived, unit, radius,
    )

    new_memory, new_labels = patch(copied, copied_labels, choices, step_index, sizes)
    return (grad_batch, loss.reshape(count), new_memory, new_labels.reshape(slots))


def solution(mesh):
    placed = (
        P(("grp", "dev"), None),
        P(("grp", "dev")),
        P(("grp", "dev"), None),
        P(("grp", "dev")),
        P(("grp", "dev")),
        P(),
    )
    return jax.shard_map(
        per_device,
        mesh=mesh,
        in_specs=placed,
        out_specs=(
            P(("grp", "dev"), None),
            P(("grp", "dev")),
            P(("grp", "dev"), None),
            P(("grp", "dev")),
        ),
        check_vma=False,
    )
```

```python
import functools
import math

import jax
import jax.numpy as jnp
from jax import lax
from jax.experimental import pallas as pl
from jax.experimental.pallas import tpu as pltpu
from jax.sharding import PartitionSpec as P

pos_scale = 2.0
neg_scale = 50.0
margin = 0.5
lanes = 128
log2e = math.log2(math.e)
vmem_bytes = 20 * 1024 * 1024
vmem_most = 56 * 1024 * 1024
f32 = jnp.float32
bf16 = jnp.bfloat16


def call(body, outs, *args, work=0, limit=vmem_bytes, **kw):
    return pl.pallas_call(
        body,
        out_shape=outs,
        compiler_params=pltpu.CompilerParams(vmem_limit_bytes=limit),
        cost_estimate=pl.CostEstimate(flops=work, bytes_accessed=0, transcendentals=0),
        **kw,
    )(*args)


def shaped(shape, dtype):
    return jax.ShapeDtypeStruct(shape, dtype)


def in_vmem(value):
    return pltpu.with_memory_space_constraint(value, pltpu.VMEM)


def rounded_up(value, unit):
    return (value + unit - 1) // unit * unit


def blocks_of(width):
    return width // lanes


def rows_as_lanes(parts, rows):
    row = lax.broadcasted_iota(jnp.int32, (rows, lanes), 0)
    out = jnp.zeros((rows, lanes), f32)
    for at, part in enumerate(parts):
        out = jnp.where(row == at, part, out)
    return out


def prepare_kernel(rows_ref, labels_ref, stored_ref, keep_ref, packed_ref, unit_ref, radius_ref, slot_ref, copy_ref):
    stored = stored_ref[...]
    slot_ref[...] = jnp.where(keep_ref[...] > 0, stored, -1)
    copy_ref[...] = stored
    rows = rows_ref[...].astype(f32)
    count, width = rows.shape
    radius = jnp.sqrt(jnp.sum(rows * rows, axis=1, keepdims=True) + 1e-06)
    unit = rows / radius
    unit_ref[...] = unit
    radius_ref[...] = jnp.broadcast_to(radius, radius_ref.shape)
    anchors = unit.astype(bf16)
    for at in range(blocks_of(width)):
        packed_ref[at * count : (at + 1) * count, :] = anchors[:, at * lanes : (at + 1) * lanes]
    row = jnp.concatenate([labels_ref[...].astype(f32), jnp.zeros((1, lanes - count), f32)], axis=1)
    high = jnp.floor(row * (1.0 / 256.0))
    tail = packed_ref.shape[0] - blocks_of(width) * count
    packed_ref[blocks_of(width) * count :, :] = rows_as_lanes([high, row - high * 256.0], tail).astype(bf16)


def diagonal(count):
    across = lax.broadcasted_iota(jnp.int32, (count, count), 1)
    down = lax.broadcasted_iota(jnp.int32, (count, count), 0)
    return across == down


def to_column(row):
    count = row.shape[1]
    spread = jnp.broadcast_to(row, (count, count))
    return jnp.sum(jnp.where(diagonal(count), spread, 0.0), axis=1, keepdims=True)


def to_row(column):
    count = column.shape[0]
    spread = jnp.broadcast_to(column, (count, count))
    return jnp.sum(jnp.where(diagonal(count), spread, 0.0), axis=0, keepdims=True)


def keys_kernel(memory_ref, *refs):
    keys_ref = refs[-1]
    rows = memory_ref[...].astype(f32)
    radius = jnp.sqrt(jnp.sum(rows * rows, axis=1, keepdims=True) + 1e-06)
    keys_ref[...] = (rows / radius).astype(bf16)


def keys_of(memory, place, after):
    slots, width = memory.shape
    block = math.gcd(512, slots)
    spec = pl.BlockSpec((block, width), lambda i: (i, 0))
    return call(
        keys_kernel,
        [shaped((slots, width), bf16)],
        pltpu.with_memory_space_constraint(memory, place), *after,
        work=64 * slots * width * width,
        grid=(slots // block,),
        in_specs=[spec] + [pl.BlockSpec(memory_space=pl.ANY)] * len(after),
        out_specs=[spec],
    )[0]


def join_kernel(blocks, *refs):
    block_refs, out_ref = refs[:blocks], refs[-1]
    first = 0
    for ref in block_refs:
        out_ref[first : first + ref.shape[0], :] = ref[...]
        first += ref.shape[0]


def join(blocks, after):
    rows = sum(block.shape[0] for block in blocks)
    return call(
        functools.partial(join_kernel, len(blocks)),
        [shaped((rows, blocks[0].shape[1]), blocks[0].dtype)],
        *blocks, *after,
        in_specs=[pl.BlockSpec(memory_space=pltpu.VMEM)] * len(blocks)
        + [pl.BlockSpec(memory_space=pl.ANY)] * len(after),
    )[0]


def positions(step, count, slots, groups, line, cores):
    first = lax.rem(step, slots // count) * count
    crossing = lax.rem(step, cores)
    members = line * cores
    devices_all = groups * members
    grp = lax.axis_index("grp")
    dev = lax.axis_index("dev")
    target = grp * members + (dev ^ crossing)
    source = lax.rem(target + devices_all - lax.rem(step, devices_all), devices_all)
    source_grp = lax.div(source, members)
    source_line = lax.div(lax.rem(source, members), cores)
    step = lax.div(dev, cores) ^ source_line
    return first, crossing, grp ^ source_grp, lax.rem(line - step, line)


def pick_kernel(groups, sizes, step_ref, *refs):
    blocks_refs, out_ref = refs[:groups], refs[-1]
    rows = out_ref.shape[0]
    _, _, grp_place, line_place = positions(step_ref[0], *sizes)
    for place, ref in enumerate(blocks_refs):

        @pl.when(grp_place == place)
        def _():
            out_ref[...] = ref[pl.ds(pl.multiple_of(line_place * rows, 16), rows), :]


def pick(blocks, step, sizes, after):
    line = sizes[3]
    return call(
        functools.partial(pick_kernel, len(blocks), sizes),
        [shaped((blocks[0].shape[0] // line, lanes), bf16)],
        step, *blocks, *after,
        in_specs=[pl.BlockSpec(memory_space=pltpu.SMEM)]
        + [pl.BlockSpec(memory_space=pltpu.VMEM)] * len(blocks)
        + [pl.BlockSpec(memory_space=pl.ANY)] * len(after),
    )[0]


def patch_kernel(choices, sizes, step_ref, stored_ref, labels_ref, *refs):
    moved_refs, (memory_ref, new_labels_ref, rows_ref, sem) = refs[:choices], refs[choices:]
    count, width = rows_ref.shape
    first, crossing, _, _ = positions(step_ref[0], *sizes)
    moved = moved_refs[0][...]
    for choice in range(1, choices):
        moved = jnp.where(crossing == choice, moved_refs[choice][...], moved)
    for at in range(blocks_of(width)):
        rows_ref[:, at * lanes : (at + 1) * lanes] = moved[at * count : (at + 1) * count, :]
    target = memory_ref.at[pl.ds(pl.multiple_of(first, count), count), :]
    copy = pltpu.make_async_copy(rows_ref, target, sem)
    copy.start()
    digits = moved[blocks_of(width) * count :, :].astype(f32)
    row = (digits[0:1, :] * 256.0 + digits[1:2, :]).astype(jnp.int32)
    old = labels_ref[...]
    turned = pltpu.roll(jnp.broadcast_to(row, old.shape), lax.rem(first, lanes), 1)
    slot = lax.broadcasted_iota(jnp.int32, old.shape, 0) * lanes + lax.broadcasted_iota(jnp.int32, old.shape, 1)
    new_labels_ref[...] = jnp.where((slot >= first) & (slot < first + count), turned, old)
    copy.wait()


def patch(stored, labels, choices, step, sizes):
    count, width = sizes[0], stored.shape[1]
    return call(
        functools.partial(patch_kernel, len(choices), sizes),
        [shaped(stored.shape, bf16), shaped(labels.shape, jnp.int32)],
        step, stored, labels, *choices,
        in_specs=[pl.BlockSpec(memory_space=pltpu.SMEM), pl.BlockSpec(memory_space=pl.ANY)]
        + [pl.BlockSpec(memory_space=pltpu.VMEM)] * (1 + len(choices)),
        out_specs=[pl.BlockSpec(memory_space=pl.ANY), pl.BlockSpec(memory_space=pltpu.VMEM)],
        scratch_shapes=[pltpu.VMEM((count, width), bf16), pltpu.SemaphoreType.DMA],
        input_output_aliases={1: 0},
    )


def split_digits(row):
    high = row.astype(bf16).astype(f32)
    return [high, row - high]


def sum_rows(size):
    return rounded_up(8 * (rounded_up(size, lanes) // lanes), 16)


def block_kernel(blocks, sides, unit, count, copies, scratch, *refs):
    if copies:
        source_ref, target_ref, sem = refs[blocks + 2 * sides], refs[-scratch - 1], refs[-1]
        copy = pltpu.make_async_copy(source_ref, target_ref, sem)
        copy.start()
        refs = refs[: -scratch - 1] + refs[-scratch : -1]
        scratch -= 1
    rows_refs, keys_refs = refs[:blocks], refs[blocks : blocks + sides]
    label_refs = refs[blocks + sides : blocks + 2 * sides]
    out_refs = refs[-scratch - blocks : -scratch]
    anchors_ref, labels_ref, total_ref, pos_ref, neg_ref = refs[-scratch:-4]
    scores_refs, weight_refs = refs[-4:-2], refs[-2:]
    slots, width = keys_refs[0].shape
    parts = blocks_of(width)
    packed = rows_refs[0].shape[0]
    members = packed // (parts * count + 16)
    size = members * count
    columns = []
    for block, ref in enumerate(rows_refs):
        for member in range(members):
            first = member * (parts * count + 16)
            to = block * size + member * count
            for at in range(parts):
                anchors_ref[to : to + count, at * lanes : (at + 1) * lanes] = ref[
                    first + at * count : first + (at + 1) * count, :
                ]
            digits = ref[first + parts * count : first + parts * count + 16, :].astype(f32)
            columns.append(to_column((digits[0:1, :] * 256.0 + digits[1:2, :])[:, :count]))
    rows = blocks * size
    labels_ref[...] = jnp.broadcast_to(jnp.concatenate(columns, axis=0), labels_ref.shape)
    pos_ref[...] = jnp.zeros_like(pos_ref)
    neg_ref[...] = jnp.zeros_like(neg_ref)
    anchors = anchors_ref[...]
    units = [(side, at) for side in range(sides) for at in range(0, slots, unit)]
    quarter = rows // 4

    def score_unit(at):
        side, first = units[at]
        scores_refs[at % 2][...] = lax.dot_general(
            anchors, keys_refs[side][first : first + unit, :], (((1,), (1,)), ((), ())), preferred_element_type=f32
        )

    def term_unit(at, which):
        side, first = units[at]
        part = slice(which * quarter, (which + 1) * quarter)
        weights_ref = weight_refs[at // 2 % 2]
        wanted = labels_ref[part, :]
        pos_sum, neg_sum = pos_ref[part, :], neg_ref[part, :]
        for piece in range(0, unit, lanes):
            slot_labels = label_refs[side][:, first + piece : first + piece + lanes].astype(f32)
            neg_shift = jnp.where(slot_labels < 0.0, -1e30, -neg_scale * margin * log2e)
            same = wanted == slot_labels
            slope = jnp.where(same, -pos_scale * log2e, neg_scale * log2e)
            shift = jnp.where(same, pos_scale * margin * log2e, neg_shift)
            term = jnp.exp2(scores_refs[at % 2][part, piece : piece + lanes] * slope + shift)
            pos = jnp.where(same, term, 0.0)
            neg = jnp.where(same, 0.0, term)
            pos_sum += pos
            neg_sum += neg
            to = slice(at % 2 * unit + piece, at % 2 * unit + piece + lanes)
            weights_ref[part, to] = neg.astype(bf16)
            weights_ref[rows + which * quarter : rows + (which + 1) * quarter, to] = pos.astype(bf16)
        pos_ref[part, :] = pos_sum
        neg_ref[part, :] = neg_sum

    def weigh_half(pair, half):
        side, first = units[2 * pair]
        part = slice(half * (width // 2), (half + 1) * (width // 2))
        more = jnp.dot(
            weight_refs[pair % 2][...], keys_refs[side][first : first + 2 * unit, part], preferred_element_type=f32
        )
        total_ref[:, part] = more if pair == 0 else total_ref[:, part] + more

    score_unit(0)
    for at in range(len(units)):
        term_unit(at, 0)
        if at + 1 < len(units):
            score_unit(at + 1)
        term_unit(at, 1)
        term_unit(at, 2)
        if at >= 2:
            weigh_half(at // 2 - 1, at % 2)
        term_unit(at, 3)
    weigh_half(len(units) // 2 - 1, 0)
    weigh_half(len(units) // 2 - 1, 1)
    total = total_ref[...]
    pos_sum = jnp.sum(pos_ref[...], axis=1, keepdims=True)
    neg_sum = jnp.sum(neg_ref[...], axis=1, keepdims=True)
    floats = anchors.astype(f32)
    sums = [pos_sum, neg_sum]
    for which in range(2):
        value = total[which * rows : (which + 1) * rows, :]
        along = jnp.sum(value * floats, axis=1, keepdims=True)
        sums.append(along)
        rest = value - along * floats
        for block, ref in enumerate(out_refs):
            for at in range(parts):
                first = (which * parts + at) * size
                ref[first : first + size, :] = rest[
                    block * size : (block + 1) * size, at * lanes : (at + 1) * lanes
                ].astype(ref.dtype)
    for block, ref in enumerate(out_refs):
        lines = []
        for first in range(0, size, lanes):
            last = min(first + lanes, size)
            for value in sums:
                row = to_row(value[block * size + first : block * size + last])
                if last - first < lanes:
                    row = jnp.concatenate([row, jnp.zeros((1, lanes - last + first), f32)], axis=1)
                lines += split_digits(row)
        first = 2 * parts * size
        ref[first:, :] = rows_as_lanes(lines, ref.shape[0] - first).astype(ref.dtype)
    if copies:
        copy.wait()


def block_sums(blocks, keys, labels, count, dtype, after, copied=()):
    slots, width = keys[0].shape
    parts = blocks_of(width)
    size = blocks[0].shape[0] // (parts * count + 16) * count
    rows = len(blocks) * size
    unit = math.gcd(256, slots // 2)
    anywhere = pl.BlockSpec(memory_space=pl.ANY)
    vmem = pl.BlockSpec(memory_space=pltpu.VMEM)
    return call(
        functools.partial(block_kernel, len(blocks), len(keys), unit, count, len(copied), 9 + len(copied)),
        [shaped((2 * parts * size + sum_rows(size), lanes), dtype)] * len(blocks)
        + [shaped(value.shape, value.dtype) for value in copied],
        *blocks, *[in_vmem(k) for k in keys], *labels, *copied, *after,
        work=12 * size * len(blocks) * slots * len(keys) * width,
        in_specs=[vmem] * (len(blocks) + 2 * len(keys)) + [anywhere] * (len(copied) + len(after)),
        out_specs=[vmem] * len(blocks) + [anywhere] * len(copied),
        scratch_shapes=[
            pltpu.VMEM((rows, width), bf16),
            pltpu.VMEM((rows, lanes), f32),
            pltpu.VMEM((2 * rows, width), f32),
            pltpu.VMEM((rows, lanes), f32),
            pltpu.VMEM((rows, lanes), f32),
            pltpu.VMEM((rows, unit), f32),
            pltpu.VMEM((rows, unit), f32),
            pltpu.VMEM((2 * rows, 2 * unit), bf16),
            pltpu.VMEM((2 * rows, 2 * unit), bf16),
        ]
        + [pltpu.SemaphoreType.DMA] * len(copied),
    )


def add_kernel(arrived, size, count, *refs):
    in_refs, out_refs = refs[: 1 + arrived], refs[-(size // count) :]
    columns = (in_refs[0].shape[0] - sum_rows(size)) // size

    def total(first, rows):
        value = in_refs[0][first : first + rows, :]
        for ref in in_refs[1:]:
            value = value + ref[first : first + rows, :].astype(f32)
        return value

    sums = total(columns * size, sum_rows(size))
    for block, ref in enumerate(out_refs):
        for at in range(columns):
            part = total(at * size + block * count, count)
            ref[at * count : (at + 1) * count, :] = part.astype(ref.dtype)
        group, lane = divmod(block * count, lanes)
        lines = []
        for which in range(4):
            row = 8 * group + 2 * which
            lines += split_digits(sums[row : row + 1, :] + sums[row + 1 : row + 2, :])
        packed = rows_as_lanes(lines, ref.shape[0] - columns * count)
        if lane:
            packed = pltpu.roll(packed, lanes - lane, 1)
        ref[columns * count :, :] = packed.astype(ref.dtype)


def add(held, arrived, size, count, columns, after):
    shape = (columns * count + sum_rows(count), lanes)
    outs = [shaped(shape, f32 if b == 0 else bf16) for b in range(size // count)]
    return call(
        functools.partial(add_kernel, len(arrived), size, count),
        outs,
        held, *arrived, *after,
        in_specs=[pl.BlockSpec(memory_space=pltpu.VMEM)] * (1 + len(arrived))
        + [pl.BlockSpec(memory_space=pl.ANY)] * len(after),
    )


def finish_kernel(arrived, *refs):
    held_ref, arrived_refs = refs[0], refs[1 : 1 + arrived]
    unit_ref, radius_ref, grad_ref, loss_ref = refs[1 + arrived :]
    count, width = unit_ref.shape
    parts = blocks_of(width)
    total = held_ref[...]
    for ref in arrived_refs:
        total = total + ref[...].astype(f32)
    sums = []
    for which in range(4):
        row = 2 * parts * count + 2 * which
        sums.append((total[row : row + 1, :] + total[row + 1 : row + 2, :])[:, :count])
    pos, neg = sums[:2]
    loss_ref[...] = jnp.log(1.0 + pos) / pos_scale + jnp.log(1.0 + neg) / neg_scale
    scales = [to_column(1.0 / (1.0 + row)) for row in (neg, pos)]
    alongs = [to_column(row) for row in sums[2:]]
    unit = unit_ref[...]
    anchors = unit.astype(bf16).astype(f32)
    push, pull = [
        jnp.concatenate([total[(first + at) * count : (first + at + 1) * count, :] for at in range(parts)], axis=1)
        for first in (0, parts)
    ]
    grad_unit = (push + alongs[0] * anchors) * scales[0] - (pull + alongs[1] * anchors) * scales[1]
    along = jnp.sum(unit * grad_unit, axis=1, keepdims=True)
    grad_ref[...] = (grad_unit - unit * along) / radius_ref[:, :1]


def per_device(batch_rows, batch_labels, memory, memory_labels, keep_bits, step_index):
    groups = lax.axis_size("grp")
    members = lax.axis_size("dev")
    cores = 2 if members % 2 == 0 else 1
    line = members // cores
    count, width = batch_rows.shape
    slots = memory.shape[0]

    def exchange(value, axis, step):
        if axis == "grp":
            return lax.ppermute(value, "grp", [(i, i ^ step) for i in range(groups)])
        jump = step * cores if axis == "line" else step
        return lax.ppermute(value, "dev", [(i, i ^ jump) for i in range(members)])

    folded = (slots // lanes, lanes)
    parts = blocks_of(width)
    packed, unit, radius, slot_labels, copied_labels = call(
        prepare_kernel,
        [
            pltpu.VMEM((parts * count + 16, lanes), bf16),
            pltpu.VMEM((count, width), f32),
            pltpu.VMEM((count, lanes), f32),
            pltpu.VMEM(folded, jnp.int32),
            pltpu.VMEM(folded, jnp.int32),
        ],
        batch_rows, batch_labels.reshape(1, count), memory_labels.reshape(folded), keep_bits.reshape(folded),
        limit=vmem_most,
    )

    labels = [slot_labels] + [exchange(slot_labels, "core", s) for s in range(1, cores)]
    memories = [memory] + [exchange(memory, "core", s) for s in range(1, cores)]

    part = packed
    for s in range(line - 1, 0, -1):
        part = join([part, exchange(packed, "line", s)], labels if s == 1 else [])
    labels = [value.reshape(1, slots) for value in labels]
    blocks = [part] + [None] * (groups - 1)
    for s in range(groups - 1, 0, -1):
        blocks[s] = exchange(part, "grp", s)
    keys = [keys_of(memory, pltpu.HBM, [part])] + [keys_of(value, pltpu.VMEM, [part]) for value in memories[1:]]

    size = count * line
    arrived, after = [], []
    places = list(range(groups - 1, 0, -1))
    while places:
        now = places[:1] if not after else places[:2]
        places = places[len(now) :]
        after = block_sums([blocks[s] for s in now], keys, labels, count, bf16, after)
        arrived += [exchange(value, "grp", s) for s, value in zip(now, after)]
    held, copied = block_sums([part], keys, labels, count, f32, after, [memory])
    sizes = (count, slots, groups, line, cores)
    moved = pick(blocks, step_index, sizes, after)
    choices = [moved] + [exchange(moved, "core", s) for s in range(1, cores)]

    sums, *others = add(held, arrived, size, count, 2 * parts, choices)
    order = sorted(range(1, line), key=lambda step: (step != line // 2, -step))
    arrived = [exchange(others[line - 1 - step], "line", step) for step in order]
    grad_batch, loss = call(
        functools.partial(finish_kernel, len(arrived)),
        [shaped((count, width), f32), shaped((1, count), f32)],
        sums, *arrived, unit, radius,
    )

    new_memory, new_labels = patch(copied, copied_labels, choices, step_index, sizes)
    return (grad_batch, loss.reshape(count), new_memory, new_labels.reshape(slots))


def solution(mesh):
    placed = (
        P(("grp", "dev"), None),
        P(("grp", "dev")),
        P(("grp", "dev"), None),
        P(("grp", "dev")),
        P(("grp", "dev")),
        P(),
    )
    return jax.shard_map(
        per_device,
        mesh=mesh,
        in_specs=placed,
        out_specs=(
            P(("grp", "dev"), None),
            P(("grp", "dev")),
            P(("grp", "dev"), None),
            P(("grp", "dev")),
        ),
        check_vma=False,
    )
```

```python
import functools
import math

import jax
import jax.numpy as jnp
from jax import lax
from jax.experimental import pallas as pl
from jax.experimental.pallas import tpu as pltpu
from jax.sharding import PartitionSpec as P

pos_scale = 2.0
neg_scale = 50.0
margin = 0.5
lanes = 128
log2e = math.log2(math.e)
vmem_bytes = 20 * 1024 * 1024
vmem_most = 56 * 1024 * 1024
f32 = jnp.float32
bf16 = jnp.bfloat16


def call(body, outs, *args, work=0, limit=vmem_bytes, **kw):
    return pl.pallas_call(
        body,
        out_shape=outs,
        compiler_params=pltpu.CompilerParams(vmem_limit_bytes=limit),
        cost_estimate=pl.CostEstimate(flops=work, bytes_accessed=0, transcendentals=0),
        **kw,
    )(*args)


def shaped(shape, dtype):
    return jax.ShapeDtypeStruct(shape, dtype)


def in_vmem(value):
    return pltpu.with_memory_space_constraint(value, pltpu.VMEM)


def rounded_up(value, unit):
    return (value + unit - 1) // unit * unit


def blocks_of(width):
    return width // lanes


def rows_as_lanes(parts, rows):
    row = lax.broadcasted_iota(jnp.int32, (rows, lanes), 0)
    out = jnp.zeros((rows, lanes), f32)
    for at, part in enumerate(parts):
        out = jnp.where(row == at, part, out)
    return out


def prepare_kernel(rows_ref, labels_ref, stored_ref, keep_ref, packed_ref, unit_ref, radius_ref, slot_ref, copy_ref):
    stored = stored_ref[...]
    slot_ref[...] = jnp.where(keep_ref[...] > 0, stored, -1)
    copy_ref[...] = stored
    rows = rows_ref[...].astype(f32)
    count, width = rows.shape
    radius = jnp.sqrt(jnp.sum(rows * rows, axis=1, keepdims=True) + 1e-06)
    unit = rows / radius
    unit_ref[...] = unit
    radius_ref[...] = jnp.broadcast_to(radius, radius_ref.shape)
    anchors = unit.astype(bf16)
    for at in range(blocks_of(width)):
        packed_ref[at * count : (at + 1) * count, :] = anchors[:, at * lanes : (at + 1) * lanes]
    row = jnp.concatenate([labels_ref[...].astype(f32), jnp.zeros((1, lanes - count), f32)], axis=1)
    high = jnp.floor(row * (1.0 / 256.0))
    tail = packed_ref.shape[0] - blocks_of(width) * count
    packed_ref[blocks_of(width) * count :, :] = rows_as_lanes([high, row - high * 256.0], tail).astype(bf16)


def diagonal(count):
    across = lax.broadcasted_iota(jnp.int32, (count, count), 1)
    down = lax.broadcasted_iota(jnp.int32, (count, count), 0)
    return across == down


def to_column(row):
    count = row.shape[1]
    spread = jnp.broadcast_to(row, (count, count))
    return jnp.sum(jnp.where(diagonal(count), spread, 0.0), axis=1, keepdims=True)


def to_row(column):
    count = column.shape[0]
    spread = jnp.broadcast_to(column, (count, count))
    return jnp.sum(jnp.where(diagonal(count), spread, 0.0), axis=0, keepdims=True)


def keys_kernel(memory_ref, *refs):
    keys_ref = refs[-1]
    rows = memory_ref[...].astype(f32)
    radius = jnp.sqrt(jnp.sum(rows * rows, axis=1, keepdims=True) + 1e-06)
    keys_ref[...] = (rows / radius).astype(bf16)


def keys_of(memory, place, after):
    slots, width = memory.shape
    block = math.gcd(512, slots)
    spec = pl.BlockSpec((block, width), lambda i: (i, 0))
    return call(
        keys_kernel,
        [shaped((slots, width), bf16)],
        pltpu.with_memory_space_constraint(memory, place), *after,
        work=64 * slots * width * width,
        grid=(slots // block,),
        in_specs=[spec] + [pl.BlockSpec(memory_space=pl.ANY)] * len(after),
        out_specs=[spec],
    )[0]


def join_kernel(blocks, *refs):
    block_refs, out_ref = refs[:blocks], refs[-1]
    first = 0
    for ref in block_refs:
        out_ref[first : first + ref.shape[0], :] = ref[...]
        first += ref.shape[0]


def join(blocks, after):
    rows = sum(block.shape[0] for block in blocks)
    return call(
        functools.partial(join_kernel, len(blocks)),
        [shaped((rows, blocks[0].shape[1]), blocks[0].dtype)],
        *blocks, *after,
        in_specs=[pl.BlockSpec(memory_space=pltpu.VMEM)] * len(blocks)
        + [pl.BlockSpec(memory_space=pl.ANY)] * len(after),
    )[0]


def positions(step, count, slots, groups, line, cores):
    first = lax.rem(step, slots // count) * count
    crossing = lax.rem(step, cores)
    members = line * cores
    devices_all = groups * members
    grp = lax.axis_index("grp")
    dev = lax.axis_index("dev")
    target = grp * members + (dev ^ crossing)
    source = lax.rem(target + devices_all - lax.rem(step, devices_all), devices_all)
    source_grp = lax.div(source, members)
    source_line = lax.div(lax.rem(source, members), cores)
    step = lax.div(dev, cores) ^ source_line
    return first, crossing, grp ^ source_grp, lax.rem(line - step, line)


def pick_kernel(groups, sizes, step_ref, *refs):
    blocks_refs, out_ref = refs[:groups], refs[-1]
    rows = out_ref.shape[0]
    _, _, grp_place, line_place = positions(step_ref[0], *sizes)
    for place, ref in enumerate(blocks_refs):

        @pl.when(grp_place == place)
        def _():
            out_ref[...] = ref[pl.ds(pl.multiple_of(line_place * rows, 16), rows), :]


def pick(blocks, step, sizes, after):
    line = sizes[3]
    return call(
        functools.partial(pick_kernel, len(blocks), sizes),
        [shaped((blocks[0].shape[0] // line, lanes), bf16)],
        step, *blocks, *after,
        in_specs=[pl.BlockSpec(memory_space=pltpu.SMEM)]
        + [pl.BlockSpec(memory_space=pltpu.VMEM)] * len(blocks)
        + [pl.BlockSpec(memory_space=pl.ANY)] * len(after),
    )[0]


def patch_kernel(choices, sizes, step_ref, stored_ref, labels_ref, *refs):
    moved_refs, (memory_ref, new_labels_ref, rows_ref, sem) = refs[:choices], refs[choices:]
    count, width = rows_ref.shape
    first, crossing, _, _ = positions(step_ref[0], *sizes)
    moved = moved_refs[0][...]
    for choice in range(1, choices):
        moved = jnp.where(crossing == choice, moved_refs[choice][...], moved)
    for at in range(blocks_of(width)):
        rows_ref[:, at * lanes : (at + 1) * lanes] = moved[at * count : (at + 1) * count, :]
    target = memory_ref.at[pl.ds(pl.multiple_of(first, count), count), :]
    copy = pltpu.make_async_copy(rows_ref, target, sem)
    copy.start()
    digits = moved[blocks_of(width) * count :, :].astype(f32)
    row = (digits[0:1, :] * 256.0 + digits[1:2, :]).astype(jnp.int32)
    old = labels_ref[...]
    turned = pltpu.roll(jnp.broadcast_to(row, old.shape), lax.rem(first, lanes), 1)
    slot = lax.broadcasted_iota(jnp.int32, old.shape, 0) * lanes + lax.broadcasted_iota(jnp.int32, old.shape, 1)
    new_labels_ref[...] = jnp.where((slot >= first) & (slot < first + count), turned, old)
    copy.wait()


def patch(stored, labels, choices, step, sizes):
    count, width = sizes[0], stored.shape[1]
    return call(
        functools.partial(patch_kernel, len(choices), sizes),
        [shaped(stored.shape, bf16), shaped(labels.shape, jnp.int32)],
        step, stored, labels, *choices,
        in_specs=[pl.BlockSpec(memory_space=pltpu.SMEM), pl.BlockSpec(memory_space=pl.ANY)]
        + [pl.BlockSpec(memory_space=pltpu.VMEM)] * (1 + len(choices)),
        out_specs=[pl.BlockSpec(memory_space=pl.ANY), pl.BlockSpec(memory_space=pltpu.VMEM)],
        scratch_shapes=[pltpu.VMEM((count, width), bf16), pltpu.SemaphoreType.DMA],
        input_output_aliases={1: 0},
    )


def split_digits(row):
    high = row.astype(bf16).astype(f32)
    return [high, row - high]


def sum_rows(size):
    return rounded_up(8 * (rounded_up(size, lanes) // lanes), 16)


def block_kernel(blocks, sides, unit, count, copies, scratch, *refs):
    if copies:
        source_ref, target_ref, sem = refs[blocks + 2 * sides], refs[-scratch - 1], refs[-1]
        copy = pltpu.make_async_copy(source_ref, target_ref, sem)
        copy.start()
        refs = refs[: -scratch - 1] + refs[-scratch : -1]
        scratch -= 1
    rows_refs, keys_refs = refs[:blocks], refs[blocks : blocks + sides]
    label_refs = refs[blocks + sides : blocks + 2 * sides]
    out_refs = refs[-scratch - blocks : -scratch]
    anchors_ref, labels_ref, total_ref, *sum_refs = refs[-scratch:-4]
    scores_refs, weight_refs = refs[-4:-2], refs[-2:]
    slots, width = keys_refs[0].shape
    parts = blocks_of(width)
    packed = rows_refs[0].shape[0]
    members = packed // (parts * count + 16)
    size = members * count
    columns = []
    for block, ref in enumerate(rows_refs):
        for member in range(members):
            first = member * (parts * count + 16)
            to = block * size + member * count
            for at in range(parts):
                anchors_ref[to : to + count, at * lanes : (at + 1) * lanes] = ref[
                    first + at * count : first + (at + 1) * count, :
                ]
            digits = ref[first + parts * count : first + parts * count + 16, :].astype(f32)
            columns.append(to_column((digits[0:1, :] * 256.0 + digits[1:2, :])[:, :count]))
    rows = blocks * size
    labels_ref[...] = jnp.broadcast_to(jnp.concatenate(columns, axis=0), labels_ref.shape)
    for ref in sum_refs:
        ref[...] = jnp.zeros_like(ref)
    anchors = anchors_ref[...]
    units = [(side, at) for side in range(sides) for at in range(0, slots, unit)]
    quarter = rows // 4

    def score_unit(at):
        side, first = units[at]
        scores_refs[at % 2][...] = lax.dot_general(
            anchors, keys_refs[side][first : first + unit, :], (((1,), (1,)), ((), ())), preferred_element_type=f32
        )

    def term_unit(at, which):
        side, first = units[at]
        part = slice(which * quarter, (which + 1) * quarter)
        weights_ref = weight_refs[at // 2 % 2]
        wanted = labels_ref[part, :]
        pos_sum, neg_sum, push_along, pull_along = [ref[part, :] for ref in sum_refs]
        for piece in range(0, unit, lanes):
            slot_labels = label_refs[side][:, first + piece : first + piece + lanes].astype(f32)
            neg_shift = jnp.where(slot_labels < 0.0, -1e30, -neg_scale * margin * log2e)
            same = wanted == slot_labels
            slope = jnp.where(same, -pos_scale * log2e, neg_scale * log2e)
            shift = jnp.where(same, pos_scale * margin * log2e, neg_shift)
            scores = scores_refs[at % 2][part, piece : piece + lanes]
            term = jnp.exp2(scores * slope + shift)
            pos = jnp.where(same, term, 0.0)
            neg = jnp.where(same, 0.0, term)
            pos_sum += pos
            neg_sum += neg
            push_along += neg * scores
            pull_along += pos * scores
            to = slice(at % 2 * unit + piece, at % 2 * unit + piece + lanes)
            weights_ref[part, to] = neg.astype(bf16)
            weights_ref[rows + which * quarter : rows + (which + 1) * quarter, to] = pos.astype(bf16)
        for ref, value in zip(sum_refs, (pos_sum, neg_sum, push_along, pull_along)):
            ref[part, :] = value

    def weigh_half(pair, half):
        side, first = units[2 * pair]
        part = slice(half * (width // 2), (half + 1) * (width // 2))
        more = jnp.dot(
            weight_refs[pair % 2][...], keys_refs[side][first : first + 2 * unit, part], preferred_element_type=f32
        )
        total_ref[:, part] = more if pair == 0 else total_ref[:, part] + more

    score_unit(0)
    for at in range(len(units)):
        term_unit(at, 0)
        if at + 1 < len(units):
            score_unit(at + 1)
        term_unit(at, 1)
        term_unit(at, 2)
        if at >= 2:
            weigh_half(at // 2 - 1, at % 2)
        term_unit(at, 3)
    sums = [jnp.sum(ref[...], axis=1, keepdims=True) for ref in sum_refs]
    floats = anchors.astype(f32)
    for half in range(2):
        weigh_half(len(units) // 2 - 1, half)
        for which in range(2):
            for at in range(half * parts // 2, (half + 1) * parts // 2):
                columns = slice(at * lanes, (at + 1) * lanes)
                rest = total_ref[which * rows : (which + 1) * rows, columns] - sums[2 + which] * floats[:, columns]
                first = (which * parts + at) * size
                for block, ref in enumerate(out_refs):
                    ref[first : first + size, :] = rest[block * size : (block + 1) * size, :].astype(ref.dtype)
    for block, ref in enumerate(out_refs):
        lines = []
        for first in range(0, size, lanes):
            last = min(first + lanes, size)
            for value in sums:
                row = to_row(value[block * size + first : block * size + last])
                if last - first < lanes:
                    row = jnp.concatenate([row, jnp.zeros((1, lanes - last + first), f32)], axis=1)
                lines += split_digits(row)
        first = 2 * parts * size
        ref[first:, :] = rows_as_lanes(lines, ref.shape[0] - first).astype(ref.dtype)
    if copies:
        copy.wait()


def block_sums(blocks, keys, labels, count, dtype, after, copied=()):
    slots, width = keys[0].shape
    parts = blocks_of(width)
    size = blocks[0].shape[0] // (parts * count + 16) * count
    rows = len(blocks) * size
    unit = math.gcd(256, slots // 2)
    anywhere = pl.BlockSpec(memory_space=pl.ANY)
    vmem = pl.BlockSpec(memory_space=pltpu.VMEM)
    return call(
        functools.partial(block_kernel, len(blocks), len(keys), unit, count, len(copied), 11 + len(copied)),
        [shaped((2 * parts * size + sum_rows(size), lanes), dtype)] * len(blocks)
        + [shaped(value.shape, value.dtype) for value in copied],
        *blocks, *[in_vmem(k) for k in keys], *labels, *copied, *after,
        work=12 * size * len(blocks) * slots * len(keys) * width,
        in_specs=[vmem] * (len(blocks) + 2 * len(keys)) + [anywhere] * (len(copied) + len(after)),
        out_specs=[vmem] * len(blocks) + [anywhere] * len(copied),
        scratch_shapes=[
            pltpu.VMEM((rows, width), bf16),
            pltpu.VMEM((rows, lanes), f32),
            pltpu.VMEM((2 * rows, width), f32),
            pltpu.VMEM((rows, lanes), f32),
            pltpu.VMEM((rows, lanes), f32),
            pltpu.VMEM((rows, lanes), f32),
            pltpu.VMEM((rows, lanes), f32),
            pltpu.VMEM((rows, unit), f32),
            pltpu.VMEM((rows, unit), f32),
            pltpu.VMEM((2 * rows, 2 * unit), bf16),
            pltpu.VMEM((2 * rows, 2 * unit), bf16),
        ]
        + [pltpu.SemaphoreType.DMA] * len(copied),
    )


def add_kernel(arrived, size, count, *refs):
    in_refs, out_refs = refs[: 1 + arrived], refs[-(size // count) :]
    columns = (in_refs[0].shape[0] - sum_rows(size)) // size

    def total(first, rows):
        value = in_refs[0][first : first + rows, :]
        for ref in in_refs[1:]:
            value = value + ref[first : first + rows, :].astype(f32)
        return value

    sums = total(columns * size, sum_rows(size))
    for block, ref in enumerate(out_refs):
        for at in range(columns):
            part = total(at * size + block * count, count)
            ref[at * count : (at + 1) * count, :] = part.astype(ref.dtype)
        group, lane = divmod(block * count, lanes)
        lines = []
        for which in range(4):
            row = 8 * group + 2 * which
            lines += split_digits(sums[row : row + 1, :] + sums[row + 1 : row + 2, :])
        packed = rows_as_lanes(lines, ref.shape[0] - columns * count)
        if lane:
            packed = pltpu.roll(packed, lanes - lane, 1)
        ref[columns * count :, :] = packed.astype(ref.dtype)


def add(held, arrived, size, count, columns, after):
    shape = (columns * count + sum_rows(count), lanes)
    outs = [shaped(shape, f32 if b == 0 else bf16) for b in range(size // count)]
    return call(
        functools.partial(add_kernel, len(arrived), size, count),
        outs,
        held, *arrived, *after,
        in_specs=[pl.BlockSpec(memory_space=pltpu.VMEM)] * (1 + len(arrived))
        + [pl.BlockSpec(memory_space=pl.ANY)] * len(after),
    )


def finish_kernel(arrived, *refs):
    held_ref, arrived_refs = refs[0], refs[1 : 1 + arrived]
    unit_ref, radius_ref, grad_ref, loss_ref = refs[1 + arrived :]
    count, width = unit_ref.shape
    parts = blocks_of(width)
    total = held_ref[...]
    for ref in arrived_refs:
        total = total + ref[...].astype(f32)
    sums = []
    for which in range(4):
        row = 2 * parts * count + 2 * which
        sums.append((total[row : row + 1, :] + total[row + 1 : row + 2, :])[:, :count])
    pos, neg = sums[:2]
    loss_ref[...] = jnp.log(1.0 + pos) / pos_scale + jnp.log(1.0 + neg) / neg_scale
    scales = [to_column(1.0 / (1.0 + row)) for row in (neg, pos)]
    alongs = [to_column(row) for row in sums[2:]]
    unit = unit_ref[...]
    anchors = unit.astype(bf16).astype(f32)
    push, pull = [
        jnp.concatenate([total[(first + at) * count : (first + at + 1) * count, :] for at in range(parts)], axis=1)
        for first in (0, parts)
    ]
    grad_unit = (push + alongs[0] * anchors) * scales[0] - (pull + alongs[1] * anchors) * scales[1]
    along = jnp.sum(unit * grad_unit, axis=1, keepdims=True)
    grad_ref[...] = (grad_unit - unit * along) / radius_ref[:, :1]


def per_device(batch_rows, batch_labels, memory, memory_labels, keep_bits, step_index):
    groups = lax.axis_size("grp")
    members = lax.axis_size("dev")
    cores = 2 if members % 2 == 0 else 1
    line = members // cores
    count, width = batch_rows.shape
    slots = memory.shape[0]

    def exchange(value, axis, step):
        if axis == "grp":
            return lax.ppermute(value, "grp", [(i, i ^ step) for i in range(groups)])
        jump = step * cores if axis == "line" else step
        return lax.ppermute(value, "dev", [(i, i ^ jump) for i in range(members)])

    folded = (slots // lanes, lanes)
    parts = blocks_of(width)
    packed, unit, radius, slot_labels, copied_labels = call(
        prepare_kernel,
        [
            pltpu.VMEM((parts * count + 16, lanes), bf16),
            pltpu.VMEM((count, width), f32),
            pltpu.VMEM((count, lanes), f32),
            pltpu.VMEM(folded, jnp.int32),
            pltpu.VMEM(folded, jnp.int32),
        ],
        batch_rows, batch_labels.reshape(1, count), memory_labels.reshape(folded), keep_bits.reshape(folded),
        limit=vmem_most,
    )

    labels = [slot_labels] + [exchange(slot_labels, "core", s) for s in range(1, cores)]
    memories = [memory] + [exchange(memory, "core", s) for s in range(1, cores)]

    part = packed
    for s in range(line - 1, 0, -1):
        part = join([part, exchange(packed, "line", s)], labels if s == 1 else [])
    labels = [value.reshape(1, slots) for value in labels]
    blocks = [part] + [None] * (groups - 1)
    for s in range(groups - 1, 0, -1):
        blocks[s] = exchange(part, "grp", s)
    keys = [keys_of(memory, pltpu.HBM, [part])] + [keys_of(value, pltpu.VMEM, [part]) for value in memories[1:]]

    size = count * line
    arrived, after = [], []
    places = list(range(groups - 1, 0, -1))
    while places:
        now = places[:1] if not after else places[:2]
        places = places[len(now) :]
        after = block_sums([blocks[s] for s in now], keys, labels, count, bf16, after)
        arrived += [exchange(value, "grp", s) for s, value in zip(now, after)]
    held, copied = block_sums([part], keys, labels, count, f32, after, [memory])
    sizes = (count, slots, groups, line, cores)
    moved = pick(blocks, step_index, sizes, after)
    choices = [moved] + [exchange(moved, "core", s) for s in range(1, cores)]

    sums, *others = add(held, arrived, size, count, 2 * parts, choices)
    arrived = [exchange(value, "line", line - at) for at, value in enumerate(others, 1)]
    grad_batch, loss = call(
        functools.partial(finish_kernel, len(arrived)),
        [shaped((count, width), f32), shaped((1, count), f32)],
        sums, *arrived, unit, radius,
    )

    new_memory, new_labels = patch(copied, copied_labels, choices, step_index, sizes)
    return (grad_batch, loss.reshape(count), new_memory, new_labels.reshape(slots))


def solution(mesh):
    placed = (
        P(("grp", "dev"), None),
        P(("grp", "dev")),
        P(("grp", "dev"), None),
        P(("grp", "dev")),
        P(("grp", "dev")),
        P(),
    )
    return jax.shard_map(
        per_device,
        mesh=mesh,
        in_specs=placed,
        out_specs=(
            P(("grp", "dev"), None),
            P(("grp", "dev")),
            P(("grp", "dev"), None),
            P(("grp", "dev")),
        ),
        check_vma=False,
    )
```

```python
import functools
import math

import jax
import jax.numpy as jnp
from jax import lax
from jax.experimental import pallas as pl
from jax.experimental.pallas import tpu as pltpu
from jax.sharding import PartitionSpec as P

pos_scale = 2.0
neg_scale = 50.0
margin = 0.5
lanes = 128
log2e = math.log2(math.e)
vmem_bytes = 20 * 1024 * 1024
vmem_most = 56 * 1024 * 1024
f32 = jnp.float32
bf16 = jnp.bfloat16


def call(body, outs, *args, work=0, limit=vmem_bytes, **kw):
    return pl.pallas_call(
        body,
        out_shape=outs,
        compiler_params=pltpu.CompilerParams(vmem_limit_bytes=limit),
        cost_estimate=pl.CostEstimate(flops=work, bytes_accessed=0, transcendentals=0),
        **kw,
    )(*args)


def shaped(shape, dtype):
    return jax.ShapeDtypeStruct(shape, dtype)


def in_vmem(value):
    return pltpu.with_memory_space_constraint(value, pltpu.VMEM)


def rounded_up(value, unit):
    return (value + unit - 1) // unit * unit


def blocks_of(width):
    return width // lanes


def rows_as_lanes(parts, rows):
    row = lax.broadcasted_iota(jnp.int32, (rows, lanes), 0)
    out = jnp.zeros((rows, lanes), f32)
    for at, part in enumerate(parts):
        out = jnp.where(row == at, part, out)
    return out


def prepare_kernel(rows_ref, labels_ref, stored_ref, keep_ref, packed_ref, unit_ref, radius_ref, slot_ref, copy_ref):
    stored = stored_ref[...]
    slot_ref[...] = jnp.where(keep_ref[...] > 0, stored, -1)
    copy_ref[...] = stored
    rows = rows_ref[...].astype(f32)
    count, width = rows.shape
    radius = jnp.sqrt(jnp.sum(rows * rows, axis=1, keepdims=True) + 1e-06)
    unit = rows / radius
    unit_ref[...] = unit
    radius_ref[...] = jnp.broadcast_to(radius, radius_ref.shape)
    anchors = unit.astype(bf16)
    for at in range(blocks_of(width)):
        packed_ref[at * count : (at + 1) * count, :] = anchors[:, at * lanes : (at + 1) * lanes]
    row = jnp.concatenate([labels_ref[...].astype(f32), jnp.zeros((1, lanes - count), f32)], axis=1)
    high = jnp.floor(row * (1.0 / 256.0))
    tail = packed_ref.shape[0] - blocks_of(width) * count
    packed_ref[blocks_of(width) * count :, :] = rows_as_lanes([high, row - high * 256.0], tail).astype(bf16)


def diagonal(count):
    across = lax.broadcasted_iota(jnp.int32, (count, count), 1)
    down = lax.broadcasted_iota(jnp.int32, (count, count), 0)
    return across == down


def to_column(row):
    count = row.shape[1]
    spread = jnp.broadcast_to(row, (count, count))
    return jnp.sum(jnp.where(diagonal(count), spread, 0.0), axis=1, keepdims=True)


def to_row(column):
    count = column.shape[0]
    spread = jnp.broadcast_to(column, (count, count))
    return jnp.sum(jnp.where(diagonal(count), spread, 0.0), axis=0, keepdims=True)


def keys_kernel(memory_ref, *refs):
    keys_ref = refs[-1]
    rows = memory_ref[...].astype(f32)
    radius = jnp.sqrt(jnp.sum(rows * rows, axis=1, keepdims=True) + 1e-06)
    keys_ref[...] = (rows / radius).astype(bf16)


def keys_of(memory, place, after):
    slots, width = memory.shape
    block = math.gcd(512, slots)
    spec = pl.BlockSpec((block, width), lambda i: (i, 0))
    return call(
        keys_kernel,
        [shaped((slots, width), bf16)],
        pltpu.with_memory_space_constraint(memory, place), *after,
        work=64 * slots * width * width,
        grid=(slots // block,),
        in_specs=[spec] + [pl.BlockSpec(memory_space=pl.ANY)] * len(after),
        out_specs=[spec],
    )[0]


def join_kernel(blocks, *refs):
    block_refs, out_ref = refs[:blocks], refs[-1]
    first = 0
    for ref in block_refs:
        out_ref[first : first + ref.shape[0], :] = ref[...]
        first += ref.shape[0]


def join(blocks, after):
    rows = sum(block.shape[0] for block in blocks)
    return call(
        functools.partial(join_kernel, len(blocks)),
        [shaped((rows, blocks[0].shape[1]), blocks[0].dtype)],
        *blocks, *after,
        in_specs=[pl.BlockSpec(memory_space=pltpu.VMEM)] * len(blocks)
        + [pl.BlockSpec(memory_space=pl.ANY)] * len(after),
    )[0]


def positions(step, count, slots, groups, line, cores):
    first = lax.rem(step, slots // count) * count
    crossing = lax.rem(step, cores)
    members = line * cores
    devices_all = groups * members
    grp = lax.axis_index("grp")
    dev = lax.axis_index("dev")
    target = grp * members + (dev ^ crossing)
    source = lax.rem(target + devices_all - lax.rem(step, devices_all), devices_all)
    source_grp = lax.div(source, members)
    source_line = lax.div(lax.rem(source, members), cores)
    step = lax.div(dev, cores) ^ source_line
    return first, crossing, grp ^ source_grp, lax.rem(line - step, line)


def pick_kernel(groups, sizes, step_ref, *refs):
    blocks_refs, out_ref = refs[:groups], refs[-1]
    rows = out_ref.shape[0]
    _, _, grp_place, line_place = positions(step_ref[0], *sizes)
    for place, ref in enumerate(blocks_refs):

        @pl.when(grp_place == place)
        def _():
            out_ref[...] = ref[pl.ds(pl.multiple_of(line_place * rows, 16), rows), :]


def pick(blocks, step, sizes, after):
    line = sizes[3]
    return call(
        functools.partial(pick_kernel, len(blocks), sizes),
        [shaped((blocks[0].shape[0] // line, lanes), bf16)],
        step, *blocks, *after,
        in_specs=[pl.BlockSpec(memory_space=pltpu.SMEM)]
        + [pl.BlockSpec(memory_space=pltpu.VMEM)] * len(blocks)
        + [pl.BlockSpec(memory_space=pl.ANY)] * len(after),
    )[0]


def patch_kernel(choices, sizes, step_ref, stored_ref, labels_ref, *refs):
    moved_refs, (memory_ref, new_labels_ref, rows_ref, sem) = refs[:choices], refs[choices:]
    count, width = rows_ref.shape
    first, crossing, _, _ = positions(step_ref[0], *sizes)
    moved = moved_refs[0][...]
    for choice in range(1, choices):
        moved = jnp.where(crossing == choice, moved_refs[choice][...], moved)
    for at in range(blocks_of(width)):
        rows_ref[:, at * lanes : (at + 1) * lanes] = moved[at * count : (at + 1) * count, :]
    target = memory_ref.at[pl.ds(pl.multiple_of(first, count), count), :]
    copy = pltpu.make_async_copy(rows_ref, target, sem)
    copy.start()
    digits = moved[blocks_of(width) * count :, :].astype(f32)
    row = (digits[0:1, :] * 256.0 + digits[1:2, :]).astype(jnp.int32)
    old = labels_ref[...]
    turned = pltpu.roll(jnp.broadcast_to(row, old.shape), lax.rem(first, lanes), 1)
    slot = lax.broadcasted_iota(jnp.int32, old.shape, 0) * lanes + lax.broadcasted_iota(jnp.int32, old.shape, 1)
    new_labels_ref[...] = jnp.where((slot >= first) & (slot < first + count), turned, old)
    copy.wait()


def patch(stored, labels, choices, step, sizes):
    count, width = sizes[0], stored.shape[1]
    return call(
        functools.partial(patch_kernel, len(choices), sizes),
        [shaped(stored.shape, bf16), shaped(labels.shape, jnp.int32)],
        step, stored, labels, *choices,
        in_specs=[pl.BlockSpec(memory_space=pltpu.SMEM), pl.BlockSpec(memory_space=pl.ANY)]
        + [pl.BlockSpec(memory_space=pltpu.VMEM)] * (1 + len(choices)),
        out_specs=[pl.BlockSpec(memory_space=pl.ANY), pl.BlockSpec(memory_space=pltpu.VMEM)],
        scratch_shapes=[pltpu.VMEM((count, width), bf16), pltpu.SemaphoreType.DMA],
        input_output_aliases={1: 0},
    )


def split_digits(row):
    high = row.astype(bf16).astype(f32)
    return [high, row - high]


def sum_rows(size):
    return rounded_up(8 * (rounded_up(size, lanes) // lanes), 16)


def block_kernel(blocks, sides, unit, count, copies, scratch, *refs):
    if copies:
        source_ref, target_ref, sem = refs[blocks + 2 * sides], refs[-scratch - 1], refs[-1]
        copy = pltpu.make_async_copy(source_ref, target_ref, sem)
        copy.start()
        refs = refs[: -scratch - 1] + refs[-scratch : -1]
        scratch -= 1
    rows_refs, keys_refs = refs[:blocks], refs[blocks : blocks + sides]
    label_refs = refs[blocks + sides : blocks + 2 * sides]
    out_refs = refs[-scratch - blocks : -scratch]
    anchors_ref, labels_ref, total_ref, pos_ref, neg_ref, wanted_ref, bias_ref = refs[-scratch:-4]
    scores_refs, weight_refs = refs[-4:-2], refs[-2:]
    slots, width = keys_refs[0].shape
    parts = blocks_of(width)
    packed = rows_refs[0].shape[0]
    members = packed // (parts * count + 16)
    size = members * count
    columns = []
    for block, ref in enumerate(rows_refs):
        for member in range(members):
            first = member * (parts * count + 16)
            to = block * size + member * count
            for at in range(parts):
                anchors_ref[to : to + count, at * lanes : (at + 1) * lanes] = ref[
                    first + at * count : first + (at + 1) * count, :
                ]
            digits = ref[first + parts * count : first + parts * count + 16, :].astype(f32)
            columns.append(to_column((digits[0:1, :] * 256.0 + digits[1:2, :])[:, :count]))
    rows = blocks * size
    labels_ref[...] = jnp.broadcast_to(jnp.concatenate(columns, axis=0), labels_ref.shape)
    pos_ref[...] = jnp.zeros_like(pos_ref)
    neg_ref[...] = jnp.zeros_like(neg_ref)
    anchors = anchors_ref[...]
    units = [(side, at) for side in range(sides) for at in range(0, slots, unit)]
    some = min(64, rows)
    for side in range(sides):
        slot_labels = label_refs[side][...].astype(f32)
        wanted_ref[side : side + 1, :] = slot_labels
        bias_ref[side : side + 1, :] = jnp.where(slot_labels < 0.0, -1e30, 0.0)

    def score_unit(at):
        side, first = units[at]
        scores_refs[at % 2][...] = lax.dot_general(
            anchors, keys_refs[side][first : first + unit, :], (((1,), (1,)), ((), ())), preferred_element_type=f32
        )

    def term_unit(at, which):
        side, first = units[at]
        part = slice(which * some, (which + 1) * some)
        weights_ref = weight_refs[at // 2 % 2]
        wanted = labels_ref[part, :]
        pos_sum, neg_sum = pos_ref[part, :], neg_ref[part, :]
        for piece in range(0, unit, lanes):
            columns = slice(first + piece, first + piece + lanes)
            same = wanted == wanted_ref[side : side + 1, columns]
            slope = jnp.where(same, -pos_scale * log2e, neg_scale * log2e)
            scores = scores_refs[at % 2][part, piece : piece + lanes]
            term = jnp.exp2(scores * slope + bias_ref[side : side + 1, columns])
            pos = jnp.where(same, term, 0.0)
            neg = jnp.where(same, 0.0, term)
            pos_sum += pos
            neg_sum += neg
            to = slice(at % 2 * unit + piece, at % 2 * unit + piece + lanes)
            weights_ref[part, to] = neg.astype(bf16)
            weights_ref[rows + which * some : rows + (which + 1) * some, to] = pos.astype(bf16)
        pos_ref[part, :] = pos_sum
        neg_ref[part, :] = neg_sum

    def weigh_half(pair, half):
        side, first = units[2 * pair]
        part = slice(half * (width // 2), (half + 1) * (width // 2))
        more = jnp.dot(
            weight_refs[pair % 2][...], keys_refs[side][first : first + 2 * unit, part], preferred_element_type=f32
        )
        total_ref[:, part] = more if pair == 0 else total_ref[:, part] + more

    score_unit(0)
    for at in range(len(units)):
        groups = rows // some
        for which in range(groups):
            term_unit(at, which)
            if which == 0 and at + 1 < len(units):
                score_unit(at + 1)
            if which == max(groups - 2, 0) and at >= 2:
                weigh_half(at // 2 - 1, at % 2)
    weigh_half(len(units) // 2 - 1, 0)
    weigh_half(len(units) // 2 - 1, 1)
    total = total_ref[...]
    pos_sum = jnp.sum(pos_ref[...], axis=1, keepdims=True)
    neg_sum = jnp.sum(neg_ref[...], axis=1, keepdims=True)
    floats = anchors.astype(f32)
    sums = [pos_sum, neg_sum]
    for which in range(2):
        value = total[which * rows : (which + 1) * rows, :]
        along = jnp.sum(value * floats, axis=1, keepdims=True)
        sums.append(along)
        rest = value - along * floats
        for block, ref in enumerate(out_refs):
            for at in range(parts):
                first = (which * parts + at) * size
                ref[first : first + size, :] = rest[
                    block * size : (block + 1) * size, at * lanes : (at + 1) * lanes
                ].astype(ref.dtype)
    for block, ref in enumerate(out_refs):
        lines = []
        for first in range(0, size, lanes):
            last = min(first + lanes, size)
            for value in sums:
                row = to_row(value[block * size + first : block * size + last])
                if last - first < lanes:
                    row = jnp.concatenate([row, jnp.zeros((1, lanes - last + first), f32)], axis=1)
                lines += split_digits(row)
        first = 2 * parts * size
        ref[first:, :] = rows_as_lanes(lines, ref.shape[0] - first).astype(ref.dtype)
    if copies:
        copy.wait()


def block_sums(blocks, keys, labels, count, dtype, after, copied=()):
    slots, width = keys[0].shape
    parts = blocks_of(width)
    size = blocks[0].shape[0] // (parts * count + 16) * count
    rows = len(blocks) * size
    unit = math.gcd(256, slots // 2)
    anywhere = pl.BlockSpec(memory_space=pl.ANY)
    vmem = pl.BlockSpec(memory_space=pltpu.VMEM)
    return call(
        functools.partial(block_kernel, len(blocks), len(keys), unit, count, len(copied), 11 + len(copied)),
        [shaped((2 * parts * size + sum_rows(size), lanes), dtype)] * len(blocks)
        + [shaped(value.shape, value.dtype) for value in copied],
        *blocks, *[in_vmem(k) for k in keys], *labels, *copied, *after,
        work=12 * size * len(blocks) * slots * len(keys) * width,
        in_specs=[vmem] * (len(blocks) + 2 * len(keys)) + [anywhere] * (len(copied) + len(after)),
        out_specs=[vmem] * len(blocks) + [anywhere] * len(copied),
        scratch_shapes=[
            pltpu.VMEM((rows, width), bf16),
            pltpu.VMEM((rows, lanes), f32),
            pltpu.VMEM((2 * rows, width), f32),
            pltpu.VMEM((rows, lanes), f32),
            pltpu.VMEM((rows, lanes), f32),
            pltpu.VMEM((len(keys), slots), f32),
            pltpu.VMEM((len(keys), slots), f32),
            pltpu.VMEM((rows, unit), f32),
            pltpu.VMEM((rows, unit), f32),
            pltpu.VMEM((2 * rows, 2 * unit), bf16),
            pltpu.VMEM((2 * rows, 2 * unit), bf16),
        ]
        + [pltpu.SemaphoreType.DMA] * len(copied),
    )


def add_kernel(arrived, size, count, *refs):
    in_refs, out_refs = refs[: 1 + arrived], refs[-(size // count) :]
    columns = (in_refs[0].shape[0] - sum_rows(size)) // size

    def total(first, rows):
        value = in_refs[0][first : first + rows, :]
        for ref in in_refs[1:]:
            value = value + ref[first : first + rows, :].astype(f32)
        return value

    sums = total(columns * size, sum_rows(size))
    for block, ref in enumerate(out_refs):
        for at in range(columns):
            part = total(at * size + block * count, count)
            ref[at * count : (at + 1) * count, :] = part.astype(ref.dtype)
        group, lane = divmod(block * count, lanes)
        lines = []
        for which in range(4):
            row = 8 * group + 2 * which
            lines += split_digits(sums[row : row + 1, :] + sums[row + 1 : row + 2, :])
        packed = rows_as_lanes(lines, ref.shape[0] - columns * count)
        if lane:
            packed = pltpu.roll(packed, lanes - lane, 1)
        ref[columns * count :, :] = packed.astype(ref.dtype)


def add(held, arrived, size, count, columns, after):
    shape = (columns * count + sum_rows(count), lanes)
    outs = [shaped(shape, f32 if b == 0 else bf16) for b in range(size // count)]
    return call(
        functools.partial(add_kernel, len(arrived), size, count),
        outs,
        held, *arrived, *after,
        in_specs=[pl.BlockSpec(memory_space=pltpu.VMEM)] * (1 + len(arrived))
        + [pl.BlockSpec(memory_space=pl.ANY)] * len(after),
    )


def finish_kernel(arrived, *refs):
    held_ref, arrived_refs = refs[0], refs[1 : 1 + arrived]
    unit_ref, radius_ref, grad_ref, loss_ref = refs[1 + arrived :]
    count, width = unit_ref.shape
    parts = blocks_of(width)
    total = held_ref[...]
    for ref in arrived_refs:
        total = total + ref[...].astype(f32)
    sums = []
    for which in range(4):
        row = 2 * parts * count + 2 * which
        sums.append((total[row : row + 1, :] + total[row + 1 : row + 2, :])[:, :count])
    pos, neg = [row * math.exp(scale) for row, scale in zip(sums, (pos_scale * margin, -neg_scale * margin))]
    loss_ref[...] = jnp.log(1.0 + pos) / pos_scale + jnp.log(1.0 + neg) / neg_scale
    scales = [
        to_column(math.exp(-neg_scale * margin) / (1.0 + neg)),
        to_column(math.exp(pos_scale * margin) / (1.0 + pos)),
    ]
    alongs = [to_column(row) for row in sums[2:]]
    unit = unit_ref[...]
    anchors = unit.astype(bf16).astype(f32)
    push, pull = [
        jnp.concatenate([total[(first + at) * count : (first + at + 1) * count, :] for at in range(parts)], axis=1)
        for first in (0, parts)
    ]
    grad_unit = (push + alongs[0] * anchors) * scales[0] - (pull + alongs[1] * anchors) * scales[1]
    along = jnp.sum(unit * grad_unit, axis=1, keepdims=True)
    grad_ref[...] = (grad_unit - unit * along) / radius_ref[:, :1]


def per_device(batch_rows, batch_labels, memory, memory_labels, keep_bits, step_index):
    groups = lax.axis_size("grp")
    members = lax.axis_size("dev")
    cores = 2 if members % 2 == 0 else 1
    line = members // cores
    count, width = batch_rows.shape
    slots = memory.shape[0]

    def exchange(value, axis, step):
        if axis == "grp":
            return lax.ppermute(value, "grp", [(i, i ^ step) for i in range(groups)])
        jump = step * cores if axis == "line" else step
        return lax.ppermute(value, "dev", [(i, i ^ jump) for i in range(members)])

    folded = (slots // lanes, lanes)
    parts = blocks_of(width)
    packed, unit, radius, slot_labels, copied_labels = call(
        prepare_kernel,
        [
            pltpu.VMEM((parts * count + 16, lanes), bf16),
            pltpu.VMEM((count, width), f32),
            pltpu.VMEM((count, lanes), f32),
            pltpu.VMEM(folded, jnp.int32),
            pltpu.VMEM(folded, jnp.int32),
        ],
        batch_rows, batch_labels.reshape(1, count), memory_labels.reshape(folded), keep_bits.reshape(folded),
        limit=vmem_most,
    )

    labels = [slot_labels] + [exchange(slot_labels, "core", s) for s in range(1, cores)]
    memories = [memory] + [exchange(memory, "core", s) for s in range(1, cores)]

    part = packed
    for s in range(line - 1, 0, -1):
        part = join([part, exchange(packed, "line", s)], labels if s == 1 else [])
    labels = [value.reshape(1, slots) for value in labels]
    blocks = [part] + [None] * (groups - 1)
    for s in range(groups - 1, 0, -1):
        blocks[s] = exchange(part, "grp", s)
    keys = [keys_of(memory, pltpu.HBM, [part])] + [keys_of(value, pltpu.VMEM, [part]) for value in memories[1:]]

    size = count * line
    arrived, after = [], []
    places = list(range(groups - 1, 0, -1))
    while places:
        now = places[:1] if not after else places[:2]
        places = places[len(now) :]
        after = block_sums([blocks[s] for s in now], keys, labels, count, bf16, after)
        arrived += [exchange(value, "grp", s) for s, value in zip(now, after)]
    held, copied = block_sums([part], keys, labels, count, f32, after, [memory])
    sizes = (count, slots, groups, line, cores)
    moved = pick(blocks, step_index, sizes, after)
    choices = [moved] + [exchange(moved, "core", s) for s in range(1, cores)]

    sums, *others = add(held, arrived, size, count, 2 * parts, choices)
    arrived = [exchange(value, "line", line - at) for at, value in enumerate(others, 1)]
    grad_batch, loss = call(
        functools.partial(finish_kernel, len(arrived)),
        [shaped((count, width), f32), shaped((1, count), f32)],
        sums, *arrived, unit, radius,
    )

    new_memory, new_labels = patch(copied, copied_labels, choices, step_index, sizes)
    return (grad_batch, loss.reshape(count), new_memory, new_labels.reshape(slots))


def solution(mesh):
    placed = (
        P(("grp", "dev"), None),
        P(("grp", "dev")),
        P(("grp", "dev"), None),
        P(("grp", "dev")),
        P(("grp", "dev")),
        P(),
    )
    return jax.shard_map(
        per_device,
        mesh=mesh,
        in_specs=placed,
        out_specs=(
            P(("grp", "dev"), None),
            P(("grp", "dev")),
            P(("grp", "dev"), None),
            P(("grp", "dev")),
        ),
        check_vma=False,
    )
```

```python
import functools
import math

import jax
import jax.numpy as jnp
from jax import lax
from jax.experimental import pallas as pl
from jax.experimental.pallas import tpu as pltpu
from jax.sharding import PartitionSpec as P

pos_scale = 2.0
neg_scale = 50.0
margin = 0.5
lanes = 128
log2e = math.log2(math.e)
vmem_bytes = 20 * 1024 * 1024
vmem_most = 56 * 1024 * 1024
f32 = jnp.float32
bf16 = jnp.bfloat16


def call(body, outs, *args, work=0, limit=vmem_bytes, **kw):
    return pl.pallas_call(
        body,
        out_shape=outs,
        compiler_params=pltpu.CompilerParams(vmem_limit_bytes=limit),
        cost_estimate=pl.CostEstimate(flops=work, bytes_accessed=0, transcendentals=0),
        **kw,
    )(*args)


def shaped(shape, dtype):
    return jax.ShapeDtypeStruct(shape, dtype)


def in_vmem(value):
    return pltpu.with_memory_space_constraint(value, pltpu.VMEM)


def rounded_up(value, unit):
    return (value + unit - 1) // unit * unit


def blocks_of(width):
    return width // lanes


def rows_as_lanes(parts, rows):
    row = lax.broadcasted_iota(jnp.int32, (rows, lanes), 0)
    out = jnp.zeros((rows, lanes), f32)
    for at, part in enumerate(parts):
        out = jnp.where(row == at, part, out)
    return out


def prepare_kernel(rows_ref, labels_ref, stored_ref, keep_ref, packed_ref, unit_ref, radius_ref, slot_ref, copy_ref):
    stored = stored_ref[...]
    slot_ref[...] = jnp.where(keep_ref[...] > 0, stored, -1)
    copy_ref[...] = stored
    rows = rows_ref[...].astype(f32)
    count, width = rows.shape
    radius = jnp.sqrt(jnp.sum(rows * rows, axis=1, keepdims=True) + 1e-06)
    unit = rows / radius
    unit_ref[...] = unit
    radius_ref[...] = jnp.broadcast_to(radius, radius_ref.shape)
    anchors = unit.astype(bf16)
    for at in range(blocks_of(width)):
        packed_ref[at * count : (at + 1) * count, :] = anchors[:, at * lanes : (at + 1) * lanes]
    row = jnp.concatenate([labels_ref[...].astype(f32), jnp.zeros((1, lanes - count), f32)], axis=1)
    high = jnp.floor(row * (1.0 / 256.0))
    tail = packed_ref.shape[0] - blocks_of(width) * count
    packed_ref[blocks_of(width) * count :, :] = rows_as_lanes([high, row - high * 256.0], tail).astype(bf16)


def diagonal(count):
    across = lax.broadcasted_iota(jnp.int32, (count, count), 1)
    down = lax.broadcasted_iota(jnp.int32, (count, count), 0)
    return across == down


def to_column(row):
    count = row.shape[1]
    spread = jnp.broadcast_to(row, (count, count))
    return jnp.sum(jnp.where(diagonal(count), spread, 0.0), axis=1, keepdims=True)


def to_row(column):
    count = column.shape[0]
    spread = jnp.broadcast_to(column, (count, count))
    return jnp.sum(jnp.where(diagonal(count), spread, 0.0), axis=0, keepdims=True)


def keys_kernel(memory_ref, *refs):
    keys_ref = refs[-1]
    rows = memory_ref[...].astype(f32)
    radius = jnp.sqrt(jnp.sum(rows * rows, axis=1, keepdims=True) + 1e-06)
    keys_ref[...] = (rows / radius).astype(bf16)


def keys_of(memory, place, after):
    slots, width = memory.shape
    block = math.gcd(512, slots)
    spec = pl.BlockSpec((block, width), lambda i: (i, 0))
    return call(
        keys_kernel,
        [shaped((slots, width), bf16)],
        pltpu.with_memory_space_constraint(memory, place), *after,
        work=64 * slots * width * width,
        grid=(slots // block,),
        in_specs=[spec] + [pl.BlockSpec(memory_space=pl.ANY)] * len(after),
        out_specs=[spec],
    )[0]


def join_kernel(blocks, *refs):
    block_refs, out_ref = refs[:blocks], refs[-1]
    first = 0
    for ref in block_refs:
        out_ref[first : first + ref.shape[0], :] = ref[...]
        first += ref.shape[0]


def join(blocks, after):
    rows = sum(block.shape[0] for block in blocks)
    return call(
        functools.partial(join_kernel, len(blocks)),
        [shaped((rows, blocks[0].shape[1]), blocks[0].dtype)],
        *blocks, *after,
        in_specs=[pl.BlockSpec(memory_space=pltpu.VMEM)] * len(blocks)
        + [pl.BlockSpec(memory_space=pl.ANY)] * len(after),
    )[0]


def positions(step, count, slots, groups, line, cores):
    first = lax.rem(step, slots // count) * count
    crossing = lax.rem(step, cores)
    members = line * cores
    devices_all = groups * members
    grp = lax.axis_index("grp")
    dev = lax.axis_index("dev")
    target = grp * members + (dev ^ crossing)
    source = lax.rem(target + devices_all - lax.rem(step, devices_all), devices_all)
    source_grp = lax.div(source, members)
    source_line = lax.div(lax.rem(source, members), cores)
    step = lax.div(dev, cores) ^ source_line
    return first, crossing, grp ^ source_grp, lax.rem(line - step, line)


def pick_kernel(groups, sizes, step_ref, *refs):
    blocks_refs, out_ref = refs[:groups], refs[-1]
    rows = out_ref.shape[0]
    _, _, grp_place, line_place = positions(step_ref[0], *sizes)
    for place, ref in enumerate(blocks_refs):

        @pl.when(grp_place == place)
        def _():
            out_ref[...] = ref[pl.ds(pl.multiple_of(line_place * rows, 16), rows), :]


def pick(blocks, step, sizes, after):
    line = sizes[3]
    return call(
        functools.partial(pick_kernel, len(blocks), sizes),
        [shaped((blocks[0].shape[0] // line, lanes), bf16)],
        step, *blocks, *after,
        in_specs=[pl.BlockSpec(memory_space=pltpu.SMEM)]
        + [pl.BlockSpec(memory_space=pltpu.VMEM)] * len(blocks)
        + [pl.BlockSpec(memory_space=pl.ANY)] * len(after),
    )[0]


def patch_kernel(choices, sizes, step_ref, stored_ref, labels_ref, *refs):
    moved_refs, (memory_ref, new_labels_ref, rows_ref, sem) = refs[:choices], refs[choices:]
    count, width = rows_ref.shape
    first, crossing, _, _ = positions(step_ref[0], *sizes)
    moved = moved_refs[0][...]
    for choice in range(1, choices):
        moved = jnp.where(crossing == choice, moved_refs[choice][...], moved)
    for at in range(blocks_of(width)):
        rows_ref[:, at * lanes : (at + 1) * lanes] = moved[at * count : (at + 1) * count, :]
    target = memory_ref.at[pl.ds(pl.multiple_of(first, count), count), :]
    copy = pltpu.make_async_copy(rows_ref, target, sem)
    copy.start()
    digits = moved[blocks_of(width) * count :, :].astype(f32)
    row = (digits[0:1, :] * 256.0 + digits[1:2, :]).astype(jnp.int32)
    old = labels_ref[...]
    turned = pltpu.roll(jnp.broadcast_to(row, old.shape), lax.rem(first, lanes), 1)
    slot = lax.broadcasted_iota(jnp.int32, old.shape, 0) * lanes + lax.broadcasted_iota(jnp.int32, old.shape, 1)
    new_labels_ref[...] = jnp.where((slot >= first) & (slot < first + count), turned, old)
    copy.wait()


def patch(stored, labels, choices, step, sizes):
    count, width = sizes[0], stored.shape[1]
    return call(
        functools.partial(patch_kernel, len(choices), sizes),
        [shaped(stored.shape, bf16), shaped(labels.shape, jnp.int32)],
        step, stored, labels, *choices,
        in_specs=[pl.BlockSpec(memory_space=pltpu.SMEM), pl.BlockSpec(memory_space=pl.ANY)]
        + [pl.BlockSpec(memory_space=pltpu.VMEM)] * (1 + len(choices)),
        out_specs=[pl.BlockSpec(memory_space=pl.ANY), pl.BlockSpec(memory_space=pltpu.VMEM)],
        scratch_shapes=[pltpu.VMEM((count, width), bf16), pltpu.SemaphoreType.DMA],
        input_output_aliases={1: 0},
    )


def split_digits(row):
    high = row.astype(bf16).astype(f32)
    return [high, row - high]


def sum_rows(size):
    return rounded_up(8 * (rounded_up(size, lanes) // lanes), 16)


def block_kernel(blocks, sides, unit, count, copies, scratch, *refs):
    if copies:
        source_ref, target_ref, sem = refs[blocks + 2 * sides], refs[-scratch - 1], refs[-1]
        copy = pltpu.make_async_copy(source_ref, target_ref, sem)
        copy.start()
        refs = refs[: -scratch - 1] + refs[-scratch : -1]
        scratch -= 1
    rows_refs, keys_refs = refs[:blocks], refs[blocks : blocks + sides]
    label_refs = refs[blocks + sides : blocks + 2 * sides]
    out_refs = refs[-scratch - blocks : -scratch]
    anchors_ref, labels_ref, total_ref, pos_ref, neg_ref = refs[-scratch:-4]
    scores_refs, weight_refs = refs[-4:-2], refs[-2:]
    slots, width = keys_refs[0].shape
    parts = blocks_of(width)
    packed = rows_refs[0].shape[0]
    members = packed // (parts * count + 16)
    size = members * count
    columns = []
    for block, ref in enumerate(rows_refs):
        for member in range(members):
            first = member * (parts * count + 16)
            to = block * size + member * count
            for at in range(parts):
                anchors_ref[to : to + count, at * lanes : (at + 1) * lanes] = ref[
                    first + at * count : first + (at + 1) * count, :
                ]
            digits = ref[first + parts * count : first + parts * count + 16, :].astype(f32)
            columns.append(to_column((digits[0:1, :] * 256.0 + digits[1:2, :])[:, :count]))
    rows = blocks * size
    labels_ref[...] = jnp.broadcast_to(jnp.concatenate(columns, axis=0), labels_ref.shape)
    pos_ref[...] = jnp.zeros_like(pos_ref)
    neg_ref[...] = jnp.zeros_like(neg_ref)
    anchors = anchors_ref[...]
    units = [(side, at) for side in range(sides) for at in range(0, slots, unit)]
    runs = []
    for side in range(sides):
        left = slots // unit
        while left:
            length = min(4, left)
            if side == sides - 1 and length == left and left > 1:
                length -= 1
            runs.append(length)
            left -= length
    starts = [sum(runs[:run]) for run in range(len(runs))]
    run_of = [run for run, length in enumerate(runs) for _ in range(length)]
    quarter = rows // 4

    def score_unit(at):
        side, first = units[at]
        scores_refs[at % 2][...] = lax.dot_general(
            anchors, keys_refs[side][first : first + unit, :], (((1,), (1,)), ((), ())), preferred_element_type=f32
        )

    def term_unit(at, which):
        side, first = units[at]
        part = slice(which * quarter, (which + 1) * quarter)
        weights_ref = weight_refs[run_of[at] % 2]
        base = (at - starts[run_of[at]]) * unit
        wanted = labels_ref[part, :]
        pos_sum, neg_sum = pos_ref[part, :], neg_ref[part, :]
        for piece in range(0, unit, lanes):
            slot_labels = label_refs[side][:, first + piece : first + piece + lanes].astype(f32)
            neg_shift = jnp.where(slot_labels < 0.0, -1e30, -neg_scale * margin * log2e)
            same = wanted == slot_labels
            slope = jnp.where(same, -pos_scale * log2e, neg_scale * log2e)
            shift = jnp.where(same, pos_scale * margin * log2e, neg_shift)
            term = jnp.exp2(scores_refs[at % 2][part, piece : piece + lanes] * slope + shift)
            pos = jnp.where(same, term, 0.0)
            neg = jnp.where(same, 0.0, term)
            pos_sum += pos
            neg_sum += neg
            to = slice(base + piece, base + piece + lanes)
            weights_ref[part, to] = neg.astype(bf16)
            weights_ref[rows + which * quarter : rows + (which + 1) * quarter, to] = pos.astype(bf16)
        pos_ref[part, :] = pos_sum
        neg_ref[part, :] = neg_sum

    def weigh_half(run, half):
        side, first = units[starts[run]]
        span = runs[run] * unit
        part = slice(half * (width // 2), (half + 1) * (width // 2))
        more = jnp.dot(
            weight_refs[run % 2][:, :span], keys_refs[side][first : first + span, part], preferred_element_type=f32
        )
        total_ref[:, part] = more if run == 0 else total_ref[:, part] + more

    score_unit(0)
    waiting = []
    for at in range(len(units)):
        if at in starts and at:
            waiting += [(run_of[at] - 1, 0), (run_of[at] - 1, 1)]
        left = runs[run_of[at]] - (at - starts[run_of[at]])
        now, waiting = waiting[: -(-len(waiting) // left)], waiting[-(-len(waiting) // left) :]
        term_unit(at, 0)
        if at + 1 < len(units):
            score_unit(at + 1)
        term_unit(at, 1)
        term_unit(at, 2)
        for run, half in now:
            weigh_half(run, half)
        term_unit(at, 3)
    weigh_half(len(runs) - 1, 0)
    weigh_half(len(runs) - 1, 1)
    total = total_ref[...]
    pos_sum = jnp.sum(pos_ref[...], axis=1, keepdims=True)
    neg_sum = jnp.sum(neg_ref[...], axis=1, keepdims=True)
    floats = anchors.astype(f32)
    sums = [pos_sum, neg_sum]
    for which in range(2):
        value = total[which * rows : (which + 1) * rows, :]
        along = jnp.sum(value * floats, axis=1, keepdims=True)
        sums.append(along)
        rest = value - along * floats
        for block, ref in enumerate(out_refs):
            for at in range(parts):
                first = (which * parts + at) * size
                ref[first : first + size, :] = rest[
                    block * size : (block + 1) * size, at * lanes : (at + 1) * lanes
                ].astype(ref.dtype)
    for block, ref in enumerate(out_refs):
        lines = []
        for first in range(0, size, lanes):
            last = min(first + lanes, size)
            for value in sums:
                row = to_row(value[block * size + first : block * size + last])
                if last - first < lanes:
                    row = jnp.concatenate([row, jnp.zeros((1, lanes - last + first), f32)], axis=1)
                lines += split_digits(row)
        first = 2 * parts * size
        ref[first:, :] = rows_as_lanes(lines, ref.shape[0] - first).astype(ref.dtype)
    if copies:
        copy.wait()


def block_sums(blocks, keys, labels, count, dtype, after, copied=()):
    slots, width = keys[0].shape
    parts = blocks_of(width)
    size = blocks[0].shape[0] // (parts * count + 16) * count
    rows = len(blocks) * size
    unit = math.gcd(256, slots // 2)
    anywhere = pl.BlockSpec(memory_space=pl.ANY)
    vmem = pl.BlockSpec(memory_space=pltpu.VMEM)
    return call(
        functools.partial(block_kernel, len(blocks), len(keys), unit, count, len(copied), 9 + len(copied)),
        [shaped((2 * parts * size + sum_rows(size), lanes), dtype)] * len(blocks)
        + [shaped(value.shape, value.dtype) for value in copied],
        *blocks, *[in_vmem(k) for k in keys], *labels, *copied, *after,
        work=12 * size * len(blocks) * slots * len(keys) * width,
        in_specs=[vmem] * (len(blocks) + 2 * len(keys)) + [anywhere] * (len(copied) + len(after)),
        out_specs=[vmem] * len(blocks) + [anywhere] * len(copied),
        scratch_shapes=[
            pltpu.VMEM((rows, width), bf16),
            pltpu.VMEM((rows, lanes), f32),
            pltpu.VMEM((2 * rows, width), f32),
            pltpu.VMEM((rows, lanes), f32),
            pltpu.VMEM((rows, lanes), f32),
            pltpu.VMEM((rows, unit), f32),
            pltpu.VMEM((rows, unit), f32),
            pltpu.VMEM((2 * rows, 4 * unit), bf16),
            pltpu.VMEM((2 * rows, 4 * unit), bf16),
        ]
        + [pltpu.SemaphoreType.DMA] * len(copied),
    )


def add_kernel(arrived, size, count, *refs):
    in_refs, out_refs = refs[: 1 + arrived], refs[-(size // count) :]
    columns = (in_refs[0].shape[0] - sum_rows(size)) // size

    def total(first, rows):
        value = in_refs[0][first : first + rows, :]
        for ref in in_refs[1:]:
            value = value + ref[first : first + rows, :].astype(f32)
        return value

    sums = total(columns * size, sum_rows(size))
    for block, ref in enumerate(out_refs):
        for at in range(columns):
            part = total(at * size + block * count, count)
            ref[at * count : (at + 1) * count, :] = part.astype(ref.dtype)
        group, lane = divmod(block * count, lanes)
        lines = []
        for which in range(4):
            row = 8 * group + 2 * which
            lines += split_digits(sums[row : row + 1, :] + sums[row + 1 : row + 2, :])
        packed = rows_as_lanes(lines, ref.shape[0] - columns * count)
        if lane:
            packed = pltpu.roll(packed, lanes - lane, 1)
        ref[columns * count :, :] = packed.astype(ref.dtype)


def add(held, arrived, size, count, columns, after):
    shape = (columns * count + sum_rows(count), lanes)
    outs = [shaped(shape, f32 if b == 0 else bf16) for b in range(size // count)]
    return call(
        functools.partial(add_kernel, len(arrived), size, count),
        outs,
        held, *arrived, *after,
        in_specs=[pl.BlockSpec(memory_space=pltpu.VMEM)] * (1 + len(arrived))
        + [pl.BlockSpec(memory_space=pl.ANY)] * len(after),
    )


def finish_kernel(arrived, *refs):
    held_ref, arrived_refs = refs[0], refs[1 : 1 + arrived]
    unit_ref, radius_ref, grad_ref, loss_ref = refs[1 + arrived :]
    count, width = unit_ref.shape
    parts = blocks_of(width)
    total = held_ref[...]
    for ref in arrived_refs:
        total = total + ref[...].astype(f32)
    sums = []
    for which in range(4):
        row = 2 * parts * count + 2 * which
        sums.append((total[row : row + 1, :] + total[row + 1 : row + 2, :])[:, :count])
    pos, neg = sums[:2]
    loss_ref[...] = jnp.log(1.0 + pos) / pos_scale + jnp.log(1.0 + neg) / neg_scale
    scales = [to_column(1.0 / (1.0 + row)) for row in (neg, pos)]
    alongs = [to_column(row) for row in sums[2:]]
    unit = unit_ref[...]
    anchors = unit.astype(bf16).astype(f32)
    push, pull = [
        jnp.concatenate([total[(first + at) * count : (first + at + 1) * count, :] for at in range(parts)], axis=1)
        for first in (0, parts)
    ]
    grad_unit = (push + alongs[0] * anchors) * scales[0] - (pull + alongs[1] * anchors) * scales[1]
    along = jnp.sum(unit * grad_unit, axis=1, keepdims=True)
    grad_ref[...] = (grad_unit - unit * along) / radius_ref[:, :1]


def per_device(batch_rows, batch_labels, memory, memory_labels, keep_bits, step_index):
    groups = lax.axis_size("grp")
    members = lax.axis_size("dev")
    cores = 2 if members % 2 == 0 else 1
    line = members // cores
    count, width = batch_rows.shape
    slots = memory.shape[0]

    def exchange(value, axis, step):
        if axis == "grp":
            return lax.ppermute(value, "grp", [(i, i ^ step) for i in range(groups)])
        jump = step * cores if axis == "line" else step
        return lax.ppermute(value, "dev", [(i, i ^ jump) for i in range(members)])

    folded = (slots // lanes, lanes)
    parts = blocks_of(width)
    packed, unit, radius, slot_labels, copied_labels = call(
        prepare_kernel,
        [
            pltpu.VMEM((parts * count + 16, lanes), bf16),
            pltpu.VMEM((count, width), f32),
            pltpu.VMEM((count, lanes), f32),
            pltpu.VMEM(folded, jnp.int32),
            pltpu.VMEM(folded, jnp.int32),
        ],
        batch_rows, batch_labels.reshape(1, count), memory_labels.reshape(folded), keep_bits.reshape(folded),
        limit=vmem_most,
    )

    labels = [slot_labels] + [exchange(slot_labels, "core", s) for s in range(1, cores)]
    memories = [memory] + [exchange(memory, "core", s) for s in range(1, cores)]

    part = packed
    for s in range(line - 1, 0, -1):
        part = join([part, exchange(packed, "line", s)], labels if s == 1 else [])
    labels = [value.reshape(1, slots) for value in labels]
    blocks = [part] + [None] * (groups - 1)
    for s in range(groups - 1, 0, -1):
        blocks[s] = exchange(part, "grp", s)
    keys = [keys_of(memory, pltpu.HBM, [part])] + [keys_of(value, pltpu.VMEM, [part]) for value in memories[1:]]

    size = count * line
    arrived, after = [], []
    places = list(range(groups - 1, 0, -1))
    while places:
        now = places[:1] if not after else places[:2]
        places = places[len(now) :]
        after = block_sums([blocks[s] for s in now], keys, labels, count, bf16, after)
        arrived += [exchange(value, "grp", s) for s, value in zip(now, after)]
    held, copied = block_sums([part], keys, labels, count, f32, after, [memory])
    sizes = (count, slots, groups, line, cores)
    moved = pick(blocks, step_index, sizes, after)
    choices = [moved] + [exchange(moved, "core", s) for s in range(1, cores)]

    sums, *others = add(held, arrived, size, count, 2 * parts, choices)
    arrived = [exchange(value, "line", line - at) for at, value in enumerate(others, 1)]
    grad_batch, loss = call(
        functools.partial(finish_kernel, len(arrived)),
        [shaped((count, width), f32), shaped((1, count), f32)],
        sums, *arrived, unit, radius,
    )

    new_memory, new_labels = patch(copied, copied_labels, choices, step_index, sizes)
    return (grad_batch, loss.reshape(count), new_memory, new_labels.reshape(slots))


def solution(mesh):
    placed = (
        P(("grp", "dev"), None),
        P(("grp", "dev")),
        P(("grp", "dev"), None),
        P(("grp", "dev")),
        P(("grp", "dev")),
        P(),
    )
    return jax.shard_map(
        per_device,
        mesh=mesh,
        in_specs=placed,
        out_specs=(
            P(("grp", "dev"), None),
            P(("grp", "dev")),
            P(("grp", "dev"), None),
            P(("grp", "dev")),
        ),
        check_vma=False,
    )
```

```python
import functools
import math

import jax
import jax.numpy as jnp
from jax import lax
from jax.experimental import pallas as pl
from jax.experimental.pallas import tpu as pltpu
from jax.sharding import PartitionSpec as P

pos_scale = 2.0
neg_scale = 50.0
margin = 0.5
lanes = 128
log2e = math.log2(math.e)
vmem_bytes = 20 * 1024 * 1024
vmem_most = 56 * 1024 * 1024
f32 = jnp.float32
bf16 = jnp.bfloat16


def call(body, outs, *args, work=0, limit=vmem_bytes, **kw):
    return pl.pallas_call(
        body,
        out_shape=outs,
        compiler_params=pltpu.CompilerParams(vmem_limit_bytes=limit),
        cost_estimate=pl.CostEstimate(flops=work, bytes_accessed=0, transcendentals=0),
        **kw,
    )(*args)


def shaped(shape, dtype):
    return jax.ShapeDtypeStruct(shape, dtype)


def in_vmem(value):
    return pltpu.with_memory_space_constraint(value, pltpu.VMEM)


def rounded_up(value, unit):
    return (value + unit - 1) // unit * unit


def blocks_of(width):
    return width // lanes


def rows_as_lanes(parts, rows):
    row = lax.broadcasted_iota(jnp.int32, (rows, lanes), 0)
    out = jnp.zeros((rows, lanes), f32)
    for at, part in enumerate(parts):
        out = jnp.where(row == at, part, out)
    return out


def prepare_kernel(rows_ref, labels_ref, stored_ref, keep_ref, packed_ref, unit_ref, radius_ref, slot_ref, copy_ref):
    stored = stored_ref[...]
    slot_ref[...] = jnp.where(keep_ref[...] > 0, stored, -1)
    copy_ref[...] = stored
    rows = rows_ref[...].astype(f32)
    count, width = rows.shape
    radius = jnp.sqrt(jnp.sum(rows * rows, axis=1, keepdims=True) + 1e-06)
    unit = rows / radius
    unit_ref[...] = unit
    radius_ref[...] = jnp.broadcast_to(radius, radius_ref.shape)
    anchors = unit.astype(bf16)
    for at in range(blocks_of(width)):
        packed_ref[at * count : (at + 1) * count, :] = anchors[:, at * lanes : (at + 1) * lanes]
    row = jnp.concatenate([labels_ref[...].astype(f32), jnp.zeros((1, lanes - count), f32)], axis=1)
    high = jnp.floor(row * (1.0 / 256.0))
    tail = packed_ref.shape[0] - blocks_of(width) * count
    packed_ref[blocks_of(width) * count :, :] = rows_as_lanes([high, row - high * 256.0], tail).astype(bf16)


def diagonal(count):
    across = lax.broadcasted_iota(jnp.int32, (count, count), 1)
    down = lax.broadcasted_iota(jnp.int32, (count, count), 0)
    return across == down


def to_column(row):
    count = row.shape[1]
    spread = jnp.broadcast_to(row, (count, count))
    return jnp.sum(jnp.where(diagonal(count), spread, 0.0), axis=1, keepdims=True)


def to_row(column):
    count = column.shape[0]
    spread = jnp.broadcast_to(column, (count, count))
    return jnp.sum(jnp.where(diagonal(count), spread, 0.0), axis=0, keepdims=True)


def keys_kernel(memory_ref, *refs):
    keys_ref = refs[-1]
    rows = memory_ref[...].astype(f32)
    radius = jnp.sqrt(jnp.sum(rows * rows, axis=1, keepdims=True) + 1e-06)
    keys_ref[...] = (rows / radius).astype(bf16)


def keys_of(memory, place, after):
    slots, width = memory.shape
    block = math.gcd(512, slots)
    spec = pl.BlockSpec((block, width), lambda i: (i, 0))
    return call(
        keys_kernel,
        [shaped((slots, width), bf16)],
        pltpu.with_memory_space_constraint(memory, place), *after,
        work=64 * slots * width * width,
        grid=(slots // block,),
        in_specs=[spec] + [pl.BlockSpec(memory_space=pl.ANY)] * len(after),
        out_specs=[spec],
    )[0]


def join_kernel(blocks, *refs):
    block_refs, out_ref = refs[:blocks], refs[-1]
    first = 0
    for ref in block_refs:
        out_ref[first : first + ref.shape[0], :] = ref[...]
        first += ref.shape[0]


def join(blocks, after):
    rows = sum(block.shape[0] for block in blocks)
    return call(
        functools.partial(join_kernel, len(blocks)),
        [shaped((rows, blocks[0].shape[1]), blocks[0].dtype)],
        *blocks, *after,
        in_specs=[pl.BlockSpec(memory_space=pltpu.VMEM)] * len(blocks)
        + [pl.BlockSpec(memory_space=pl.ANY)] * len(after),
    )[0]


def positions(step, count, slots, groups, line, cores):
    first = lax.rem(step, slots // count) * count
    crossing = lax.rem(step, cores)
    members = line * cores
    devices_all = groups * members
    grp = lax.axis_index("grp")
    dev = lax.axis_index("dev")
    target = grp * members + (dev ^ crossing)
    source = lax.rem(target + devices_all - lax.rem(step, devices_all), devices_all)
    source_grp = lax.div(source, members)
    source_line = lax.div(lax.rem(source, members), cores)
    step = lax.div(dev, cores) ^ source_line
    return first, crossing, grp ^ source_grp, lax.rem(line - step, line)


def pick_kernel(groups, sizes, step_ref, *refs):
    blocks_refs, out_ref = refs[:groups], refs[-1]
    rows = out_ref.shape[0]
    _, _, grp_place, line_place = positions(step_ref[0], *sizes)
    for place, ref in enumerate(blocks_refs):

        @pl.when(grp_place == place)
        def _():
            out_ref[...] = ref[pl.ds(pl.multiple_of(line_place * rows, 16), rows), :]


def pick(blocks, step, sizes, after):
    line = sizes[3]
    return call(
        functools.partial(pick_kernel, len(blocks), sizes),
        [shaped((blocks[0].shape[0] // line, lanes), bf16)],
        step, *blocks, *after,
        in_specs=[pl.BlockSpec(memory_space=pltpu.SMEM)]
        + [pl.BlockSpec(memory_space=pltpu.VMEM)] * len(blocks)
        + [pl.BlockSpec(memory_space=pl.ANY)] * len(after),
    )[0]


def patch_kernel(choices, sizes, step_ref, stored_ref, labels_ref, *refs):
    moved_refs, (memory_ref, new_labels_ref, rows_ref, sem) = refs[:choices], refs[choices:]
    count, width = rows_ref.shape
    first, crossing, _, _ = positions(step_ref[0], *sizes)
    moved = moved_refs[0][...]
    for choice in range(1, choices):
        moved = jnp.where(crossing == choice, moved_refs[choice][...], moved)
    for at in range(blocks_of(width)):
        rows_ref[:, at * lanes : (at + 1) * lanes] = moved[at * count : (at + 1) * count, :]
    target = memory_ref.at[pl.ds(pl.multiple_of(first, count), count), :]
    copy = pltpu.make_async_copy(rows_ref, target, sem)
    copy.start()
    digits = moved[blocks_of(width) * count :, :].astype(f32)
    row = (digits[0:1, :] * 256.0 + digits[1:2, :]).astype(jnp.int32)
    old = labels_ref[...]
    turned = pltpu.roll(jnp.broadcast_to(row, old.shape), lax.rem(first, lanes), 1)
    slot = lax.broadcasted_iota(jnp.int32, old.shape, 0) * lanes + lax.broadcasted_iota(jnp.int32, old.shape, 1)
    new_labels_ref[...] = jnp.where((slot >= first) & (slot < first + count), turned, old)
    copy.wait()


def patch(stored, labels, choices, step, sizes):
    count, width = sizes[0], stored.shape[1]
    return call(
        functools.partial(patch_kernel, len(choices), sizes),
        [shaped(stored.shape, bf16), shaped(labels.shape, jnp.int32)],
        step, stored, labels, *choices,
        in_specs=[pl.BlockSpec(memory_space=pltpu.SMEM), pl.BlockSpec(memory_space=pl.ANY)]
        + [pl.BlockSpec(memory_space=pltpu.VMEM)] * (1 + len(choices)),
        out_specs=[pl.BlockSpec(memory_space=pl.ANY), pl.BlockSpec(memory_space=pltpu.VMEM)],
        scratch_shapes=[pltpu.VMEM((count, width), bf16), pltpu.SemaphoreType.DMA],
        input_output_aliases={1: 0},
    )


def split_digits(row):
    high = row.astype(bf16).astype(f32)
    return [high, row - high]


def sum_rows(size):
    return rounded_up(8 * (rounded_up(size, lanes) // lanes), 16)


def block_kernel(blocks, sides, unit, count, copies, scratch, *refs):
    if copies:
        source_ref, target_ref, sem = refs[blocks + 2 * sides], refs[-scratch - 1], refs[-1]
        copy = pltpu.make_async_copy(source_ref, target_ref, sem)
        copy.start()
        refs = refs[: -scratch - 1] + refs[-scratch : -1]
        scratch -= 1
    rows_refs, keys_refs = refs[:blocks], refs[blocks : blocks + sides]
    label_refs = refs[blocks + sides : blocks + 2 * sides]
    out_refs = refs[-scratch - blocks : -scratch]
    anchors_ref, labels_ref, total_ref, pos_ref, neg_ref = refs[-scratch:-4]
    scores_refs, weight_refs = refs[-4:-2], refs[-2:]
    slots, width = keys_refs[0].shape
    parts = blocks_of(width)
    packed = rows_refs[0].shape[0]
    members = packed // (parts * count + 16)
    size = members * count
    columns = []
    for block, ref in enumerate(rows_refs):
        for member in range(members):
            first = member * (parts * count + 16)
            to = block * size + member * count
            for at in range(parts):
                anchors_ref[to : to + count, at * lanes : (at + 1) * lanes] = ref[
                    first + at * count : first + (at + 1) * count, :
                ]
            digits = ref[first + parts * count : first + parts * count + 16, :].astype(f32)
            columns.append(to_column((digits[0:1, :] * 256.0 + digits[1:2, :])[:, :count]))
    rows = blocks * size
    labels_ref[...] = jnp.broadcast_to(jnp.concatenate(columns, axis=0), labels_ref.shape)
    pos_ref[...] = jnp.zeros_like(pos_ref)
    neg_ref[...] = jnp.zeros_like(neg_ref)
    anchors = anchors_ref[...]
    units = [(side, at) for side in range(sides) for at in range(0, slots, unit)]
    longest = 4 if blocks == 1 else 2
    runs = []
    for side in range(sides):
        left = slots // unit
        while left:
            length = min(longest, left)
            if blocks == 1 and side == sides - 1 and length == left and left > 1:
                length -= 1
            runs.append(length)
            left -= length
    starts = [sum(runs[:run]) for run in range(len(runs))]
    run_of = [run for run, length in enumerate(runs) for _ in range(length)]
    quarter = rows // 4

    def score_unit(at):
        side, first = units[at]
        scores_refs[at % 2][...] = lax.dot_general(
            anchors, keys_refs[side][first : first + unit, :], (((1,), (1,)), ((), ())), preferred_element_type=f32
        )

    def term_unit(at, which):
        side, first = units[at]
        part = slice(which * quarter, (which + 1) * quarter)
        weights_ref = weight_refs[run_of[at] % 2]
        base = (at - starts[run_of[at]]) * unit
        wanted = labels_ref[part, :]
        pos_sum, neg_sum = pos_ref[part, :], neg_ref[part, :]
        for piece in range(0, unit, lanes):
            slot_labels = label_refs[side][:, first + piece : first + piece + lanes].astype(f32)
            neg_shift = jnp.where(slot_labels < 0.0, -1e30, -neg_scale * margin * log2e)
            same = wanted == slot_labels
            slope = jnp.where(same, -pos_scale * log2e, neg_scale * log2e)
            shift = jnp.where(same, pos_scale * margin * log2e, neg_shift)
            term = jnp.exp2(scores_refs[at % 2][part, piece : piece + lanes] * slope + shift)
            pos = jnp.where(same, term, 0.0)
            neg = jnp.where(same, 0.0, term)
            pos_sum += pos
            neg_sum += neg
            to = slice(base + piece, base + piece + lanes)
            weights_ref[part, to] = neg.astype(bf16)
            weights_ref[rows + which * quarter : rows + (which + 1) * quarter, to] = pos.astype(bf16)
        pos_ref[part, :] = pos_sum
        neg_ref[part, :] = neg_sum

    def weigh_half(run, half):
        side, first = units[starts[run]]
        span = runs[run] * unit
        part = slice(half * (width // 2), (half + 1) * (width // 2))
        more = jnp.dot(
            weight_refs[run % 2][:, :span], keys_refs[side][first : first + span, part], preferred_element_type=f32
        )
        total_ref[:, part] = more if run == 0 else total_ref[:, part] + more

    score_unit(0)
    waiting = []
    for at in range(len(units)):
        if at in starts and at:
            waiting += [(run_of[at] - 1, 0), (run_of[at] - 1, 1)]
        left = runs[run_of[at]] - (at - starts[run_of[at]])
        now, waiting = waiting[: -(-len(waiting) // left)], waiting[-(-len(waiting) // left) :]
        term_unit(at, 0)
        if at + 1 < len(units):
            score_unit(at + 1)
        term_unit(at, 1)
        term_unit(at, 2)
        for run, half in now:
            weigh_half(run, half)
        term_unit(at, 3)
    weigh_half(len(runs) - 1, 0)
    weigh_half(len(runs) - 1, 1)
    total = total_ref[...]
    pos_sum = jnp.sum(pos_ref[...], axis=1, keepdims=True)
    neg_sum = jnp.sum(neg_ref[...], axis=1, keepdims=True)
    floats = anchors.astype(f32)
    sums = [pos_sum, neg_sum]
    for which in range(2):
        value = total[which * rows : (which + 1) * rows, :]
        along = jnp.sum(value * floats, axis=1, keepdims=True)
        sums.append(along)
        rest = value - along * floats
        for block, ref in enumerate(out_refs):
            for at in range(parts):
                first = (which * parts + at) * size
                ref[first : first + size, :] = rest[
                    block * size : (block + 1) * size, at * lanes : (at + 1) * lanes
                ].astype(ref.dtype)
    for block, ref in enumerate(out_refs):
        lines = []
        for first in range(0, size, lanes):
            last = min(first + lanes, size)
            for value in sums:
                row = to_row(value[block * size + first : block * size + last])
                if last - first < lanes:
                    row = jnp.concatenate([row, jnp.zeros((1, lanes - last + first), f32)], axis=1)
                lines += split_digits(row)
        first = 2 * parts * size
        ref[first:, :] = rows_as_lanes(lines, ref.shape[0] - first).astype(ref.dtype)
    if copies:
        copy.wait()


def block_sums(blocks, keys, labels, count, dtype, after, copied=()):
    slots, width = keys[0].shape
    parts = blocks_of(width)
    size = blocks[0].shape[0] // (parts * count + 16) * count
    rows = len(blocks) * size
    unit = math.gcd(256, slots // 2)
    anywhere = pl.BlockSpec(memory_space=pl.ANY)
    vmem = pl.BlockSpec(memory_space=pltpu.VMEM)
    return call(
        functools.partial(block_kernel, len(blocks), len(keys), unit, count, len(copied), 9 + len(copied)),
        [shaped((2 * parts * size + sum_rows(size), lanes), dtype)] * len(blocks)
        + [shaped(value.shape, value.dtype) for value in copied],
        *blocks, *[in_vmem(k) for k in keys], *labels, *copied, *after,
        work=12 * size * len(blocks) * slots * len(keys) * width,
        in_specs=[vmem] * (len(blocks) + 2 * len(keys)) + [anywhere] * (len(copied) + len(after)),
        out_specs=[vmem] * len(blocks) + [anywhere] * len(copied),
        scratch_shapes=[
            pltpu.VMEM((rows, width), bf16),
            pltpu.VMEM((rows, lanes), f32),
            pltpu.VMEM((2 * rows, width), f32),
            pltpu.VMEM((rows, lanes), f32),
            pltpu.VMEM((rows, lanes), f32),
            pltpu.VMEM((rows, unit), f32),
            pltpu.VMEM((rows, unit), f32),
            pltpu.VMEM((2 * rows, (4 if len(blocks) == 1 else 2) * unit), bf16),
            pltpu.VMEM((2 * rows, (4 if len(blocks) == 1 else 2) * unit), bf16),
        ]
        + [pltpu.SemaphoreType.DMA] * len(copied),
    )


def add_kernel(arrived, size, count, *refs):
    in_refs, out_refs = refs[: 1 + arrived], refs[-(size // count) :]
    columns = (in_refs[0].shape[0] - sum_rows(size)) // size

    def total(first, rows):
        value = in_refs[0][first : first + rows, :]
        for ref in in_refs[1:]:
            value = value + ref[first : first + rows, :].astype(f32)
        return value

    sums = total(columns * size, sum_rows(size))
    for block, ref in enumerate(out_refs):
        for at in range(columns):
            part = total(at * size + block * count, count)
            ref[at * count : (at + 1) * count, :] = part.astype(ref.dtype)
        group, lane = divmod(block * count, lanes)
        lines = []
        for which in range(4):
            row = 8 * group + 2 * which
            lines += split_digits(sums[row : row + 1, :] + sums[row + 1 : row + 2, :])
        packed = rows_as_lanes(lines, ref.shape[0] - columns * count)
        if lane:
            packed = pltpu.roll(packed, lanes - lane, 1)
        ref[columns * count :, :] = packed.astype(ref.dtype)


def add(held, arrived, size, count, columns, after):
    shape = (columns * count + sum_rows(count), lanes)
    outs = [shaped(shape, f32 if b == 0 else bf16) for b in range(size // count)]
    return call(
        functools.partial(add_kernel, len(arrived), size, count),
        outs,
        held, *arrived, *after,
        in_specs=[pl.BlockSpec(memory_space=pltpu.VMEM)] * (1 + len(arrived))
        + [pl.BlockSpec(memory_space=pl.ANY)] * len(after),
    )


def finish_kernel(arrived, *refs):
    held_ref, arrived_refs = refs[0], refs[1 : 1 + arrived]
    unit_ref, radius_ref, grad_ref, loss_ref = refs[1 + arrived :]
    count, width = unit_ref.shape
    parts = blocks_of(width)
    total = held_ref[...]
    for ref in arrived_refs:
        total = total + ref[...].astype(f32)
    sums = []
    for which in range(4):
        row = 2 * parts * count + 2 * which
        sums.append((total[row : row + 1, :] + total[row + 1 : row + 2, :])[:, :count])
    pos, neg = sums[:2]
    loss_ref[...] = jnp.log(1.0 + pos) / pos_scale + jnp.log(1.0 + neg) / neg_scale
    scales = [to_column(1.0 / (1.0 + row)) for row in (neg, pos)]
    alongs = [to_column(row) for row in sums[2:]]
    unit = unit_ref[...]
    anchors = unit.astype(bf16).astype(f32)
    push, pull = [
        jnp.concatenate([total[(first + at) * count : (first + at + 1) * count, :] for at in range(parts)], axis=1)
        for first in (0, parts)
    ]
    grad_unit = (push + alongs[0] * anchors) * scales[0] - (pull + alongs[1] * anchors) * scales[1]
    along = jnp.sum(unit * grad_unit, axis=1, keepdims=True)
    grad_ref[...] = (grad_unit - unit * along) / radius_ref[:, :1]


def per_device(batch_rows, batch_labels, memory, memory_labels, keep_bits, step_index):
    groups = lax.axis_size("grp")
    members = lax.axis_size("dev")
    cores = 2 if members % 2 == 0 else 1
    line = members // cores
    count, width = batch_rows.shape
    slots = memory.shape[0]

    def exchange(value, axis, step):
        if axis == "grp":
            return lax.ppermute(value, "grp", [(i, i ^ step) for i in range(groups)])
        jump = step * cores if axis == "line" else step
        return lax.ppermute(value, "dev", [(i, i ^ jump) for i in range(members)])

    folded = (slots // lanes, lanes)
    parts = blocks_of(width)
    packed, unit, radius, slot_labels, copied_labels = call(
        prepare_kernel,
        [
            pltpu.VMEM((parts * count + 16, lanes), bf16),
            pltpu.VMEM((count, width), f32),
            pltpu.VMEM((count, lanes), f32),
            pltpu.VMEM(folded, jnp.int32),
            pltpu.VMEM(folded, jnp.int32),
        ],
        batch_rows, batch_labels.reshape(1, count), memory_labels.reshape(folded), keep_bits.reshape(folded),
        limit=vmem_most,
    )

    labels = [slot_labels] + [exchange(slot_labels, "core", s) for s in range(1, cores)]
    memories = [memory] + [exchange(memory, "core", s) for s in range(1, cores)]

    part = packed
    for s in range(line - 1, 0, -1):
        part = join([part, exchange(packed, "line", s)], labels if s == 1 else [])
    labels = [value.reshape(1, slots) for value in labels]
    blocks = [part] + [None] * (groups - 1)
    for s in range(groups - 1, 0, -1):
        blocks[s] = exchange(part, "grp", s)
    keys = [keys_of(memory, pltpu.HBM, [part])] + [keys_of(value, pltpu.VMEM, [part]) for value in memories[1:]]

    size = count * line
    arrived, after = [], []
    places = list(range(groups - 1, 0, -1))
    while places:
        now = places[:1] if not after else places[:2]
        places = places[len(now) :]
        after = block_sums([blocks[s] for s in now], keys, labels, count, bf16, after)
        arrived += [exchange(value, "grp", s) for s, value in zip(now, after)]
    held, copied = block_sums([part], keys, labels, count, f32, after, [memory])
    sizes = (count, slots, groups, line, cores)
    moved = pick(blocks, step_index, sizes, after)
    choices = [moved] + [exchange(moved, "core", s) for s in range(1, cores)]

    sums, *others = add(held, arrived, size, count, 2 * parts, choices)
    arrived = [exchange(value, "line", line - at) for at, value in enumerate(others, 1)]
    grad_batch, loss = call(
        functools.partial(finish_kernel, len(arrived)),
        [shaped((count, width), f32), shaped((1, count), f32)],
        sums, *arrived, unit, radius,
    )

    new_memory, new_labels = patch(copied, copied_labels, choices, step_index, sizes)
    return (grad_batch, loss.reshape(count), new_memory, new_labels.reshape(slots))


def solution(mesh):
    placed = (
        P(("grp", "dev"), None),
        P(("grp", "dev")),
        P(("grp", "dev"), None),
        P(("grp", "dev")),
        P(("grp", "dev")),
        P(),
    )
    return jax.shard_map(
        per_device,
        mesh=mesh,
        in_specs=placed,
        out_specs=(
            P(("grp", "dev"), None),
            P(("grp", "dev")),
            P(("grp", "dev"), None),
            P(("grp", "dev")),
        ),
        check_vma=False,
    )
```

```python
import functools
import math

import jax
import jax.numpy as jnp
from jax import lax
from jax.experimental import pallas as pl
from jax.experimental.pallas import tpu as pltpu
from jax.sharding import PartitionSpec as P

pos_scale = 2.0
neg_scale = 50.0
margin = 0.5
lanes = 128
log2e = math.log2(math.e)
vmem_bytes = 20 * 1024 * 1024
vmem_most = 56 * 1024 * 1024
f32 = jnp.float32
bf16 = jnp.bfloat16


def call(body, outs, *args, work=0, limit=vmem_bytes, **kw):
    return pl.pallas_call(
        body,
        out_shape=outs,
        compiler_params=pltpu.CompilerParams(vmem_limit_bytes=limit),
        cost_estimate=pl.CostEstimate(flops=work, bytes_accessed=0, transcendentals=0),
        **kw,
    )(*args)


def shaped(shape, dtype):
    return jax.ShapeDtypeStruct(shape, dtype)


def in_vmem(value):
    return pltpu.with_memory_space_constraint(value, pltpu.VMEM)


def rounded_up(value, unit):
    return (value + unit - 1) // unit * unit


def blocks_of(width):
    return width // lanes


def rows_as_lanes(parts, rows):
    row = lax.broadcasted_iota(jnp.int32, (rows, lanes), 0)
    out = jnp.zeros((rows, lanes), f32)
    for at, part in enumerate(parts):
        out = jnp.where(row == at, part, out)
    return out


def prepare_kernel(rows_ref, labels_ref, stored_ref, keep_ref, packed_ref, unit_ref, radius_ref, slot_ref):
    slot_ref[...] = jnp.where(keep_ref[...] > 0, stored_ref[...], -1)
    rows = rows_ref[...].astype(f32)
    count, width = rows.shape
    radius = jnp.sqrt(jnp.sum(rows * rows, axis=1, keepdims=True) + 1e-06)
    unit = rows / radius
    unit_ref[...] = unit
    radius_ref[...] = jnp.broadcast_to(radius, radius_ref.shape)
    anchors = unit.astype(bf16)
    for at in range(blocks_of(width)):
        packed_ref[at * count : (at + 1) * count, :] = anchors[:, at * lanes : (at + 1) * lanes]
    row = jnp.concatenate([labels_ref[...].astype(f32), jnp.zeros((1, lanes - count), f32)], axis=1)
    high = jnp.floor(row * (1.0 / 256.0))
    tail = packed_ref.shape[0] - blocks_of(width) * count
    packed_ref[blocks_of(width) * count :, :] = rows_as_lanes([high, row - high * 256.0], tail).astype(bf16)


def diagonal(count):
    across = lax.broadcasted_iota(jnp.int32, (count, count), 1)
    down = lax.broadcasted_iota(jnp.int32, (count, count), 0)
    return across == down


def to_column(row):
    count = row.shape[1]
    spread = jnp.broadcast_to(row, (count, count))
    return jnp.sum(jnp.where(diagonal(count), spread, 0.0), axis=1, keepdims=True)


def to_row(column):
    count = column.shape[0]
    spread = jnp.broadcast_to(column, (count, count))
    return jnp.sum(jnp.where(diagonal(count), spread, 0.0), axis=0, keepdims=True)


def keys_kernel(memory_ref, *refs):
    keys_ref = refs[-1]
    rows = memory_ref[...].astype(f32)
    radius = jnp.sqrt(jnp.sum(rows * rows, axis=1, keepdims=True) + 1e-06)
    keys_ref[...] = (rows / radius).astype(bf16)


def keys_of(memory, place, after):
    slots, width = memory.shape
    block = math.gcd(512, slots)
    spec = pl.BlockSpec((block, width), lambda i: (i, 0))
    return call(
        keys_kernel,
        [shaped((slots, width), bf16)],
        pltpu.with_memory_space_constraint(memory, place), *after,
        work=64 * slots * width * width,
        grid=(slots // block,),
        in_specs=[spec] + [pl.BlockSpec(memory_space=pl.ANY)] * len(after),
        out_specs=[spec],
    )[0]


def join_kernel(blocks, *refs):
    block_refs, out_ref = refs[:blocks], refs[-1]
    first = 0
    for ref in block_refs:
        out_ref[first : first + ref.shape[0], :] = ref[...]
        first += ref.shape[0]


def join(blocks, after):
    rows = sum(block.shape[0] for block in blocks)
    return call(
        functools.partial(join_kernel, len(blocks)),
        [shaped((rows, blocks[0].shape[1]), blocks[0].dtype)],
        *blocks, *after,
        in_specs=[pl.BlockSpec(memory_space=pltpu.VMEM)] * len(blocks)
        + [pl.BlockSpec(memory_space=pl.ANY)] * len(after),
    )[0]


def positions(step, count, slots, groups, line, cores):
    first = lax.rem(step, slots // count) * count
    crossing = lax.rem(step, cores)
    members = line * cores
    devices_all = groups * members
    grp = lax.axis_index("grp")
    dev = lax.axis_index("dev")
    target = grp * members + (dev ^ crossing)
    source = lax.rem(target + devices_all - lax.rem(step, devices_all), devices_all)
    source_grp = lax.div(source, members)
    source_line = lax.div(lax.rem(source, members), cores)
    step = lax.div(dev, cores) ^ source_line
    return first, crossing, grp ^ source_grp, lax.rem(line - step, line)


def pick_kernel(groups, sizes, step_ref, *refs):
    blocks_refs, out_ref = refs[:groups], refs[-1]
    rows = out_ref.shape[0]
    _, _, grp_place, line_place = positions(step_ref[0], *sizes)
    for place, ref in enumerate(blocks_refs):

        @pl.when(grp_place == place)
        def _():
            out_ref[...] = ref[pl.ds(pl.multiple_of(line_place * rows, 16), rows), :]


def pick(blocks, step, sizes, after):
    line = sizes[3]
    return call(
        functools.partial(pick_kernel, len(blocks), sizes),
        [shaped((blocks[0].shape[0] // line, lanes), bf16)],
        step, *blocks, *after,
        in_specs=[pl.BlockSpec(memory_space=pltpu.SMEM)]
        + [pl.BlockSpec(memory_space=pltpu.VMEM)] * len(blocks)
        + [pl.BlockSpec(memory_space=pl.ANY)] * len(after),
    )[0]


def patch_kernel(choices, sizes, step_ref, stored_ref, labels_ref, *refs):
    moved_refs, (memory_ref, new_labels_ref, rows_ref, sem) = refs[:choices], refs[choices:]
    count, width = rows_ref.shape
    first, crossing, _, _ = positions(step_ref[0], *sizes)
    moved = moved_refs[0][...]
    for choice in range(1, choices):
        moved = jnp.where(crossing == choice, moved_refs[choice][...], moved)
    for at in range(blocks_of(width)):
        rows_ref[:, at * lanes : (at + 1) * lanes] = moved[at * count : (at + 1) * count, :]
    target = memory_ref.at[pl.ds(pl.multiple_of(first, count), count), :]
    copy = pltpu.make_async_copy(rows_ref, target, sem)
    copy.start()
    digits = moved[blocks_of(width) * count :, :].astype(f32)
    row = (digits[0:1, :] * 256.0 + digits[1:2, :]).astype(jnp.int32)
    old = labels_ref[...]
    turned = pltpu.roll(jnp.broadcast_to(row, old.shape), lax.rem(first, lanes), 1)
    slot = lax.broadcasted_iota(jnp.int32, old.shape, 0) * lanes + lax.broadcasted_iota(jnp.int32, old.shape, 1)
    new_labels_ref[...] = jnp.where((slot >= first) & (slot < first + count), turned, old)
    copy.wait()


def patch(stored, labels, choices, step, sizes):
    count, width = sizes[0], stored.shape[1]
    return call(
        functools.partial(patch_kernel, len(choices), sizes),
        [shaped(stored.shape, bf16), shaped(labels.shape, jnp.int32)],
        step, stored, labels, *choices,
        in_specs=[pl.BlockSpec(memory_space=pltpu.SMEM), pl.BlockSpec(memory_space=pl.ANY)]
        + [pl.BlockSpec(memory_space=pltpu.VMEM)] * (1 + len(choices)),
        out_specs=[pl.BlockSpec(memory_space=pl.ANY), pl.BlockSpec(memory_space=pltpu.VMEM)],
        scratch_shapes=[pltpu.VMEM((count, width), bf16), pltpu.SemaphoreType.DMA],
        input_output_aliases={1: 0},
    )


def split_digits(row):
    high = row.astype(bf16).astype(f32)
    return [high, row - high]


def sum_rows(size):
    return rounded_up(8 * (rounded_up(size, lanes) // lanes), 16)


def block_kernel(blocks, sides, unit, count, copies, scratch, *refs):
    if copies:
        source_ref, target_ref, sem = refs[blocks + 2 * sides], refs[-scratch - 1], refs[-1]
        copy = pltpu.make_async_copy(source_ref, target_ref, sem)
        copy.start()
        refs = refs[: -scratch - 1] + refs[-scratch : -1]
        scratch -= 1
    rows_refs, keys_refs = refs[:blocks], refs[blocks : blocks + sides]
    label_refs = refs[blocks + sides : blocks + 2 * sides]
    out_refs = refs[-scratch - blocks : -scratch]
    anchors_ref, labels_ref, total_ref, pos_ref, neg_ref = refs[-scratch:-4]
    scores_refs, weight_refs = refs[-4:-2], refs[-2:]
    slots, width = keys_refs[0].shape
    parts = blocks_of(width)
    packed = rows_refs[0].shape[0]
    members = packed // (parts * count + 16)
    size = members * count
    columns = []
    for block, ref in enumerate(rows_refs):
        for member in range(members):
            first = member * (parts * count + 16)
            to = block * size + member * count
            for at in range(parts):
                anchors_ref[to : to + count, at * lanes : (at + 1) * lanes] = ref[
                    first + at * count : first + (at + 1) * count, :
                ]
            digits = ref[first + parts * count : first + parts * count + 16, :].astype(f32)
            columns.append(to_column((digits[0:1, :] * 256.0 + digits[1:2, :])[:, :count]))
    rows = blocks * size
    labels_ref[...] = jnp.broadcast_to(jnp.concatenate(columns, axis=0), labels_ref.shape)
    pos_ref[...] = jnp.zeros_like(pos_ref)
    neg_ref[...] = jnp.zeros_like(neg_ref)
    anchors = anchors_ref[...]
    units = [(side, at) for side in range(sides) for at in range(0, slots, unit)]
    longest = 4 if blocks == 1 else 2
    runs = []
    for side in range(sides):
        left = slots // unit
        while left:
            length = min(longest, left)
            if blocks == 1 and side == sides - 1 and length == left and left > 1:
                length -= 1
            runs.append(length)
            left -= length
    starts = [sum(runs[:run]) for run in range(len(runs))]
    run_of = [run for run, length in enumerate(runs) for _ in range(length)]
    cuts = max(rows // 32, 4)
    quarter = rows // cuts

    def score_unit(at):
        side, first = units[at]
        scores_refs[at % 2][...] = lax.dot_general(
            anchors, keys_refs[side][first : first + unit, :], (((1,), (1,)), ((), ())), preferred_element_type=f32
        )

    def term_unit(at, which):
        side, first = units[at]
        part = slice(which * quarter, (which + 1) * quarter)
        weights_ref = weight_refs[run_of[at] % 2]
        base = (at - starts[run_of[at]]) * unit
        wanted = labels_ref[part, :]
        pos_sum, neg_sum = pos_ref[part, :], neg_ref[part, :]
        for piece in range(0, unit, lanes):
            slot_labels = label_refs[side][:, first + piece : first + piece + lanes].astype(f32)
            neg_shift = jnp.where(slot_labels < 0.0, -1e30, -neg_scale * margin * log2e)
            same = wanted == slot_labels
            slope = jnp.where(same, -pos_scale * log2e, neg_scale * log2e)
            shift = jnp.where(same, pos_scale * margin * log2e, neg_shift)
            term = jnp.exp2(scores_refs[at % 2][part, piece : piece + lanes] * slope + shift)
            pos = jnp.where(same, term, 0.0)
            neg = jnp.where(same, 0.0, term)
            pos_sum += pos
            neg_sum += neg
            to = slice(base + piece, base + piece + lanes)
            weights_ref[part, to] = neg.astype(bf16)
            weights_ref[rows + which * quarter : rows + (which + 1) * quarter, to] = pos.astype(bf16)
        pos_ref[part, :] = pos_sum
        neg_ref[part, :] = neg_sum

    def weigh_half(run, half):
        side, first = units[starts[run]]
        span = runs[run] * unit
        part = slice(half * (width // 2), (half + 1) * (width // 2))
        more = jnp.dot(
            weight_refs[run % 2][:, :span], keys_refs[side][first : first + span, part], preferred_element_type=f32
        )
        total_ref[:, part] = more if run == 0 else total_ref[:, part] + more

    score_unit(0)
    waiting = []
    for at in range(len(units)):
        if at in starts and at:
            waiting += [(run_of[at] - 1, 0), (run_of[at] - 1, 1)]
        left = runs[run_of[at]] - (at - starts[run_of[at]])
        now, waiting = waiting[: -(-len(waiting) // left)], waiting[-(-len(waiting) // left) :]
        for which in range(cuts):
            if which == cuts // 4 and at + 1 < len(units):
                score_unit(at + 1)
            if which == cuts - cuts // 4:
                for run, half in now:
                    weigh_half(run, half)
            term_unit(at, which)
    weigh_half(len(runs) - 1, 0)
    weigh_half(len(runs) - 1, 1)
    total = total_ref[...]
    pos_sum = jnp.sum(pos_ref[...], axis=1, keepdims=True)
    neg_sum = jnp.sum(neg_ref[...], axis=1, keepdims=True)
    floats = anchors.astype(f32)
    sums = [pos_sum, neg_sum]
    for which in range(2):
        value = total[which * rows : (which + 1) * rows, :]
        along = jnp.sum(value * floats, axis=1, keepdims=True)
        sums.append(along)
        rest = value - along * floats
        for block, ref in enumerate(out_refs):
            for at in range(parts):
                first = (which * parts + at) * size
                ref[first : first + size, :] = rest[
                    block * size : (block + 1) * size, at * lanes : (at + 1) * lanes
                ].astype(ref.dtype)
    for block, ref in enumerate(out_refs):
        lines = []
        for first in range(0, size, lanes):
            last = min(first + lanes, size)
            for value in sums:
                row = to_row(value[block * size + first : block * size + last])
                if last - first < lanes:
                    row = jnp.concatenate([row, jnp.zeros((1, lanes - last + first), f32)], axis=1)
                lines += split_digits(row)
        first = 2 * parts * size
        ref[first:, :] = rows_as_lanes(lines, ref.shape[0] - first).astype(ref.dtype)
    if copies:
        copy.wait()


def block_sums(blocks, keys, labels, count, dtype, after, copied=()):
    slots, width = keys[0].shape
    parts = blocks_of(width)
    size = blocks[0].shape[0] // (parts * count + 16) * count
    rows = len(blocks) * size
    unit = math.gcd(256, slots // 2)
    anywhere = pl.BlockSpec(memory_space=pl.ANY)
    vmem = pl.BlockSpec(memory_space=pltpu.VMEM)
    return call(
        functools.partial(block_kernel, len(blocks), len(keys), unit, count, len(copied), 9 + len(copied)),
        [shaped((2 * parts * size + sum_rows(size), lanes), dtype)] * len(blocks)
        + [shaped(value.shape, value.dtype) for value in copied],
        *blocks, *[in_vmem(k) for k in keys], *labels, *copied, *after,
        work=12 * size * len(blocks) * slots * len(keys) * width,
        in_specs=[vmem] * (len(blocks) + 2 * len(keys)) + [anywhere] * (len(copied) + len(after)),
        out_specs=[vmem] * len(blocks) + [anywhere] * len(copied),
        scratch_shapes=[
            pltpu.VMEM((rows, width), bf16),
            pltpu.VMEM((rows, lanes), f32),
            pltpu.VMEM((2 * rows, width), f32),
            pltpu.VMEM((rows, lanes), f32),
            pltpu.VMEM((rows, lanes), f32),
            pltpu.VMEM((rows, unit), f32),
            pltpu.VMEM((rows, unit), f32),
            pltpu.VMEM((2 * rows, (4 if len(blocks) == 1 else 2) * unit), bf16),
            pltpu.VMEM((2 * rows, (4 if len(blocks) == 1 else 2) * unit), bf16),
        ]
        + [pltpu.SemaphoreType.DMA] * len(copied),
    )


def add_kernel(arrived, size, count, *refs):
    in_refs, out_refs = refs[: 1 + arrived], refs[-(size // count) :]
    columns = (in_refs[0].shape[0] - sum_rows(size)) // size

    def total(first, rows):
        value = in_refs[0][first : first + rows, :]
        for ref in in_refs[1:]:
            value = value + ref[first : first + rows, :].astype(f32)
        return value

    sums = total(columns * size, sum_rows(size))
    for block, ref in enumerate(out_refs):
        for at in range(columns):
            part = total(at * size + block * count, count)
            ref[at * count : (at + 1) * count, :] = part.astype(ref.dtype)
        group, lane = divmod(block * count, lanes)
        lines = []
        for which in range(4):
            row = 8 * group + 2 * which
            lines += split_digits(sums[row : row + 1, :] + sums[row + 1 : row + 2, :])
        packed = rows_as_lanes(lines, ref.shape[0] - columns * count)
        if lane:
            packed = pltpu.roll(packed, lanes - lane, 1)
        ref[columns * count :, :] = packed.astype(ref.dtype)


def add(held, arrived, size, count, columns, after):
    shape = (columns * count + sum_rows(count), lanes)
    outs = [shaped(shape, f32 if b == 0 else bf16) for b in range(size // count)]
    return call(
        functools.partial(add_kernel, len(arrived), size, count),
        outs,
        held, *arrived, *after,
        in_specs=[pl.BlockSpec(memory_space=pltpu.VMEM)] * (1 + len(arrived))
        + [pl.BlockSpec(memory_space=pl.ANY)] * len(after),
    )


def finish_kernel(arrived, *refs):
    held_ref, arrived_refs = refs[0], refs[1 : 1 + arrived]
    unit_ref, radius_ref, grad_ref, loss_ref = refs[1 + arrived :]
    count, width = unit_ref.shape
    parts = blocks_of(width)
    total = held_ref[...]
    for ref in arrived_refs:
        total = total + ref[...].astype(f32)
    sums = []
    for which in range(4):
        row = 2 * parts * count + 2 * which
        sums.append((total[row : row + 1, :] + total[row + 1 : row + 2, :])[:, :count])
    pos, neg = sums[:2]
    loss_ref[...] = jnp.log(1.0 + pos) / pos_scale + jnp.log(1.0 + neg) / neg_scale
    scales = [to_column(1.0 / (1.0 + row)) for row in (neg, pos)]
    alongs = [to_column(row) for row in sums[2:]]
    unit = unit_ref[...]
    anchors = unit.astype(bf16).astype(f32)
    push, pull = [
        jnp.concatenate([total[(first + at) * count : (first + at + 1) * count, :] for at in range(parts)], axis=1)
        for first in (0, parts)
    ]
    grad_unit = (push + alongs[0] * anchors) * scales[0] - (pull + alongs[1] * anchors) * scales[1]
    along = jnp.sum(unit * grad_unit, axis=1, keepdims=True)
    grad_ref[...] = (grad_unit - unit * along) / radius_ref[:, :1]


def per_device(batch_rows, batch_labels, memory, memory_labels, keep_bits, step_index):
    groups = lax.axis_size("grp")
    members = lax.axis_size("dev")
    cores = 2 if members % 2 == 0 else 1
    line = members // cores
    count, width = batch_rows.shape
    slots = memory.shape[0]

    def exchange(value, axis, step):
        if axis == "grp":
            return lax.ppermute(value, "grp", [(i, i ^ step) for i in range(groups)])
        jump = step * cores if axis == "line" else step
        return lax.ppermute(value, "dev", [(i, i ^ jump) for i in range(members)])

    folded = (slots // lanes, lanes)
    parts = blocks_of(width)
    packed, unit, radius, slot_labels = call(
        prepare_kernel,
        [
            pltpu.VMEM((parts * count + 16, lanes), bf16),
            pltpu.VMEM((count, width), f32),
            pltpu.VMEM((count, lanes), f32),
            pltpu.VMEM(folded, jnp.int32),
        ],
        batch_rows, batch_labels.reshape(1, count), memory_labels.reshape(folded), keep_bits.reshape(folded),
        limit=vmem_most,
    )

    labels = [slot_labels] + [exchange(slot_labels, "core", s) for s in range(1, cores)]
    memories = [memory] + [exchange(memory, "core", s) for s in range(1, cores)]

    part = packed
    for s in range(line - 1, 0, -1):
        part = join([part, exchange(packed, "line", s)], labels if s == 1 else [])
    labels = [value.reshape(1, slots) for value in labels]
    blocks = [part] + [None] * (groups - 1)
    for s in range(groups - 1, 0, -1):
        blocks[s] = exchange(part, "grp", s)
    keys = [keys_of(memory, pltpu.HBM, [part])] + [keys_of(value, pltpu.VMEM, [part]) for value in memories[1:]]

    size = count * line
    arrived, after = [], []
    places = list(range(groups - 1, 0, -1))
    while places:
        now = places[:1] if not after else places[:2]
        places = places[len(now) :]
        after = block_sums([blocks[s] for s in now], keys, labels, count, bf16, after)
        arrived += [exchange(value, "grp", s) for s, value in zip(now, after)]
    held, copied = block_sums([part], keys, labels, count, f32, after, [memory])
    sizes = (count, slots, groups, line, cores)
    moved = pick(blocks, step_index, sizes, after)
    choices = [moved] + [exchange(moved, "core", s) for s in range(1, cores)]

    sums, *others = add(held, arrived, size, count, 2 * parts, choices)
    arrived = [exchange(value, "line", line - at) for at, value in enumerate(others, 1)]
    grad_batch, loss = call(
        functools.partial(finish_kernel, len(arrived)),
        [shaped((count, width), f32), shaped((1, count), f32)],
        sums, *arrived, unit, radius,
    )

    new_memory, new_labels = patch(copied, memory_labels.reshape(folded), choices, step_index, sizes)
    return (grad_batch, loss.reshape(count), new_memory, new_labels.reshape(slots))


def solution(mesh):
    placed = (
        P(("grp", "dev"), None),
        P(("grp", "dev")),
        P(("grp", "dev"), None),
        P(("grp", "dev")),
        P(("grp", "dev")),
        P(),
    )
    return jax.shard_map(
        per_device,
        mesh=mesh,
        in_specs=placed,
        out_specs=(
            P(("grp", "dev"), None),
            P(("grp", "dev")),
            P(("grp", "dev"), None),
            P(("grp", "dev")),
        ),
        check_vma=False,
    )
```

```python
import functools
import math

import jax
import jax.numpy as jnp
from jax import lax
from jax.experimental import pallas as pl
from jax.experimental.pallas import tpu as pltpu
from jax.sharding import PartitionSpec as P

pos_scale = 2.0
neg_scale = 50.0
margin = 0.5
lanes = 128
log2e = math.log2(math.e)
vmem_bytes = 20 * 1024 * 1024
vmem_most = 56 * 1024 * 1024
f32 = jnp.float32
bf16 = jnp.bfloat16


def call(body, outs, *args, work=0, limit=vmem_bytes, **kw):
    return pl.pallas_call(
        body,
        out_shape=outs,
        compiler_params=pltpu.CompilerParams(vmem_limit_bytes=limit),
        cost_estimate=pl.CostEstimate(flops=work, bytes_accessed=0, transcendentals=0),
        **kw,
    )(*args)


def shaped(shape, dtype):
    return jax.ShapeDtypeStruct(shape, dtype)


def in_vmem(value):
    return pltpu.with_memory_space_constraint(value, pltpu.VMEM)


def rounded_up(value, unit):
    return (value + unit - 1) // unit * unit


def blocks_of(width):
    return width // lanes


def rows_as_lanes(parts, rows):
    row = lax.broadcasted_iota(jnp.int32, (rows, lanes), 0)
    out = jnp.zeros((rows, lanes), f32)
    for at, part in enumerate(parts):
        out = jnp.where(row == at, part, out)
    return out


def prepare_kernel(rows_ref, labels_ref, stored_ref, keep_ref, packed_ref, unit_ref, radius_ref, slot_ref):
    slot_ref[...] = jnp.where(keep_ref[...] > 0, stored_ref[...], -1)
    rows = rows_ref[...].astype(f32)
    count, width = rows.shape
    radius = jnp.sqrt(jnp.sum(rows * rows, axis=1, keepdims=True) + 1e-06)
    unit = rows / radius
    unit_ref[...] = unit
    radius_ref[...] = jnp.broadcast_to(radius, radius_ref.shape)
    anchors = unit.astype(bf16)
    for at in range(blocks_of(width)):
        packed_ref[at * count : (at + 1) * count, :] = anchors[:, at * lanes : (at + 1) * lanes]
    row = jnp.concatenate([labels_ref[...].astype(f32), jnp.zeros((1, lanes - count), f32)], axis=1)
    high = jnp.floor(row * (1.0 / 256.0))
    tail = packed_ref.shape[0] - blocks_of(width) * count
    packed_ref[blocks_of(width) * count :, :] = rows_as_lanes([high, row - high * 256.0], tail).astype(bf16)


def diagonal(count):
    across = lax.broadcasted_iota(jnp.int32, (count, count), 1)
    down = lax.broadcasted_iota(jnp.int32, (count, count), 0)
    return across == down


def to_column(row):
    count = row.shape[1]
    spread = jnp.broadcast_to(row, (count, count))
    return jnp.sum(jnp.where(diagonal(count), spread, 0.0), axis=1, keepdims=True)


def to_row(column):
    count = column.shape[0]
    spread = jnp.broadcast_to(column, (count, count))
    return jnp.sum(jnp.where(diagonal(count), spread, 0.0), axis=0, keepdims=True)


def keys_kernel(memory_ref, *refs):
    keys_ref = refs[-1]
    rows = memory_ref[...].astype(f32)
    radius = jnp.sqrt(jnp.sum(rows * rows, axis=1, keepdims=True) + 1e-06)
    keys_ref[...] = (rows / radius).astype(bf16)


def keys_of(memory, place, after):
    slots, width = memory.shape
    block = math.gcd(256 if place == pltpu.HBM else 512, slots)
    spec = pl.BlockSpec((block, width), lambda i: (i, 0))
    return call(
        keys_kernel,
        [shaped((slots, width), bf16)],
        pltpu.with_memory_space_constraint(memory, place), *after,
        work=64 * slots * width * width,
        grid=(slots // block,),
        in_specs=[spec] + [pl.BlockSpec(memory_space=pl.ANY)] * len(after),
        out_specs=[spec],
    )[0]


def join_kernel(blocks, *refs):
    block_refs, out_ref = refs[:blocks], refs[-1]
    first = 0
    for ref in block_refs:
        out_ref[first : first + ref.shape[0], :] = ref[...]
        first += ref.shape[0]


def join(blocks, after):
    rows = sum(block.shape[0] for block in blocks)
    return call(
        functools.partial(join_kernel, len(blocks)),
        [shaped((rows, blocks[0].shape[1]), blocks[0].dtype)],
        *blocks, *after,
        in_specs=[pl.BlockSpec(memory_space=pltpu.VMEM)] * len(blocks)
        + [pl.BlockSpec(memory_space=pl.ANY)] * len(after),
    )[0]


def positions(step, count, slots, groups, line, cores):
    first = lax.rem(step, slots // count) * count
    crossing = lax.rem(step, cores)
    members = line * cores
    devices_all = groups * members
    grp = lax.axis_index("grp")
    dev = lax.axis_index("dev")
    target = grp * members + (dev ^ crossing)
    source = lax.rem(target + devices_all - lax.rem(step, devices_all), devices_all)
    source_grp = lax.div(source, members)
    source_line = lax.div(lax.rem(source, members), cores)
    step = lax.div(dev, cores) ^ source_line
    return first, crossing, grp ^ source_grp, lax.rem(line - step, line)


def pick_kernel(groups, sizes, step_ref, *refs):
    blocks_refs, out_ref = refs[:groups], refs[-1]
    rows = out_ref.shape[0]
    _, _, grp_place, line_place = positions(step_ref[0], *sizes)
    for place, ref in enumerate(blocks_refs):

        @pl.when(grp_place == place)
        def _():
            out_ref[...] = ref[pl.ds(pl.multiple_of(line_place * rows, 16), rows), :]


def pick(blocks, step, sizes, after):
    line = sizes[3]
    return call(
        functools.partial(pick_kernel, len(blocks), sizes),
        [shaped((blocks[0].shape[0] // line, lanes), bf16)],
        step, *blocks, *after,
        in_specs=[pl.BlockSpec(memory_space=pltpu.SMEM)]
        + [pl.BlockSpec(memory_space=pltpu.VMEM)] * len(blocks)
        + [pl.BlockSpec(memory_space=pl.ANY)] * len(after),
    )[0]


def patch_kernel(choices, sizes, step_ref, stored_ref, labels_ref, *refs):
    moved_refs, (memory_ref, new_labels_ref, rows_ref, sem) = refs[:choices], refs[choices:]
    count, width = rows_ref.shape
    first, crossing, _, _ = positions(step_ref[0], *sizes)
    moved = moved_refs[0][...]
    for choice in range(1, choices):
        moved = jnp.where(crossing == choice, moved_refs[choice][...], moved)
    for at in range(blocks_of(width)):
        rows_ref[:, at * lanes : (at + 1) * lanes] = moved[at * count : (at + 1) * count, :]
    target = memory_ref.at[pl.ds(pl.multiple_of(first, count), count), :]
    copy = pltpu.make_async_copy(rows_ref, target, sem)
    copy.start()
    digits = moved[blocks_of(width) * count :, :].astype(f32)
    row = (digits[0:1, :] * 256.0 + digits[1:2, :]).astype(jnp.int32)
    old = labels_ref[...]
    turned = pltpu.roll(jnp.broadcast_to(row, old.shape), lax.rem(first, lanes), 1)
    slot = lax.broadcasted_iota(jnp.int32, old.shape, 0) * lanes + lax.broadcasted_iota(jnp.int32, old.shape, 1)
    new_labels_ref[...] = jnp.where((slot >= first) & (slot < first + count), turned, old)
    copy.wait()


def patch(stored, labels, choices, step, sizes):
    count, width = sizes[0], stored.shape[1]
    return call(
        functools.partial(patch_kernel, len(choices), sizes),
        [shaped(stored.shape, bf16), shaped(labels.shape, jnp.int32)],
        step, stored, labels, *choices,
        in_specs=[pl.BlockSpec(memory_space=pltpu.SMEM), pl.BlockSpec(memory_space=pl.ANY)]
        + [pl.BlockSpec(memory_space=pltpu.VMEM)] * (1 + len(choices)),
        out_specs=[pl.BlockSpec(memory_space=pl.ANY), pl.BlockSpec(memory_space=pltpu.VMEM)],
        scratch_shapes=[pltpu.VMEM((count, width), bf16), pltpu.SemaphoreType.DMA],
        input_output_aliases={1: 0},
    )


def split_digits(row):
    high = row.astype(bf16).astype(f32)
    return [high, row - high]


def sum_rows(size):
    return rounded_up(8 * (rounded_up(size, lanes) // lanes), 16)


def block_kernel(blocks, sides, unit, count, copies, scratch, *refs):
    if copies:
        source_ref, target_ref, sem = refs[blocks + 2 * sides], refs[-scratch - 1], refs[-1]
        copy = pltpu.make_async_copy(source_ref, target_ref, sem)
        copy.start()
        refs = refs[: -scratch - 1] + refs[-scratch : -1]
        scratch -= 1
    rows_refs, keys_refs = refs[:blocks], refs[blocks : blocks + sides]
    label_refs = refs[blocks + sides : blocks + 2 * sides]
    out_refs = refs[-scratch - blocks : -scratch]
    anchors_ref, labels_ref, total_ref, pos_ref, neg_ref = refs[-scratch:-4]
    scores_refs, weight_refs = refs[-4:-2], refs[-2:]
    slots, width = keys_refs[0].shape
    parts = blocks_of(width)
    packed = rows_refs[0].shape[0]
    members = packed // (parts * count + 16)
    size = members * count
    columns = []
    for block, ref in enumerate(rows_refs):
        for member in range(members):
            first = member * (parts * count + 16)
            to = block * size + member * count
            for at in range(parts):
                anchors_ref[to : to + count, at * lanes : (at + 1) * lanes] = ref[
                    first + at * count : first + (at + 1) * count, :
                ]
            digits = ref[first + parts * count : first + parts * count + 16, :].astype(f32)
            columns.append(to_column((digits[0:1, :] * 256.0 + digits[1:2, :])[:, :count]))
    rows = blocks * size
    labels_ref[...] = jnp.broadcast_to(jnp.concatenate(columns, axis=0), labels_ref.shape)
    pos_ref[...] = jnp.zeros_like(pos_ref)
    neg_ref[...] = jnp.zeros_like(neg_ref)
    anchors = anchors_ref[...]
    units = [(side, at) for side in range(sides) for at in range(0, slots, unit)]
    longest = 4 if blocks == 1 else 2
    runs = []
    for side in range(sides):
        left = slots // unit
        while left:
            length = min(longest, left)
            if blocks == 1 and side == sides - 1 and length == left and left > 1:
                length -= 1
            runs.append(length)
            left -= length
    starts = [sum(runs[:run]) for run in range(len(runs))]
    run_of = [run for run, length in enumerate(runs) for _ in range(length)]
    cuts = max(rows // 32, 4)
    quarter = rows // cuts

    def score_unit(at):
        side, first = units[at]
        scores_refs[at % 2][...] = lax.dot_general(
            anchors, keys_refs[side][first : first + unit, :], (((1,), (1,)), ((), ())), preferred_element_type=f32
        )

    def term_unit(at, which):
        side, first = units[at]
        part = slice(which * quarter, (which + 1) * quarter)
        weights_ref = weight_refs[run_of[at] % 2]
        base = (at - starts[run_of[at]]) * unit
        wanted = labels_ref[part, :]
        pos_sum, neg_sum = pos_ref[part, :], neg_ref[part, :]
        for piece in range(0, unit, lanes):
            slot_labels = label_refs[side][:, first + piece : first + piece + lanes].astype(f32)
            neg_shift = jnp.where(slot_labels < 0.0, -1e30, -neg_scale * margin * log2e)
            same = wanted == slot_labels
            slope = jnp.where(same, -pos_scale * log2e, neg_scale * log2e)
            shift = jnp.where(same, pos_scale * margin * log2e, neg_shift)
            term = jnp.exp2(scores_refs[at % 2][part, piece : piece + lanes] * slope + shift)
            pos = jnp.where(same, term, 0.0)
            neg = jnp.where(same, 0.0, term)
            pos_sum += pos
            neg_sum += neg
            to = slice(base + piece, base + piece + lanes)
            weights_ref[part, to] = neg.astype(bf16)
            weights_ref[rows + which * quarter : rows + (which + 1) * quarter, to] = pos.astype(bf16)
        pos_ref[part, :] = pos_sum
        neg_ref[part, :] = neg_sum

    def weigh_half(run, half):
        side, first = units[starts[run]]
        span = runs[run] * unit
        part = slice(half * (width // 2), (half + 1) * (width // 2))
        more = jnp.dot(
            weight_refs[run % 2][:, :span], keys_refs[side][first : first + span, part], preferred_element_type=f32
        )
        total_ref[:, part] = more if run == 0 else total_ref[:, part] + more

    score_unit(0)
    waiting = []
    for at in range(len(units)):
        if at in starts and at:
            waiting += [(run_of[at] - 1, 0), (run_of[at] - 1, 1)]
        left = runs[run_of[at]] - (at - starts[run_of[at]])
        now, waiting = waiting[: -(-len(waiting) // left)], waiting[-(-len(waiting) // left) :]
        for which in range(cuts):
            if which == cuts // 4 and at + 1 < len(units):
                score_unit(at + 1)
            if which == cuts - cuts // 4:
                for run, half in now:
                    weigh_half(run, half)
            term_unit(at, which)
    weigh_half(len(runs) - 1, 0)
    weigh_half(len(runs) - 1, 1)
    total = total_ref[...]
    pos_sum = jnp.sum(pos_ref[...], axis=1, keepdims=True)
    neg_sum = jnp.sum(neg_ref[...], axis=1, keepdims=True)
    floats = anchors.astype(f32)
    sums = [pos_sum, neg_sum]
    for which in range(2):
        value = total[which * rows : (which + 1) * rows, :]
        along = jnp.sum(value * floats, axis=1, keepdims=True)
        sums.append(along)
        rest = value - along * floats
        for block, ref in enumerate(out_refs):
            for at in range(parts):
                first = (which * parts + at) * size
                ref[first : first + size, :] = rest[
                    block * size : (block + 1) * size, at * lanes : (at + 1) * lanes
                ].astype(ref.dtype)
    for block, ref in enumerate(out_refs):
        lines = []
        for first in range(0, size, lanes):
            last = min(first + lanes, size)
            for value in sums:
                row = to_row(value[block * size + first : block * size + last])
                if last - first < lanes:
                    row = jnp.concatenate([row, jnp.zeros((1, lanes - last + first), f32)], axis=1)
                lines += split_digits(row)
        first = 2 * parts * size
        ref[first:, :] = rows_as_lanes(lines, ref.shape[0] - first).astype(ref.dtype)
    if copies:
        copy.wait()


def block_sums(blocks, keys, labels, count, dtype, after, copied=()):
    slots, width = keys[0].shape
    parts = blocks_of(width)
    size = blocks[0].shape[0] // (parts * count + 16) * count
    rows = len(blocks) * size
    unit = math.gcd(256, slots // 2)
    anywhere = pl.BlockSpec(memory_space=pl.ANY)
    vmem = pl.BlockSpec(memory_space=pltpu.VMEM)
    return call(
        functools.partial(block_kernel, len(blocks), len(keys), unit, count, len(copied), 9 + len(copied)),
        [shaped((2 * parts * size + sum_rows(size), lanes), dtype)] * len(blocks)
        + [shaped(value.shape, value.dtype) for value in copied],
        *blocks, *[in_vmem(k) for k in keys], *labels, *copied, *after,
        work=12 * size * len(blocks) * slots * len(keys) * width,
        in_specs=[vmem] * (len(blocks) + 2 * len(keys)) + [anywhere] * (len(copied) + len(after)),
        out_specs=[vmem] * len(blocks) + [anywhere] * len(copied),
        scratch_shapes=[
            pltpu.VMEM((rows, width), bf16),
            pltpu.VMEM((rows, lanes), f32),
            pltpu.VMEM((2 * rows, width), f32),
            pltpu.VMEM((rows, lanes), f32),
            pltpu.VMEM((rows, lanes), f32),
            pltpu.VMEM((rows, unit), f32),
            pltpu.VMEM((rows, unit), f32),
            pltpu.VMEM((2 * rows, (4 if len(blocks) == 1 else 2) * unit), bf16),
            pltpu.VMEM((2 * rows, (4 if len(blocks) == 1 else 2) * unit), bf16),
        ]
        + [pltpu.SemaphoreType.DMA] * len(copied),
    )


def add_kernel(arrived, size, count, *refs):
    in_refs, out_refs = refs[: 1 + arrived], refs[-(size // count) :]
    columns = (in_refs[0].shape[0] - sum_rows(size)) // size

    def total(first, rows):
        value = in_refs[0][first : first + rows, :]
        for ref in in_refs[1:]:
            value = value + ref[first : first + rows, :].astype(f32)
        return value

    sums = total(columns * size, sum_rows(size))
    for block, ref in enumerate(out_refs):
        for at in range(columns):
            part = total(at * size + block * count, count)
            ref[at * count : (at + 1) * count, :] = part.astype(ref.dtype)
        group, lane = divmod(block * count, lanes)
        lines = []
        for which in range(4):
            row = 8 * group + 2 * which
            lines += split_digits(sums[row : row + 1, :] + sums[row + 1 : row + 2, :])
        packed = rows_as_lanes(lines, ref.shape[0] - columns * count)
        if lane:
            packed = pltpu.roll(packed, lanes - lane, 1)
        ref[columns * count :, :] = packed.astype(ref.dtype)


def add(held, arrived, size, count, columns, after):
    shape = (columns * count + sum_rows(count), lanes)
    outs = [shaped(shape, f32 if b == 0 else bf16) for b in range(size // count)]
    return call(
        functools.partial(add_kernel, len(arrived), size, count),
        outs,
        held, *arrived, *after,
        in_specs=[pl.BlockSpec(memory_space=pltpu.VMEM)] * (1 + len(arrived))
        + [pl.BlockSpec(memory_space=pl.ANY)] * len(after),
    )


def finish_kernel(arrived, *refs):
    held_ref, arrived_refs = refs[0], refs[1 : 1 + arrived]
    unit_ref, radius_ref, grad_ref, loss_ref = refs[1 + arrived :]
    count, width = unit_ref.shape
    parts = blocks_of(width)
    total = held_ref[...]
    for ref in arrived_refs:
        total = total + ref[...].astype(f32)
    sums = []
    for which in range(4):
        row = 2 * parts * count + 2 * which
        sums.append((total[row : row + 1, :] + total[row + 1 : row + 2, :])[:, :count])
    pos, neg = sums[:2]
    loss_ref[...] = jnp.log(1.0 + pos) / pos_scale + jnp.log(1.0 + neg) / neg_scale
    scales = [to_column(1.0 / (1.0 + row)) for row in (neg, pos)]
    alongs = [to_column(row) for row in sums[2:]]
    unit = unit_ref[...]
    anchors = unit.astype(bf16).astype(f32)
    push, pull = [
        jnp.concatenate([total[(first + at) * count : (first + at + 1) * count, :] for at in range(parts)], axis=1)
        for first in (0, parts)
    ]
    grad_unit = (push + alongs[0] * anchors) * scales[0] - (pull + alongs[1] * anchors) * scales[1]
    along = jnp.sum(unit * grad_unit, axis=1, keepdims=True)
    grad_ref[...] = (grad_unit - unit * along) / radius_ref[:, :1]


def per_device(batch_rows, batch_labels, memory, memory_labels, keep_bits, step_index):
    groups = lax.axis_size("grp")
    members = lax.axis_size("dev")
    cores = 2 if members % 2 == 0 else 1
    line = members // cores
    count, width = batch_rows.shape
    slots = memory.shape[0]

    def exchange(value, axis, step):
        if axis == "grp":
            return lax.ppermute(value, "grp", [(i, i ^ step) for i in range(groups)])
        jump = step * cores if axis == "line" else step
        return lax.ppermute(value, "dev", [(i, i ^ jump) for i in range(members)])

    folded = (slots // lanes, lanes)
    parts = blocks_of(width)
    packed, unit, radius, slot_labels = call(
        prepare_kernel,
        [
            pltpu.VMEM((parts * count + 16, lanes), bf16),
            pltpu.VMEM((count, width), f32),
            pltpu.VMEM((count, lanes), f32),
            pltpu.VMEM(folded, jnp.int32),
        ],
        batch_rows, batch_labels.reshape(1, count), memory_labels.reshape(folded), keep_bits.reshape(folded),
        limit=vmem_most,
    )

    labels = [slot_labels] + [exchange(slot_labels, "core", s) for s in range(1, cores)]
    memories = [memory] + [exchange(memory, "core", s) for s in range(1, cores)]

    part = packed
    for s in range(line - 1, 0, -1):
        part = join([part, exchange(packed, "line", s)], labels if s == 1 else [])
    labels = [value.reshape(1, slots) for value in labels]
    blocks = [part] + [None] * (groups - 1)
    for s in range(groups - 1, 0, -1):
        blocks[s] = exchange(part, "grp", s)
    keys = [keys_of(memory, pltpu.HBM, [part])] + [keys_of(value, pltpu.VMEM, [part]) for value in memories[1:]]

    size = count * line
    arrived, after = [], []
    places = list(range(groups - 1, 0, -1))
    while places:
        now = places[:1] if not after else places[:2]
        places = places[len(now) :]
        after = block_sums([blocks[s] for s in now], keys, labels, count, bf16, after)
        arrived += [exchange(value, "grp", s) for s, value in zip(now, after)]
    held, copied = block_sums([part], keys, labels, count, f32, after, [memory])
    sizes = (count, slots, groups, line, cores)
    moved = pick(blocks, step_index, sizes, after)
    choices = [moved] + [exchange(moved, "core", s) for s in range(1, cores)]

    sums, *others = add(held, arrived, size, count, 2 * parts, choices)
    arrived = [exchange(value, "line", line - at) for at, value in enumerate(others, 1)]
    grad_batch, loss = call(
        functools.partial(finish_kernel, len(arrived)),
        [shaped((count, width), f32), shaped((1, count), f32)],
        sums, *arrived, unit, radius,
    )

    new_memory, new_labels = patch(copied, memory_labels.reshape(folded), choices, step_index, sizes)
    return (grad_batch, loss.reshape(count), new_memory, new_labels.reshape(slots))


def solution(mesh):
    placed = (
        P(("grp", "dev"), None),
        P(("grp", "dev")),
        P(("grp", "dev"), None),
        P(("grp", "dev")),
        P(("grp", "dev")),
        P(),
    )
    return jax.shard_map(
        per_device,
        mesh=mesh,
        in_specs=placed,
        out_specs=(
            P(("grp", "dev"), None),
            P(("grp", "dev")),
            P(("grp", "dev"), None),
            P(("grp", "dev")),
        ),
        check_vma=False,
    )
```

```python
import functools
import math

import jax
import jax.numpy as jnp
from jax import lax
from jax.experimental import pallas as pl
from jax.experimental.pallas import tpu as pltpu
from jax.sharding import PartitionSpec as P

pos_scale = 2.0
neg_scale = 50.0
margin = 0.5
lanes = 128
log2e = math.log2(math.e)
vmem_bytes = 20 * 1024 * 1024
vmem_most = 56 * 1024 * 1024
f32 = jnp.float32
bf16 = jnp.bfloat16


def call(body, outs, *args, work=0, limit=vmem_bytes, **kw):
    return pl.pallas_call(
        body,
        out_shape=outs,
        compiler_params=pltpu.CompilerParams(vmem_limit_bytes=limit),
        cost_estimate=pl.CostEstimate(flops=work, bytes_accessed=0, transcendentals=0),
        **kw,
    )(*args)


def shaped(shape, dtype):
    return jax.ShapeDtypeStruct(shape, dtype)


def in_vmem(value):
    return pltpu.with_memory_space_constraint(value, pltpu.VMEM)


def rounded_up(value, unit):
    return (value + unit - 1) // unit * unit


def blocks_of(width):
    return width // lanes


def rows_as_lanes(parts, rows):
    row = lax.broadcasted_iota(jnp.int32, (rows, lanes), 0)
    out = jnp.zeros((rows, lanes), f32)
    for at, part in enumerate(parts):
        out = jnp.where(row == at, part, out)
    return out


def prepare_kernel(rows_ref, labels_ref, stored_ref, keep_ref, packed_ref, unit_ref, radius_ref, slot_ref):
    slot_ref[...] = jnp.where(keep_ref[...] > 0, stored_ref[...], -1)
    rows = rows_ref[...].astype(f32)
    count, width = rows.shape
    radius = jnp.sqrt(jnp.sum(rows * rows, axis=1, keepdims=True) + 1e-06)
    unit = rows / radius
    unit_ref[...] = unit
    radius_ref[...] = jnp.broadcast_to(radius, radius_ref.shape)
    anchors = unit.astype(bf16)
    for at in range(blocks_of(width)):
        packed_ref[at * count : (at + 1) * count, :] = anchors[:, at * lanes : (at + 1) * lanes]
    row = jnp.concatenate([labels_ref[...].astype(f32), jnp.zeros((1, lanes - count), f32)], axis=1)
    high = jnp.floor(row * (1.0 / 256.0))
    tail = packed_ref.shape[0] - blocks_of(width) * count
    packed_ref[blocks_of(width) * count :, :] = rows_as_lanes([high, row - high * 256.0], tail).astype(bf16)


def diagonal(count):
    across = lax.broadcasted_iota(jnp.int32, (count, count), 1)
    down = lax.broadcasted_iota(jnp.int32, (count, count), 0)
    return across == down


def to_column(row):
    count = row.shape[1]
    spread = jnp.broadcast_to(row, (count, count))
    return jnp.sum(jnp.where(diagonal(count), spread, 0.0), axis=1, keepdims=True)


def to_row(column):
    count = column.shape[0]
    spread = jnp.broadcast_to(column, (count, count))
    return jnp.sum(jnp.where(diagonal(count), spread, 0.0), axis=0, keepdims=True)


def keys_kernel(memory_ref, *refs):
    keys_ref = refs[-1]
    rows = memory_ref[...].astype(f32)
    radius = jnp.sqrt(jnp.sum(rows * rows, axis=1, keepdims=True) + 1e-06)
    keys_ref[...] = (rows / radius).astype(bf16)


def keys_of(memory, place, after):
    slots, width = memory.shape
    block = math.gcd(1024, slots)
    spec = pl.BlockSpec((block, width), lambda i: (i, 0))
    return call(
        keys_kernel,
        [shaped((slots, width), bf16)],
        pltpu.with_memory_space_constraint(memory, place), *after,
        work=64 * slots * width * width,
        grid=(slots // block,),
        in_specs=[spec] + [pl.BlockSpec(memory_space=pl.ANY)] * len(after),
        out_specs=[spec],
    )[0]


def join_kernel(blocks, *refs):
    block_refs, out_ref = refs[:blocks], refs[-1]
    first = 0
    for ref in block_refs:
        out_ref[first : first + ref.shape[0], :] = ref[...]
        first += ref.shape[0]


def join(blocks, after):
    rows = sum(block.shape[0] for block in blocks)
    return call(
        functools.partial(join_kernel, len(blocks)),
        [shaped((rows, blocks[0].shape[1]), blocks[0].dtype)],
        *blocks, *after,
        in_specs=[pl.BlockSpec(memory_space=pltpu.VMEM)] * len(blocks)
        + [pl.BlockSpec(memory_space=pl.ANY)] * len(after),
    )[0]


def positions(step, count, slots, groups, line, cores):
    first = lax.rem(step, slots // count) * count
    crossing = lax.rem(step, cores)
    members = line * cores
    devices_all = groups * members
    grp = lax.axis_index("grp")
    dev = lax.axis_index("dev")
    target = grp * members + (dev ^ crossing)
    source = lax.rem(target + devices_all - lax.rem(step, devices_all), devices_all)
    source_grp = lax.div(source, members)
    source_line = lax.div(lax.rem(source, members), cores)
    step = lax.div(dev, cores) ^ source_line
    return first, crossing, grp ^ source_grp, lax.rem(line - step, line)


def pick_kernel(groups, sizes, step_ref, *refs):
    blocks_refs, out_ref = refs[:groups], refs[-1]
    rows = out_ref.shape[0]
    _, _, grp_place, line_place = positions(step_ref[0], *sizes)
    for place, ref in enumerate(blocks_refs):

        @pl.when(grp_place == place)
        def _():
            out_ref[...] = ref[pl.ds(pl.multiple_of(line_place * rows, 16), rows), :]


def pick(blocks, step, sizes, after):
    line = sizes[3]
    return call(
        functools.partial(pick_kernel, len(blocks), sizes),
        [shaped((blocks[0].shape[0] // line, lanes), bf16)],
        step, *blocks, *after,
        in_specs=[pl.BlockSpec(memory_space=pltpu.SMEM)]
        + [pl.BlockSpec(memory_space=pltpu.VMEM)] * len(blocks)
        + [pl.BlockSpec(memory_space=pl.ANY)] * len(after),
    )[0]


def patch_kernel(choices, sizes, step_ref, stored_ref, labels_ref, *refs):
    moved_refs, (memory_ref, new_labels_ref, rows_ref, sem) = refs[:choices], refs[choices:]
    count, width = rows_ref.shape
    first, crossing, _, _ = positions(step_ref[0], *sizes)
    moved = moved_refs[0][...]
    for choice in range(1, choices):
        moved = jnp.where(crossing == choice, moved_refs[choice][...], moved)
    for at in range(blocks_of(width)):
        rows_ref[:, at * lanes : (at + 1) * lanes] = moved[at * count : (at + 1) * count, :]
    target = memory_ref.at[pl.ds(pl.multiple_of(first, count), count), :]
    copy = pltpu.make_async_copy(rows_ref, target, sem)
    copy.start()
    digits = moved[blocks_of(width) * count :, :].astype(f32)
    row = (digits[0:1, :] * 256.0 + digits[1:2, :]).astype(jnp.int32)
    old = labels_ref[...]
    turned = pltpu.roll(jnp.broadcast_to(row, old.shape), lax.rem(first, lanes), 1)
    slot = lax.broadcasted_iota(jnp.int32, old.shape, 0) * lanes + lax.broadcasted_iota(jnp.int32, old.shape, 1)
    new_labels_ref[...] = jnp.where((slot >= first) & (slot < first + count), turned, old)
    copy.wait()


def patch(stored, labels, choices, step, sizes):
    count, width = sizes[0], stored.shape[1]
    return call(
        functools.partial(patch_kernel, len(choices), sizes),
        [shaped(stored.shape, bf16), shaped(labels.shape, jnp.int32)],
        step, stored, labels, *choices,
        in_specs=[pl.BlockSpec(memory_space=pltpu.SMEM), pl.BlockSpec(memory_space=pl.ANY)]
        + [pl.BlockSpec(memory_space=pltpu.VMEM)] * (1 + len(choices)),
        out_specs=[pl.BlockSpec(memory_space=pl.ANY), pl.BlockSpec(memory_space=pltpu.VMEM)],
        scratch_shapes=[pltpu.VMEM((count, width), bf16), pltpu.SemaphoreType.DMA],
        input_output_aliases={1: 0},
    )


def split_digits(row):
    high = row.astype(bf16).astype(f32)
    return [high, row - high]


def sum_rows(size):
    return rounded_up(8 * (rounded_up(size, lanes) // lanes), 16)


def block_kernel(blocks, sides, unit, count, copies, scratch, *refs):
    if copies:
        source_ref, target_ref, sem = refs[blocks + 2 * sides], refs[-scratch - 1], refs[-1]
        copy = pltpu.make_async_copy(source_ref, target_ref, sem)
        copy.start()
        refs = refs[: -scratch - 1] + refs[-scratch : -1]
        scratch -= 1
    rows_refs, keys_refs = refs[:blocks], refs[blocks : blocks + sides]
    label_refs = refs[blocks + sides : blocks + 2 * sides]
    out_refs = refs[-scratch - blocks : -scratch]
    anchors_ref, labels_ref, total_ref, pos_ref, neg_ref = refs[-scratch:-4]
    scores_refs, weight_refs = refs[-4:-2], refs[-2:]
    slots, width = keys_refs[0].shape
    parts = blocks_of(width)
    packed = rows_refs[0].shape[0]
    members = packed // (parts * count + 16)
    size = members * count
    columns = []
    for block, ref in enumerate(rows_refs):
        for member in range(members):
            first = member * (parts * count + 16)
            to = block * size + member * count
            for at in range(parts):
                anchors_ref[to : to + count, at * lanes : (at + 1) * lanes] = ref[
                    first + at * count : first + (at + 1) * count, :
                ]
            digits = ref[first + parts * count : first + parts * count + 16, :].astype(f32)
            columns.append(to_column((digits[0:1, :] * 256.0 + digits[1:2, :])[:, :count]))
    rows = blocks * size
    labels_ref[...] = jnp.broadcast_to(jnp.concatenate(columns, axis=0), labels_ref.shape)
    pos_ref[...] = jnp.zeros_like(pos_ref)
    neg_ref[...] = jnp.zeros_like(neg_ref)
    anchors = anchors_ref[...]
    units = [(side, at) for side in range(sides) for at in range(0, slots, unit)]
    longest = 4 if blocks == 1 else 2
    runs = []
    for side in range(sides):
        left = slots // unit
        while left:
            length = min(longest, left)
            if blocks == 1 and side == sides - 1 and length == left and left > 1:
                length -= 1
            runs.append(length)
            left -= length
    starts = [sum(runs[:run]) for run in range(len(runs))]
    run_of = [run for run, length in enumerate(runs) for _ in range(length)]
    cuts = max(rows // 32, 4)
    quarter = rows // cuts

    def score_unit(at):
        side, first = units[at]
        scores_refs[at % 2][...] = lax.dot_general(
            anchors, keys_refs[side][first : first + unit, :], (((1,), (1,)), ((), ())), preferred_element_type=f32
        )

    def term_unit(at, which):
        side, first = units[at]
        part = slice(which * quarter, (which + 1) * quarter)
        weights_ref = weight_refs[run_of[at] % 2]
        base = (at - starts[run_of[at]]) * unit
        wanted = labels_ref[part, :]
        pos_sum, neg_sum = pos_ref[part, :], neg_ref[part, :]
        for piece in range(0, unit, lanes):
            slot_labels = label_refs[side][:, first + piece : first + piece + lanes].astype(f32)
            neg_shift = jnp.where(slot_labels < 0.0, -1e30, -neg_scale * margin * log2e)
            same = wanted == slot_labels
            slope = jnp.where(same, -pos_scale * log2e, neg_scale * log2e)
            shift = jnp.where(same, pos_scale * margin * log2e, neg_shift)
            term = jnp.exp2(scores_refs[at % 2][part, piece : piece + lanes] * slope + shift)
            pos = jnp.where(same, term, 0.0)
            neg = jnp.where(same, 0.0, term)
            pos_sum += pos
            neg_sum += neg
            to = slice(base + piece, base + piece + lanes)
            weights_ref[part, to] = neg.astype(bf16)
            weights_ref[rows + which * quarter : rows + (which + 1) * quarter, to] = pos.astype(bf16)
        pos_ref[part, :] = pos_sum
        neg_ref[part, :] = neg_sum

    def weigh_half(run, half):
        side, first = units[starts[run]]
        span = runs[run] * unit
        part = slice(half * (width // 2), (half + 1) * (width // 2))
        more = jnp.dot(
            weight_refs[run % 2][:, :span], keys_refs[side][first : first + span, part], preferred_element_type=f32
        )
        total_ref[:, part] = more if run == 0 else total_ref[:, part] + more

    score_unit(0)
    waiting = []
    for at in range(len(units)):
        if at in starts and at:
            waiting += [(run_of[at] - 1, 0), (run_of[at] - 1, 1)]
        left = runs[run_of[at]] - (at - starts[run_of[at]])
        now, waiting = waiting[: -(-len(waiting) // left)], waiting[-(-len(waiting) // left) :]
        for which in range(cuts):
            if which == cuts // 4 and at + 1 < len(units):
                score_unit(at + 1)
            if which == cuts - cuts // 4:
                for run, half in now:
                    weigh_half(run, half)
            term_unit(at, which)
    weigh_half(len(runs) - 1, 0)
    weigh_half(len(runs) - 1, 1)
    total = total_ref[...]
    pos_sum = jnp.sum(pos_ref[...], axis=1, keepdims=True)
    neg_sum = jnp.sum(neg_ref[...], axis=1, keepdims=True)
    floats = anchors.astype(f32)
    sums = [pos_sum, neg_sum]
    for which in range(2):
        value = total[which * rows : (which + 1) * rows, :]
        along = jnp.sum(value * floats, axis=1, keepdims=True)
        sums.append(along)
        rest = value - along * floats
        for block, ref in enumerate(out_refs):
            for at in range(parts):
                first = (which * parts + at) * size
                ref[first : first + size, :] = rest[
                    block * size : (block + 1) * size, at * lanes : (at + 1) * lanes
                ].astype(ref.dtype)
    for block, ref in enumerate(out_refs):
        lines = []
        for first in range(0, size, lanes):
            last = min(first + lanes, size)
            for value in sums:
                row = to_row(value[block * size + first : block * size + last])
                if last - first < lanes:
                    row = jnp.concatenate([row, jnp.zeros((1, lanes - last + first), f32)], axis=1)
                lines += split_digits(row)
        first = 2 * parts * size
        ref[first:, :] = rows_as_lanes(lines, ref.shape[0] - first).astype(ref.dtype)
    if copies:
        copy.wait()


def block_sums(blocks, keys, labels, count, dtype, after, copied=()):
    slots, width = keys[0].shape
    parts = blocks_of(width)
    size = blocks[0].shape[0] // (parts * count + 16) * count
    rows = len(blocks) * size
    unit = math.gcd(256, slots // 2)
    anywhere = pl.BlockSpec(memory_space=pl.ANY)
    vmem = pl.BlockSpec(memory_space=pltpu.VMEM)
    return call(
        functools.partial(block_kernel, len(blocks), len(keys), unit, count, len(copied), 9 + len(copied)),
        [shaped((2 * parts * size + sum_rows(size), lanes), dtype)] * len(blocks)
        + [shaped(value.shape, value.dtype) for value in copied],
        *blocks, *[in_vmem(k) for k in keys], *labels, *copied, *after,
        work=12 * size * len(blocks) * slots * len(keys) * width,
        in_specs=[vmem] * (len(blocks) + 2 * len(keys)) + [anywhere] * (len(copied) + len(after)),
        out_specs=[vmem] * len(blocks) + [anywhere] * len(copied),
        scratch_shapes=[
            pltpu.VMEM((rows, width), bf16),
            pltpu.VMEM((rows, lanes), f32),
            pltpu.VMEM((2 * rows, width), f32),
            pltpu.VMEM((rows, lanes), f32),
            pltpu.VMEM((rows, lanes), f32),
            pltpu.VMEM((rows, unit), f32),
            pltpu.VMEM((rows, unit), f32),
            pltpu.VMEM((2 * rows, (4 if len(blocks) == 1 else 2) * unit), bf16),
            pltpu.VMEM((2 * rows, (4 if len(blocks) == 1 else 2) * unit), bf16),
        ]
        + [pltpu.SemaphoreType.DMA] * len(copied),
    )


def add_kernel(arrived, size, count, *refs):
    in_refs, out_refs = refs[: 1 + arrived], refs[-(size // count) :]
    columns = (in_refs[0].shape[0] - sum_rows(size)) // size

    def total(first, rows):
        value = in_refs[0][first : first + rows, :]
        for ref in in_refs[1:]:
            value = value + ref[first : first + rows, :].astype(f32)
        return value

    sums = total(columns * size, sum_rows(size))
    for block, ref in enumerate(out_refs):
        for at in range(columns):
            part = total(at * size + block * count, count)
            ref[at * count : (at + 1) * count, :] = part.astype(ref.dtype)
        group, lane = divmod(block * count, lanes)
        lines = []
        for which in range(4):
            row = 8 * group + 2 * which
            lines += split_digits(sums[row : row + 1, :] + sums[row + 1 : row + 2, :])
        packed = rows_as_lanes(lines, ref.shape[0] - columns * count)
        if lane:
            packed = pltpu.roll(packed, lanes - lane, 1)
        ref[columns * count :, :] = packed.astype(ref.dtype)


def add(held, arrived, size, count, columns, after):
    shape = (columns * count + sum_rows(count), lanes)
    outs = [shaped(shape, f32 if b == 0 else bf16) for b in range(size // count)]
    return call(
        functools.partial(add_kernel, len(arrived), size, count),
        outs,
        held, *arrived, *after,
        in_specs=[pl.BlockSpec(memory_space=pltpu.VMEM)] * (1 + len(arrived))
        + [pl.BlockSpec(memory_space=pl.ANY)] * len(after),
    )


def finish_kernel(arrived, *refs):
    held_ref, arrived_refs = refs[0], refs[1 : 1 + arrived]
    unit_ref, radius_ref, grad_ref, loss_ref = refs[1 + arrived :]
    count, width = unit_ref.shape
    parts = blocks_of(width)
    total = held_ref[...]
    for ref in arrived_refs:
        total = total + ref[...].astype(f32)
    sums = []
    for which in range(4):
        row = 2 * parts * count + 2 * which
        sums.append((total[row : row + 1, :] + total[row + 1 : row + 2, :])[:, :count])
    pos, neg = sums[:2]
    loss_ref[...] = jnp.log(1.0 + pos) / pos_scale + jnp.log(1.0 + neg) / neg_scale
    scales = [to_column(1.0 / (1.0 + row)) for row in (neg, pos)]
    alongs = [to_column(row) for row in sums[2:]]
    unit = unit_ref[...]
    anchors = unit.astype(bf16).astype(f32)
    push, pull = [
        jnp.concatenate([total[(first + at) * count : (first + at + 1) * count, :] for at in range(parts)], axis=1)
        for first in (0, parts)
    ]
    grad_unit = (push + alongs[0] * anchors) * scales[0] - (pull + alongs[1] * anchors) * scales[1]
    along = jnp.sum(unit * grad_unit, axis=1, keepdims=True)
    grad_ref[...] = (grad_unit - unit * along) / radius_ref[:, :1]


def per_device(batch_rows, batch_labels, memory, memory_labels, keep_bits, step_index):
    groups = lax.axis_size("grp")
    members = lax.axis_size("dev")
    cores = 2 if members % 2 == 0 else 1
    line = members // cores
    count, width = batch_rows.shape
    slots = memory.shape[0]

    def exchange(value, axis, step):
        if axis == "grp":
            return lax.ppermute(value, "grp", [(i, i ^ step) for i in range(groups)])
        jump = step * cores if axis == "line" else step
        return lax.ppermute(value, "dev", [(i, i ^ jump) for i in range(members)])

    folded = (slots // lanes, lanes)
    parts = blocks_of(width)
    packed, unit, radius, slot_labels = call(
        prepare_kernel,
        [
            pltpu.VMEM((parts * count + 16, lanes), bf16),
            pltpu.VMEM((count, width), f32),
            pltpu.VMEM((count, lanes), f32),
            pltpu.VMEM(folded, jnp.int32),
        ],
        batch_rows, batch_labels.reshape(1, count), memory_labels.reshape(folded), keep_bits.reshape(folded),
        limit=vmem_most,
    )

    labels = [slot_labels] + [exchange(slot_labels, "core", s) for s in range(1, cores)]
    memories = [memory] + [exchange(memory, "core", s) for s in range(1, cores)]

    part = packed
    for s in range(line - 1, 0, -1):
        part = join([part, exchange(packed, "line", s)], labels if s == 1 else [])
    labels = [value.reshape(1, slots) for value in labels]
    blocks = [part] + [None] * (groups - 1)
    for s in range(groups - 1, 0, -1):
        blocks[s] = exchange(part, "grp", s)
    keys = [keys_of(memory, pltpu.HBM, [part])] + [keys_of(value, pltpu.VMEM, [part]) for value in memories[1:]]

    size = count * line
    arrived, after = [], []
    places = list(range(groups - 1, 0, -1))
    while places:
        now = places[:1] if not after else places[:2]
        places = places[len(now) :]
        after = block_sums([blocks[s] for s in now], keys, labels, count, bf16, after)
        arrived += [exchange(value, "grp", s) for s, value in zip(now, after)]
    held, copied = block_sums([part], keys, labels, count, f32, after, [memory])
    sizes = (count, slots, groups, line, cores)
    moved = pick(blocks, step_index, sizes, after)
    choices = [moved] + [exchange(moved, "core", s) for s in range(1, cores)]

    sums, *others = add(held, arrived, size, count, 2 * parts, choices)
    arrived = [exchange(value, "line", line - at) for at, value in enumerate(others, 1)]
    grad_batch, loss = call(
        functools.partial(finish_kernel, len(arrived)),
        [shaped((count, width), f32), shaped((1, count), f32)],
        sums, *arrived, unit, radius,
    )

    new_memory, new_labels = patch(copied, memory_labels.reshape(folded), choices, step_index, sizes)
    return (grad_batch, loss.reshape(count), new_memory, new_labels.reshape(slots))


def solution(mesh):
    placed = (
        P(("grp", "dev"), None),
        P(("grp", "dev")),
        P(("grp", "dev"), None),
        P(("grp", "dev")),
        P(("grp", "dev")),
        P(),
    )
    return jax.shard_map(
        per_device,
        mesh=mesh,
        in_specs=placed,
        out_specs=(
            P(("grp", "dev"), None),
            P(("grp", "dev")),
            P(("grp", "dev"), None),
            P(("grp", "dev")),
        ),
        check_vma=False,
    )
```
